32 devices in a mesh: dp: 16 (over z, y, core), mp: 2 (over x).
Axes of the slice: x: 2, y: 2, z: 4, core: 2. Of those that a mesh axis runs over, the one named last changes fastest.
Arguments:
- tokens: bfloat16 [4864, 512], P(('dp', 'mp')), may hold values from -6 to 6
- out_grad: bfloat16 [4864, 512], P(('dp', 'mp')), may hold values from -6 to 6
- crop_image: int32 [256], P('dp'), may hold values from 0 to 31, as said below
- crop_res: int32 [256], P('dp'), may hold values from 0 to 1, as said below
- position_kernel: float32 [3, 3, 512], replicated, may hold values from -2 to 2
- position_bias: float32 [512], replicated, may hold values from -2 to 2
- gain_one: float32 [512], replicated, may hold values from 0.25 to 1.75
- shift_one: float32 [512], replicated, may hold values from -2 to 2
- qkv_weight: bfloat16 [512, 3, 512], P(None, None, 'mp'), may hold values from -0.25 to 0.25
- query_value_bias: bfloat16 [2, 512], P(None, 'mp'), may hold values from -2 to 2
- relative_three: float32 [3, 3, 128], replicated, may hold values from -2 to 2
- relative_five: float32 [5, 5, 192], replicated, may hold values from -1.25 to 1.25
- relative_seven: float32 [7, 7, 192], replicated, may hold values from -0.875 to 0.875
- relative_bias: float32 [512], replicated, may hold values from -2 to 2
- output_weight: bfloat16 [512, 512], P('mp'), may hold values from -0.25 to 0.25
- output_bias: float32 [512], replicated, may hold values from -2 to 2
- gain_two: float32 [512], replicated, may hold values from 0.25 to 1.75
- shift_two: float32 [512], replicated, may hold values from -2 to 2
- up_weight: bfloat16 [512, 2048], P(None, 'mp'), may hold values from -0.25 to 0.25
- up_bias: bfloat16 [2048], P('mp'), may hold values from -3 to 3
- down_weight: bfloat16 [2048, 512], P('mp'), may hold values from -0.125 to 0.125
- down_bias: float32 [512], replicated, may hold values from -2 to 2
Outputs:
- block_out: float32 [4864, 512], P(('dp', 'mp'))
- token_grad: float32 [4864, 512], P(('dp', 'mp'))
- grad_position_kernel: float32 [3, 3, 512], replicated
- grad_position_bias: float32 [512], replicated
- grad_gain_one: float32 [512], replicated
- grad_shift_one: float32 [512], replicated
- grad_qkv_weight: float32 [512, 3, 512], P(None, None, 'mp')
- grad_query_value_bias: float32 [2, 512], P(None, 'mp')
- grad_relative_three: float32 [3, 3, 128], replicated
- grad_relative_five: float32 [5, 5, 192], replicated
- grad_relative_seven: float32 [7, 7, 192], replicated
- grad_relative_bias: float32 [512], replicated
- grad_output_weight: float32 [512, 512], P('mp')
- grad_output_bias: float32 [512], replicated
- grad_gain_two: float32 [512], replicated
- grad_shift_two: float32 [512], replicated
- grad_up_weight: float32 [512, 2048], P(None, 'mp')
- grad_up_bias: float32 [2048], P('mp')
- grad_down_weight: float32 [2048, 512], P('mp')
- grad_down_bias: float32 [512], replicated
The draws below stay inside these ranges and needn't reach their ends.
Inputs may be any that keep to these rules, and one draw needn't show every extreme that they name: `crop_image`: every image id stands at exactly 8 crop slots, all within the aligned block of 8 slots of one index along dp and mp; block b holds the images b * 1 to (b + 1) - 1 in any order of slots. `crop_res`: every image has exactly two crops with 0 (7 x 7 tokens) and six with 1 (3 x 3 tokens).
All inputs are finite; a program needn't handle non-finite values.
Results may differ from the reference program's by a relative error of at most 0.019.
Values may be sent and summed in bfloat16 or wider, within the bound.
No kernel may reach another device: no remote copies, remote signals or barrier semaphores. Data moves between devices by JAX's collectives and lax.ppermute only.
A program may use at most 128 MiB of HBM per device.

```python
import jax
import jax.numpy as jnp
from jax import lax

HEAD = 64
FF = 2048
D = 512
IMG_MP = 1
CROPS = 256
TOKENS = 4864
N_DP = 16
N_MP = 2


def crop_layout(key):
    slot_count = 8 * IMG_MP
    block_count = CROPS // slot_count
    block_keys = jax.random.split(key, block_count)
    entries = jax.vmap(lambda block_key: jax.random.permutation(block_key, slot_count))(block_keys).astype(jnp.int32)
    image_base = (jnp.arange(block_count, dtype=jnp.int32) * IMG_MP)[:, None]
    images = (image_base + entries // 8).reshape(-1).astype(jnp.int32)
    crop_kinds = jnp.where(entries % 8 < 2, 0, 1).reshape(-1).astype(jnp.int32)
    return (images, crop_kinds)


def draw_crop_image(key, part):
    layout = crop_layout(key)
    return layout[0]


def draw_crop_res(key, part):
    layout = crop_layout(key)
    return layout[1]


def block_scale(own_key, shape, shards, smallest, top_value):
    loudness, own = 1.0, jax.random.fold_in(own_key, 6)
    for position, blocks in shards:
        heights = jnp.exp(jax.random.uniform(jax.random.fold_in(own, position), (blocks,), jnp.float32, smallest / len(shards), top_value / len(shards)))
        loudness = loudness * jnp.repeat(heights, shape[position] // blocks).reshape([-1 if axis == position else 1 for axis in range(len(shape))])
    return loudness


def bell_draw(rng, shape, width, reach, cuts=(), kind=jnp.bfloat16):
    drawn = jax.random.normal(rng, shape, jnp.float32) * width
    if len(cuts) > 0:
        drawn = block_scale(rng, shape, cuts, -0.22, 0.18) * drawn
    return jnp.clip(drawn, min=-reach, max=reach).astype(kind)


def setup_inputs(seed: int = 0) -> dict:
    key_of = jax.random.split(jax.random.key(seed), 23)
    tokens = bell_draw(key_of[0], (TOKENS, D), 1.0, 6.0, ((0, 32),))
    out_grad = bell_draw(key_of[1], (TOKENS, D), 1.0, 6.0, ((0, 32),))
    crop_image = draw_crop_image(jax.random.fold_in(key_of[22], 71), 0)
    crop_res = draw_crop_res(jax.random.fold_in(key_of[22], 71), 0)
    position_kernel = bell_draw(key_of[4], (3, 3, D), 9 ** -0.5, 2.0, (), jnp.float32)
    position_bias = bell_draw(key_of[5], (D,), 0.3, 2.0, (), jnp.float32)
    gain_one = jnp.clip(1.0 + 0.15 * jax.random.normal(key_of[6], (D,), jnp.float32), 0.25, 1.75)
    shift_one = bell_draw(key_of[7], (D,), 0.3, 2.0, (), jnp.float32)
    qkv_weight = bell_draw(key_of[8], (D, 3, D), D ** -0.5, 0.25, ((2, 2),))
    query_value_bias = bell_draw(key_of[9], (2, D), 0.3, 2.0, ((1, 2),))
    relative_three = bell_draw(key_of[10], (3, 3, 2 * HEAD), 9 ** -0.5, 2.0, (), jnp.float32)
    relative_five = bell_draw(key_of[11], (5, 5, 3 * HEAD), 25 ** -0.5, 1.25, (), jnp.float32)
    relative_seven = bell_draw(key_of[12], (7, 7, 3 * HEAD), 49 ** -0.5, 0.875, (), jnp.float32)
    relative_bias = bell_draw(key_of[13], (D,), 0.3, 2.0, (), jnp.float32)
    output_weight = bell_draw(key_of[14], (D, D), D ** -0.5, 0.25, ((0, 2),))
    output_bias = bell_draw(key_of[15], (D,), 0.3, 2.0, (), jnp.float32)
    gain_two = jnp.clip(1.0 + 0.15 * jax.random.normal(key_of[16], (D,), jnp.float32), 0.25, 1.75)
    shift_two = bell_draw(key_of[17], (D,), 0.3, 2.0, (), jnp.float32)
    up_weight = bell_draw(key_of[18], (D, FF), D ** -0.5, 0.25, ((1, 2),))
    up_bias = bell_draw(key_of[19], (FF,), 0.5, 3.0, ((0, 2),))
    down_weight = bell_draw(key_of[20], (FF, D), FF ** -0.5, 0.125, ((0, 2),))
    down_bias = bell_draw(key_of[21], (D,), 0.3, 2.0, (), jnp.float32)
    return dict(tokens=tokens, out_grad=out_grad, crop_image=crop_image, crop_res=crop_res, position_kernel=position_kernel, position_bias=position_bias, gain_one=gain_one, shift_one=shift_one, qkv_weight=qkv_weight, query_value_bias=query_value_bias, relative_three=relative_three, relative_five=relative_five, relative_seven=relative_seven, relative_bias=relative_bias, output_weight=output_weight, output_bias=output_bias, gain_two=gain_two, shift_two=shift_two, up_weight=up_weight, up_bias=up_bias, down_weight=down_weight, down_bias=down_bias)


HIGHEST = lax.Precision.HIGHEST
EPSILON = 1e-06

@jax.custom_vjp
def low(v):
    return lax.optimization_barrier(v.astype(jnp.bfloat16)).astype(jnp.float32)

@jax.custom_vjp
def low_back(v):
    return v

def low_keep(v):
    return (low(v), None)

def low_pass(kept, grad):
    return (grad,)

def back_keep(v):
    return (v, None)

def back_low(kept, grad):
    return (low(grad),)
low.defvjp(low_keep, low_pass)
low_back.defvjp(back_keep, back_low)

def layer_norm(inputs, norm_gain, norm_shift):
    average = lax.optimization_barrier(jnp.mean(inputs, axis=-1, keepdims=True))
    centred = inputs - average
    variance = lax.optimization_barrier(jnp.mean(centred * centred, axis=-1, keepdims=True))
    return centred * lax.rsqrt(variance + EPSILON) * norm_gain + norm_shift

def depthwise(grids, kernel):
    return lax.conv_general_dilated(grids, kernel[:, :, None, :], (1, 1), 'SAME', dimension_numbers=('NHWC', 'HWIO', 'NHWC'), feature_group_count=grids.shape[3], precision=HIGHEST)

def crop_tables(crop_kinds, crop_images, image_count):
    slot_count = crop_kinds.shape[0]
    glob_count = slot_count // 4
    local_count = slot_count - glob_count
    is_global = (crop_kinds == 0).astype(jnp.int32)
    crop_sizes = (9 + 40 * is_global).astype(jnp.int32)
    offsets = (jnp.cumsum(crop_sizes) - crop_sizes).astype(jnp.int32)
    glob_rank = (jnp.cumsum(is_global) - 1).astype(jnp.int32)
    local_rank = (jnp.cumsum(1 - is_global) - 1).astype(jnp.int32)
    glob_pick = (is_global[None, :] == 1) & (glob_rank[None, :] == jnp.arange(glob_count, dtype=jnp.int32)[:, None])
    local_pick = (is_global[None, :] == 0) & (local_rank[None, :] == jnp.arange(local_count, dtype=jnp.int32)[:, None])
    glob_start = lax.optimization_barrier(jnp.sum(jnp.where(glob_pick, offsets[None, :], 0), axis=1)).astype(jnp.int32)
    local_start = lax.optimization_barrier(jnp.sum(jnp.where(local_pick, offsets[None, :], 0), axis=1)).astype(jnp.int32)
    glob_image = lax.optimization_barrier(jnp.sum(jnp.where(glob_pick, crop_images[None, :], 0), axis=1)).astype(jnp.int32)
    local_image = lax.optimization_barrier(jnp.sum(jnp.where(local_pick, crop_images[None, :], 0), axis=1)).astype(jnp.int32)
    token_order = jnp.concatenate([(glob_start[:, None] + jnp.arange(49, dtype=jnp.int32)[None, :]).reshape(-1), (local_start[:, None] + jnp.arange(9, dtype=jnp.int32)[None, :]).reshape(-1)]).astype(jnp.int32)
    total_rows = token_order.shape[0]
    inverse = jnp.zeros((total_rows,), jnp.int32).at[token_order].set(jnp.arange(total_rows, dtype=jnp.int32))
    image_slots = jnp.arange(image_count, dtype=jnp.int32)[:, None]
    glob_hot = (glob_image[None, :] == image_slots).astype(jnp.float32)
    local_hot = (local_image[None, :] == image_slots).astype(jnp.float32)
    return (token_order, inverse, glob_hot, local_hot)

def position_conv(inputs, kernel, conv_bias, token_order, inverse, glob_count):
    chan_width = inputs.shape[1]
    packed = inputs[token_order]
    glob_rows = glob_count * 49
    glob_grid = packed[:glob_rows].reshape(glob_count, 7, 7, chan_width)
    local_grid = packed[glob_rows:].reshape(-1, 3, 3, chan_width)
    conv_rows = jnp.concatenate([depthwise(glob_grid, kernel).reshape(glob_rows, chan_width), depthwise(local_grid, kernel).reshape(-1, chan_width)], axis=0)
    return conv_rows[inverse] + conv_bias

def attend(projections, kernel, conv_bias, token_order, inverse, glob_hot, local_hot):
    chan_width = kernel.shape[2]
    head_count = chan_width // HEAD
    total_rows = token_order.shape[0]
    packed = projections[token_order].reshape(total_rows, 3, chan_width)
    queries = packed[:, 0]
    key_rows = packed[:, 1]
    values = packed[:, 2]
    weights = jnp.exp(key_rows - lax.optimization_barrier(jnp.max(key_rows, axis=0, keepdims=True)))
    glob_rows = glob_hot.shape[1] * 49
    crop_groups = ((0, glob_rows, 7, glob_hot), (glob_rows, total_rows, 3, local_hot))
    image_kv = 0.0
    image_norm = 0.0
    for row_start, row_stop, edge_cells, onehot in crop_groups:
        crop_count = onehot.shape[1]
        cell_count = edge_cells * edge_cells
        crop_weights = weights[row_start:row_stop].reshape(crop_count, cell_count, head_count, HEAD)
        crop_values = values[row_start:row_stop].reshape(crop_count, cell_count, head_count, HEAD)
        crop_kv = jnp.einsum('gthc,gthd->ghcd', crop_weights, crop_values, precision=HIGHEST)
        image_kv = image_kv + jnp.einsum('ig,ghcd->ihcd', onehot, crop_kv, precision=HIGHEST)
        image_norm = image_norm + jnp.einsum('ig,ghc->ihc', onehot, lax.optimization_barrier(jnp.sum(crop_weights, axis=1)), precision=HIGHEST)
    context = image_kv / image_norm[:, :, :, None]
    pieces = []
    for row_start, row_stop, edge_cells, onehot in crop_groups:
        crop_count = onehot.shape[1]
        cell_count = edge_cells * edge_cells
        crop_context = jnp.einsum('ig,ihcd->ghcd', onehot, context, precision=HIGHEST)
        crop_queries = queries[row_start:row_stop].reshape(crop_count, cell_count, head_count, HEAD)
        factored = jnp.einsum('gthc,ghcd->gthd', crop_queries, crop_context, precision=HIGHEST).reshape(crop_count * cell_count, chan_width)
        crop_grid = values[row_start:row_stop].reshape(crop_count, edge_cells, edge_cells, chan_width)
        relative = depthwise(crop_grid, kernel).reshape(crop_count * cell_count, chan_width) + conv_bias
        pieces.append(factored * HEAD ** (-0.5) + queries[row_start:row_stop] * relative)
    return jnp.concatenate(pieces, axis=0)[inverse]

def block_forward(params, inputs, kind_ids, image_ids):
    position_kernel, position_bias, gain_one, shift_one, qkv_weight, query_value_bias, relative_three, relative_five, relative_seven, relative_bias, output_weight, output_bias, gain_two, shift_two, up_weight, up_bias, down_weight, down_bias = params
    token_order, inverse, glob_hot, local_hot = crop_tables(kind_ids, image_ids, IMG_MP)
    residual = inputs + position_conv(inputs, position_kernel, position_bias, token_order, inverse, glob_hot.shape[1])
    normed = low(layer_norm(residual, gain_one, shift_one))
    qkv_bias = jnp.stack([query_value_bias[0], jnp.zeros_like(query_value_bias[0]), query_value_bias[1]]).reshape(-1)
    projections = low_back(jnp.dot(normed, qkv_weight.reshape(D, 3 * D), preferred_element_type=jnp.float32, precision=HIGHEST) + qkv_bias)
    full_kernel = jnp.concatenate([jnp.pad(relative_three, ((2, 2), (2, 2), (0, 0))), jnp.pad(relative_five, ((1, 1), (1, 1), (0, 0))), relative_seven], axis=2)
    attended = low(attend(projections, full_kernel, relative_bias, token_order, inverse, glob_hot, local_hot))
    projected = low_back(jnp.dot(attended, output_weight, preferred_element_type=jnp.float32, precision=HIGHEST) + output_bias)
    middle = residual + projected
    normed_two = low(layer_norm(middle, gain_two, shift_two))
    hidden_pre = low_back(jnp.dot(normed_two, up_weight, preferred_element_type=jnp.float32, precision=HIGHEST) + up_bias)
    hidden = low(jax.nn.gelu(hidden_pre, approximate=False))
    mlp_out = low_back(jnp.dot(hidden, down_weight, preferred_element_type=jnp.float32, precision=HIGHEST) + down_bias)
    return middle + mlp_out

def reference(tokens, out_grad, crop_image, crop_res, position_kernel, position_bias, gain_one, shift_one, qkv_weight, query_value_bias, relative_three, relative_five, relative_seven, relative_bias, output_weight, output_bias, gain_two, shift_two, up_weight, up_bias, down_weight, down_bias):
    params = tuple((member.astype(jnp.float32) for member in (position_kernel, position_bias, gain_one, shift_one, qkv_weight, query_value_bias, relative_three, relative_five, relative_seven, relative_bias, output_weight, output_bias, gain_two, shift_two, up_weight, up_bias, down_weight, down_bias)))
    block_count = N_DP * N_MP
    block_rows = IMG_MP * 152
    slot_count = 8 * IMG_MP
    image_ids = (crop_image.reshape(block_count, slot_count) - (jnp.arange(block_count, dtype=jnp.int32) * IMG_MP)[:, None]).astype(jnp.int32)
    kind_ids = crop_res.reshape(block_count, slot_count)

    def whole(weights, inputs):

        def one_block(members):
            block_in, block_kinds, block_images = members
            return block_forward(weights, block_in, block_kinds, block_images)
        outputs = lax.map(jax.checkpoint(one_block), (inputs.reshape(block_count, block_rows, D), kind_ids, image_ids))
        return outputs.reshape(block_count * block_rows, D)
    block_out, pullback = jax.vjp(whole, params, tokens.astype(jnp.float32))
    weight_grads, token_grad = pullback(out_grad.astype(jnp.float32))
    return (block_out, token_grad, weight_grads[0], weight_grads[1], weight_grads[2], weight_grads[3], weight_grads[4], weight_grads[5], weight_grads[6], weight_grads[7], weight_grads[8], weight_grads[9], weight_grads[10], weight_grads[11], weight_grads[12], weight_grads[13], weight_grads[14], weight_grads[15], weight_grads[16], weight_grads[17])
```

```python
import functools
import math

import jax
import jax.numpy as jnp
from jax import lax
from jax.experimental import pallas as pl
from jax.experimental.pallas import tpu as pltpu
from jax.sharding import PartitionSpec as P

HEAD = 64
D = 512
EPSILON = 1e-06
SLOTS = 8
EDGE = 7
CELLS = EDGE * EDGE
ROWS = CELLS * SLOTS
SCALE = HEAD ** (-0.5)
BF16 = jnp.bfloat16
F32 = jnp.float32


def mm(left, right):
    return jnp.dot(left, right, preferred_element_type=F32)


def mm_t(left, right):
    return lax.dot_general(left, right, (((1,), (1,)), ((), ())), preferred_element_type=F32)


def t_mm(left, right):
    return lax.dot_general(left, right, (((0,), (0,)), ((), ())), preferred_element_type=F32)


def split_mm(onehot, values):
    high = values.astype(BF16)
    low = (values - high.astype(F32)).astype(BF16)
    return mm(onehot, high) + mm(onehot, low)


def call(kernel, outs, args, scratch=(), us=3.0, smem=0, vmem=24):
    specs = [pl.BlockSpec(memory_space=pltpu.SMEM)] * smem
    specs += [pl.BlockSpec(memory_space=pltpu.VMEM)] * (len(args) - smem)
    return pl.pallas_call(
        kernel,
        out_shape=[jax.ShapeDtypeStruct(shape, kind) for shape, kind in outs],
        in_specs=specs,
        out_specs=[pl.BlockSpec(memory_space=pltpu.VMEM)] * len(outs),
        scratch_shapes=list(scratch),
        compiler_params=pltpu.CompilerParams(vmem_limit_bytes=vmem << 20),
        cost_estimate=pl.CostEstimate(
            flops=int(us * 1.0e9), bytes_accessed=1 << 18, transcendentals=0
        ),
    )(*args)


def over_lanes(width, body):
    if width % 128 == 0:

        @pl.loop(0, width // 128)
        def _(step):
            body(pl.ds(pl.multiple_of(step * 128, 128), 128))

    else:
        body(slice(0, width))


def frame_conv(source, tap, target, edge, lanes):
    half = (edge - 1) // 2
    for i in range(EDGE):
        total = [None] * EDGE
        for a in range(edge):
            row = i + a - half
            if not 0 <= row < EDGE:
                continue
            cells = [source[row * EDGE + j, :, lanes] for j in range(EDGE)]
            for b in range(edge):
                weight = tap(a, b)
                for j in range(EDGE):
                    column = j + b - half
                    if 0 <= column < EDGE:
                        term = cells[column] * weight
                        total[j] = term if total[j] is None else total[j] + term
        for j in range(EDGE):
            target[i * EDGE + j, :, lanes] = total[j]


def frame_taps(grad, source, target, edge, lanes):
    half = (edge - 1) // 2
    for a in range(edge):
        total = [None] * edge
        for i in range(EDGE):
            row = i + a - half
            if not 0 <= row < EDGE:
                continue
            cells = [source[row * EDGE + j, :, lanes] for j in range(EDGE)]
            for j in range(EDGE):
                own = grad[i * EDGE + j, :, lanes]
                for b in range(edge):
                    column = j + b - half
                    if 0 <= column < EDGE:
                        term = own * cells[column]
                        total[b] = term if total[b] is None else total[b] + term
        for b in range(edge):
            row = a * edge + b
            target[row : row + 1, lanes] = jnp.sum(total[b], axis=0, keepdims=True)


def crop_frames(kinds, base, rows):
    sub = lax.broadcasted_iota(jnp.int32, (SLOTS, rows), 0)
    lane = lax.broadcasted_iota(jnp.int32, (SLOTS, rows), 1)
    place = lax.broadcasted_iota(jnp.int32, (8, ROWS), 1)
    slot = place & (SLOTS - 1)
    cell = place >> 3
    down = (cell * 37) >> 8
    across = cell - down * EDGE
    begin = jnp.zeros((SLOTS, rows), jnp.int32)
    whole = jnp.zeros((SLOTS, rows), jnp.int32)
    begin_row = jnp.zeros((8, ROWS), jnp.int32)
    whole_row = jnp.zeros((8, ROWS), jnp.int32)
    start = jnp.int32(0)
    for s in range(SLOTS):
        large = (kinds[base + s] == 0).astype(jnp.int32)
        begin = jnp.where(sub == s, start, begin)
        whole = jnp.where(sub == s, large, whole)
        begin_row = jnp.where(slot == s, start, begin_row)
        whole_row = jnp.where(slot == s, large, whole_row)
        start = start + 9 + 40 * large
    tiles = []
    for i in range(EDGE):
        for j in range(EDGE):
            small = begin + (i * 3 + j) if i < 3 and j < 3 else jnp.full_like(begin, -1)
            token = jnp.where(whole == 1, begin + (i * EDGE + j), small)
            tiles.append(jnp.where(token == lane, 1.0, 0.0))
    to_frame = jnp.concatenate(tiles, axis=0).astype(BF16)
    corner = jnp.where((down < 3) & (across < 3), begin_row + down * 3 + across, -1)
    token_row = jnp.where(whole_row == 1, begin_row + cell, corner)
    height = lax.broadcasted_iota(jnp.int32, (rows, ROWS), 0)
    to_token = jnp.where(height == token_row[0:1], 1.0, 0.0).astype(BF16)
    return to_frame, to_token


def norm_parts(values):
    average = jnp.mean(values, axis=-1, keepdims=True)
    centred = values - average
    variance = jnp.mean(centred * centred, axis=-1, keepdims=True)
    inverse = lax.rsqrt(variance + EPSILON)
    return centred * inverse, inverse


def norm_back(grad, unit, inverse, gain):
    scaled = grad * gain
    first = jnp.mean(scaled, axis=-1, keepdims=True)
    second = jnp.mean(scaled * unit, axis=-1, keepdims=True)
    return (scaled - first - unit * second) * inverse


def column_sum(values):
    return jnp.sum(values, axis=0, keepdims=True)


def same_head(width):
    rows = lax.broadcasted_iota(jnp.int32, (width, width), 0) // HEAD
    columns = lax.broadcasted_iota(jnp.int32, (width, width), 1) // HEAD
    return rows == columns


def front_kernel(
    image,
    kinds,
    tokens,
    position_kernel,
    position_bias,
    gain,
    shift,
    qkv_weight,
    pair_bias,
    relative_kernel,
    relative_bias,
    output_weight,
    residual_out,
    normed_out,
    query_out,
    weight_out,
    value_out,
    relative_out,
    context_out,
    attended_out,
    partial_out,
    to_frame_out,
    to_token_out,
    grid_in,
    grid_out,
):
    rows = tokens.shape[0]
    width = relative_kernel.shape[2]
    to_frame, to_token = crop_frames(kinds, image() * SLOTS, rows)
    to_frame_out[...] = to_frame
    to_token_out[...] = to_token
    grid_in[...] = mm(to_frame, tokens[...]).reshape(CELLS, SLOTS, D)

    def position(lanes):
        frame_conv(grid_in, lambda a, b: position_kernel[a, b : b + 1, lanes], grid_out, 3, lanes)

    over_lanes(D, position)
    residual = tokens[...].astype(F32) + split_mm(to_token, grid_out[...].reshape(ROWS, D))
    residual = residual + position_bias[...]
    residual_out[...] = residual
    unit, _ = norm_parts(residual)
    normed = (unit * gain[...] + shift[...]).astype(BF16)
    normed_out[...] = normed
    framed = mm(to_frame, normed).astype(BF16)
    valid = mm(to_frame, jnp.ones((rows, width), BF16))
    pair = pair_bias[...].astype(F32)
    query = mm(framed, qkv_weight[:, 0:width]) + valid * pair[0:1]
    keys = mm(framed, qkv_weight[:, width : 2 * width])
    value = mm(framed, qkv_weight[:, 2 * width : 3 * width]) + valid * pair[1:2]
    keys = jnp.where(valid > 0.5, keys, -1e30)
    weight = jnp.exp(keys - jnp.max(keys, axis=0, keepdims=True))
    weight = weight / column_sum(weight)
    value_out[...] = value.reshape(CELLS, SLOTS, width)
    context = jnp.where(same_head(width), t_mm(weight.astype(BF16), value.astype(BF16)), 0.0)

    def relative(lanes):
        frame_conv(
            value_out, lambda a, b: relative_kernel[a, b : b + 1, lanes], relative_out, EDGE, lanes
        )

    over_lanes(width, relative)
    position_term = relative_out[...].reshape(ROWS, width) + relative_bias[...]
    relative_out[...] = position_term.reshape(CELLS, SLOTS, width)
    attended = SCALE * mm(query.astype(BF16), context.astype(BF16)) + query * position_term
    attended = mm(to_token, attended.astype(BF16)).astype(BF16)
    query_out[...] = query
    weight_out[...] = weight
    context_out[...] = context
    attended_out[...] = attended
    partial_out[...] = mm(attended, output_weight[...]).astype(BF16)


def mlp_kernel(
    residual,
    mine,
    other,
    out_grad,
    output_bias,
    gain,
    shift,
    up_weight,
    up_bias,
    down_weight,
    middle_out,
    normed_out,
    hidden_out,
    grad_pre_out,
    grad_bias_out,
    mlp_out,
    grad_normed_out,
):
    hidden_width = up_weight.shape[1]
    projected = mine[...].astype(F32) + other[...].astype(F32)
    middle = residual[...] + projected + output_bias[...]
    middle_out[...] = middle
    unit, _ = norm_parts(middle)
    normed = (unit * gain[...] + shift[...]).astype(BF16)
    normed_out[...] = normed
    step = min(256, hidden_width)
    for begin in range(0, hidden_width, step):
        part = slice(begin, begin + step)
        pre = mm(normed, up_weight[:, part]) + up_bias[:, part].astype(F32)
        below = 0.5 * (1.0 + lax.erf(pre * (2.0**-0.5)))
        hidden_out[:, part] = (pre * below).astype(BF16)
        slope = below + pre * jnp.exp(-0.5 * pre * pre) * ((2.0 * math.pi) ** -0.5)
        grad = (mm_t(out_grad[...], down_weight[part, :]) * slope).astype(BF16)
        grad_pre_out[:, part] = grad
        grad_bias_out[:, part] = column_sum(grad.astype(F32))
    mlp_out[...] = mm(hidden_out[...], down_weight[...]).astype(BF16)
    grad_normed_out[...] = mm_t(grad_pre_out[...], up_weight[...]).astype(BF16)


def back_kernel(
    middle,
    mine,
    other,
    out_grad,
    gain,
    output_weight,
    qkv_weight,
    query,
    weight,
    value,
    relative,
    context,
    relative_kernel,
    to_frame,
    to_token,
    grad_middle_out,
    grad_projected_out,
    grad_qkv_out,
    grad_normed_out,
    wide_sums,
    head_sums,
    grid_grad,
    grid_back,
):
    width = relative_kernel.shape[2]
    unit, inverse = norm_parts(middle[...])
    grad = mine[...].astype(F32) + other[...].astype(F32)
    cotangent = out_grad[...].astype(F32)
    grad_middle = cotangent + norm_back(grad, unit, inverse, gain[...])
    grad_middle_out[...] = grad_middle
    projected = grad_middle.astype(BF16)
    grad_projected_out[...] = projected
    wide_sums[0:1] = column_sum(projected.astype(F32))
    wide_sums[1:2] = column_sum(grad * unit)
    wide_sums[2:3] = column_sum(grad)
    wide_sums[3:4] = column_sum(cotangent)
    wide_sums[4:8] = jnp.zeros((4, D), F32)
    framed = mm(to_frame[...], projected).astype(BF16)
    attended = mm_t(framed, output_weight[...])
    attended_low = attended.astype(BF16)
    query_all = query[...]
    context_low = context[...].astype(BF16)
    grad_relative = attended * query_all
    grid_grad[...] = grad_relative.reshape(CELLS, SLOTS, width)
    relative_all = relative[...].reshape(ROWS, width)
    grad_query = SCALE * mm_t(attended_low, context_low) + attended * relative_all
    grad_context = SCALE * t_mm(query_all.astype(BF16), attended_low)
    grad_context = jnp.where(same_head(width), grad_context, 0.0)
    context_sum = lax.dot_general(
        jnp.ones((8, width), F32),
        grad_context * context[...],
        (((1,), (1,)), ((), ())),
        preferred_element_type=F32,
        precision=lax.Precision.HIGHEST,
    )[0:1]
    grad_context_low = grad_context.astype(BF16)

    def convolve(lanes):
        frame_conv(
            grid_grad,
            lambda a, b: relative_kernel[EDGE - 1 - a, EDGE - 1 - b : EDGE - b, lanes],
            grid_back,
            EDGE,
            lanes,
        )
        frame_taps(grid_grad, value, head_sums, EDGE, lanes)

    over_lanes(width, convolve)
    head_sums[49:50] = column_sum(grad_relative)
    weight_all = weight[...]
    value_low = value[...].reshape(ROWS, width).astype(BF16)
    grad_value = grid_back[...].reshape(ROWS, width) + mm(weight_all.astype(BF16), grad_context_low)
    grad_key = weight_all * (mm_t(value_low, grad_context_low) - context_sum)
    parts = []
    for grad_part in (grad_query, grad_key, grad_value):
        parts.append(mm(to_token[...], grad_part.astype(BF16)))
    head_sums[50:51] = column_sum(parts[0])
    head_sums[51:52] = column_sum(parts[2])
    head_sums[52:56] = jnp.zeros((4, width), F32)
    grad_qkv = jnp.concatenate(parts, axis=1).astype(BF16)
    grad_qkv_out[...] = grad_qkv
    grad_normed_out[...] = mm_t(grad_qkv, qkv_weight[...]).astype(BF16)


def last_kernel(
    tokens,
    residual,
    grad_middle,
    mine,
    other,
    gain,
    position_kernel,
    to_frame,
    to_token,
    middle,
    mlp_mine,
    mlp_other,
    down_bias,
    block_out,
    token_grad,
    sums,
    grid_grad,
    grid_in,
    grid_back,
):
    block_out[...] = (
        middle[...] + (mlp_mine[...].astype(F32) + mlp_other[...].astype(F32)) + down_bias[...]
    )
    unit, inverse = norm_parts(residual[...])
    grad = mine[...].astype(F32) + other[...].astype(F32)
    grad_residual = grad_middle[...] + norm_back(grad, unit, inverse, gain[...])
    grid_grad[...] = split_mm(to_frame[...], grad_residual).reshape(CELLS, SLOTS, D)
    grid_in[...] = mm(to_frame[...], tokens[...]).reshape(CELLS, SLOTS, D)

    def convolve(lanes):
        frame_conv(
            grid_grad,
            lambda a, b: position_kernel[2 - a, 2 - b : 3 - b, lanes],
            grid_back,
            3,
            lanes,
        )
        frame_taps(grid_grad, grid_in, sums, 3, lanes)

    over_lanes(D, convolve)
    token_grad[...] = grad_residual + split_mm(to_token[...], grid_back[...].reshape(ROWS, D))
    sums[9:10] = column_sum(grad_residual)
    sums[10:11] = column_sum(grad * unit)
    sums[11:12] = column_sum(grad)
    sums[12:16] = jnp.zeros((4, D), F32)


def outer_kernel(count, images, split, *refs):
    ins, outs = refs[: 2 * count * images], refs[2 * count * images :]
    core = lax.axis_index("dp") & 1 if split else 0
    for index in range(count):
        pairs = [
            (ins[2 * (index * images + image)], ins[2 * (index * images + image) + 1])
            for image in range(images)
        ]
        height = pairs[0][0].shape[1]
        if split:
            half = height // 2
            plan = [(outs[2 * index], 1 - core), (outs[2 * index + 1], core)]
        else:
            half = height
            plan = [(outs[index], 0)]
        for target, place in plan:
            begin = pl.multiple_of(place * half, 128) if split else 0
            total = None
            for left, right in pairs:
                term = t_mm(left[:, pl.ds(begin, half)], right[...])
                total = term if total is None else total + term
            target[...] = total.astype(target.dtype)


def spread_kernel(count, chips, *refs):
    ins, outs = refs[: 2 * count], refs[2 * count :]
    chip = lax.axis_index("dp") >> 1
    for index in range(count):
        keep, got = ins[2 * index], ins[2 * index + 1]
        chunk = keep.shape[0] // chips
        for step in range(chips):
            rows = pl.ds(pl.multiple_of((chip ^ step) * chunk, 16), chunk)
            total = keep[rows, :].astype(F32) + got[rows, :].astype(F32)
            outs[index * chips + step][...] = total.astype(BF16)


def total_kernel(count, chips, *refs):
    ins, outs = refs[: count * chips], refs[count * chips :]
    for index in range(count):
        total = ins[index * chips][...].astype(F32)
        for step in range(1, chips):
            total = total + ins[index * chips + step][...].astype(F32)
        outs[index][...] = total.astype(BF16)


def place_kernel(count, chips, *refs):
    ins, outs = refs[: count * chips], refs[count * chips :]
    chip = lax.axis_index("dp") >> 1
    for index in range(count):
        chunk = ins[index * chips].shape[0]
        for step in range(chips):
            rows = pl.ds(pl.multiple_of((chip ^ step) * chunk, 16), chunk)
            outs[index][rows, :] = ins[index * chips + step][...]


def widen_kernel(count, *refs):
    ins, outs = refs[: 2 * count], refs[2 * count :]
    core = lax.axis_index("dp") & 1
    for index in range(count):
        mine, other = ins[2 * index], ins[2 * index + 1]
        half = mine.shape[0]
        outs[index][pl.ds(pl.multiple_of(core * half, 16), half), :] = mine[...].astype(F32)
        outs[index][pl.ds(pl.multiple_of((1 - core) * half, 16), half), :] = other[...].astype(F32)


def turn(values, distance, axis="dp"):
    size = lax.axis_size(axis)
    return lax.ppermute(values, axis, [(i, i ^ distance) for i in range(size)])


def outer_products(products, split):
    count, images = len(products), len(products[0])
    args, outs = [], []
    for pairs in products:
        for left, right in pairs:
            args += [left, right]
        height, breadth = pairs[0][0].shape[1], pairs[0][1].shape[1]
        if split:
            outs += [((height // 2, breadth), BF16), ((height // 2, breadth), F32)]
        else:
            outs += [((height, breadth), BF16)]
    return call(functools.partial(outer_kernel, count, images, split), outs, args, us=3.0)


def sum_products(products):
    size = lax.axis_size("dp")
    heights = [pairs[0][0].shape[1] for pairs in products]
    fits = size >= 4 and size & (size - 1) == 0
    fits = fits and all(height % (size * 16) == 0 and height % 256 == 0 for height in heights)
    if not fits:
        whole = outer_products(products, False)
        return [lax.psum(one, "dp").astype(F32) for one in whole]
    count, chips = len(products), size // 2
    halves = outer_products(products, True)
    args = []
    for index in range(count):
        args += [halves[2 * index + 1], turn(halves[2 * index], 1)]
    outs = []
    for index in range(count):
        half, breadth = args[2 * index].shape
        outs += [((half // chips, breadth), BF16)] * chips
    chunks = call(functools.partial(spread_kernel, count, chips), outs, args, us=1.5)
    moved = []
    for index in range(count):
        for step in range(chips):
            chunk = chunks[index * chips + step]
            moved.append(chunk if step == 0 else turn(chunk, 2 * step))
    outs = [(moved[index * chips].shape, BF16) for index in range(count)]
    sums = call(functools.partial(total_kernel, count, chips), outs, moved, us=1.0)
    spread = []
    for index in range(count):
        for step in range(chips):
            spread.append(sums[index] if step == 0 else turn(sums[index], 2 * step))
    outs = [((sums[i].shape[0] * chips, sums[i].shape[1]), BF16) for i in range(count)]
    placed = call(functools.partial(place_kernel, count, chips), outs, spread, us=1.0)
    args, outs = [], []
    for one in placed:
        args += [one, turn(one, 1)]
        outs += [((one.shape[0] * 2, one.shape[1]), F32)]
    return call(functools.partial(widen_kernel, count), outs, args, us=1.5)


def sum_small(values):
    size = lax.axis_size("dp")
    rows, width = values.shape
    if size & (size - 1) or size < 2 or rows % size:
        return lax.psum(values, "dp")
    me = lax.axis_index("dp")
    parts = values.reshape(size, rows // size, width)
    total = None
    for step in range(size):
        part = lax.dynamic_index_in_dim(parts, me ^ step, 0, keepdims=False)
        part = part if step == 0 else turn(part, step)
        total = part if total is None else total + part
    out = parts
    for step in range(size):
        piece = total if step == 0 else turn(total, step)
        out = lax.dynamic_update_index_in_dim(out, piece, me ^ step, 0)
    return out.reshape(rows, width)


def per_device(
    tokens,
    out_grad,
    crop_image,
    crop_res,
    position_kernel,
    position_bias,
    gain_one,
    shift_one,
    qkv_weight,
    query_value_bias,
    relative_three,
    relative_five,
    relative_seven,
    relative_bias,
    output_weight,
    output_bias,
    gain_two,
    shift_two,
    up_weight,
    up_bias,
    down_weight,
    down_bias,
):
    group = lax.axis_size("mp")
    member = lax.axis_index("mp")
    rows = tokens.shape[0]
    width = qkv_weight.shape[2]
    hidden_width = up_weight.shape[1]
    pair = group == 2

    def row(vector):
        return vector.reshape(1, -1)

    full_kernel = jnp.concatenate(
        [
            jnp.pad(relative_three, ((2, 2), (2, 2), (0, 0))),
            jnp.pad(relative_five, ((1, 1), (1, 1), (0, 0))),
            relative_seven,
        ],
        axis=2,
    )
    kernel_part = lax.dynamic_slice_in_dim(full_kernel, member * width, width, 2)
    bias_part = row(lax.dynamic_slice_in_dim(relative_bias, member * width, width, 0))
    qkv_matrix = qkv_weight.reshape(D, 3 * width)

    if pair:
        token_list = [tokens, turn(tokens, 1, "mp")]
        grad_list = [out_grad, turn(out_grad, 1, "mp")]
        images = [lambda: lax.axis_index("mp"), lambda: 1 - lax.axis_index("mp")]
    else:
        token_list = list(lax.all_gather(tokens, "mp", axis=0))
        grad_list = list(lax.all_gather(out_grad, "mp", axis=0))
        images = [functools.partial(int, j) for j in range(group)]

    def meet(parts):
        if pair:
            return [(parts[0], turn(parts[1], 1, "mp")), (parts[1], turn(parts[0], 1, "mp"))]
        total = lax.psum(jnp.stack(parts), "mp")
        return [(one, jnp.zeros_like(one)) for one in total]

    def meet_own(parts):
        if pair:
            return parts[0], turn(parts[1], 1, "mp")
        total = lax.psum_scatter(jnp.concatenate(parts), "mp", scatter_dimension=0, tiled=True)
        return total, jnp.zeros_like(total)

    def own(parts):
        if pair:
            return parts[0]
        return lax.dynamic_index_in_dim(jnp.stack(parts), member, 0, keepdims=False)

    fronts = []
    for image, one in zip(images, token_list):
        outs = [
            ((rows, D), F32),
            ((rows, D), BF16),
            ((ROWS, width), F32),
            ((ROWS, width), F32),
            ((CELLS, SLOTS, width), F32),
            ((CELLS, SLOTS, width), F32),
            ((width, width), F32),
            ((rows, width), BF16),
            ((rows, D), BF16),
            ((ROWS, rows), BF16),
            ((rows, ROWS), BF16),
        ]
        args = (
            crop_res,
            one,
            position_kernel,
            row(position_bias),
            row(gain_one),
            row(shift_one),
            qkv_matrix,
            query_value_bias,
            kernel_part,
            bias_part,
            output_weight,
        )
        scratch = [pltpu.VMEM((CELLS, SLOTS, D), F32)] * 2
        fronts.append(
            call(functools.partial(front_kernel, image), outs, args, scratch, us=7.0, smem=1)
        )
    residual, normed, query, weight, value, relative, context, attended, partial, to_frame, to_token = zip(
        *fronts
    )
    mlps = []
    for index, (mine, other) in enumerate(meet(partial)):
        outs = [
            ((rows, D), F32),
            ((rows, D), BF16),
            ((rows, hidden_width), BF16),
            ((rows, hidden_width), BF16),
            ((1, hidden_width), F32),
            ((rows, D), BF16),
            ((rows, D), BF16),
        ]
        args = (
            residual[index],
            mine,
            other,
            grad_list[index],
            row(output_bias),
            row(gain_two),
            row(shift_two),
            up_weight,
            row(up_bias),
            down_weight,
        )
        mlps.append(call(mlp_kernel, outs, args, us=5.0))
    middle, normed_two, hidden, grad_pre, grad_up_bias, mlp_part, grad_two_part = zip(*mlps)
    grad_up, grad_down = sum_products(
        [list(zip(normed_two, grad_pre)), list(zip(hidden, grad_list))]
    )
    backs = []
    for index, (mine, other) in enumerate(meet(grad_two_part)):
        outs = [
            ((rows, D), F32),
            ((rows, D), BF16),
            ((rows, 3 * width), BF16),
            ((rows, D), BF16),
            ((8, D), F32),
            ((56, width), F32),
        ]
        args = (
            middle[index],
            mine,
            other,
            grad_list[index],
            row(gain_two),
            output_weight,
            qkv_matrix,
            query[index],
            weight[index],
            value[index],
            relative[index],
            context[index],
            kernel_part,
            to_frame[index],
            to_token[index],
        )
        scratch = [pltpu.VMEM((CELLS, SLOTS, width), F32)] * 2
        backs.append(call(back_kernel, outs, args, scratch, us=8.0))
    grad_middle, grad_projected, grad_qkv, grad_one_part, wide_sums, head_sums = zip(*backs)
    grad_out, grad_qkv_matrix = sum_products(
        [list(zip(attended, grad_projected)), list(zip(normed, grad_qkv))]
    )
    one_mine, one_other = meet_own(grad_one_part)
    mlp_mine, mlp_other = meet_own(mlp_part)
    outs = [((rows, D), F32), ((rows, D), F32), ((16, D), F32)]
    args = (
        tokens,
        own(residual),
        own(grad_middle),
        one_mine,
        one_other,
        row(gain_one),
        position_kernel,
        own(to_frame),
        own(to_token),
        own(middle),
        mlp_mine,
        mlp_other,
        row(down_bias),
    )
    scratch = [pltpu.VMEM((CELLS, SLOTS, D), F32)] * 3
    block_out, token_grad, own_sums = call(last_kernel, outs, args, scratch, us=5.0)

    head_total = functools.reduce(jnp.add, head_sums)
    wide_total = functools.reduce(jnp.add, wide_sums)
    bias_total = functools.reduce(jnp.add, grad_up_bias)
    if pair:
        own_total = own_sums + turn(own_sums, 1, "mp")
        relative_rows = head_total[:50]
        far = turn(relative_rows, 1, "mp")
        first = jnp.where(member == 0, relative_rows, far)
        second = jnp.where(member == 0, far, relative_rows)
        relative_total = jnp.concatenate([first, second], axis=1)
    else:
        own_total = lax.psum(own_sums, "mp")
        relative_total = lax.all_gather(head_total[:50], "mp", axis=1, tiled=True)
    pieces = [own_total[:12], wide_total[:4], relative_total]
    private = jnp.concatenate([bias_total.reshape(-1), head_total[50:52].reshape(-1)])
    pieces.append(jnp.pad(private, (0, -private.shape[0] % D)).reshape(-1, D))
    packed = jnp.concatenate(pieces, axis=0)
    size = lax.axis_size("dp")
    total = sum_small(jnp.pad(packed, ((0, -packed.shape[0] % size), (0, 0))))
    kernel_grad = total[16:65].reshape(EDGE, EDGE, D)
    tail = total[66:].reshape(-1)
    return (
        block_out,
        token_grad,
        total[:9].reshape(3, 3, D),
        total[9],
        total[10],
        total[11],
        grad_qkv_matrix.reshape(D, 3, width),
        tail[hidden_width : hidden_width + 2 * width].reshape(2, width),
        kernel_grad[2:5, 2:5, : 2 * HEAD],
        kernel_grad[1:6, 1:6, 2 * HEAD : 5 * HEAD],
        kernel_grad[:, :, 5 * HEAD :],
        total[65],
        grad_out,
        total[12],
        total[13],
        total[14],
        grad_up,
        tail[:hidden_width],
        grad_down,
        total[15],
    )


def solution(mesh):
    in_specs = (
        P(("dp", "mp"), None),
        P(("dp", "mp"), None),
        P("dp"),
        P("dp"),
        P(),
        P(),
        P(),
        P(),
        P(None, None, "mp"),
        P(None, "mp"),
        P(),
        P(),
        P(),
        P(),
        P("mp", None),
        P(),
        P(),
        P(),
        P(None, "mp"),
        P("mp"),
        P("mp", None),
        P(),
    )
    out_specs = (
        P(("dp", "mp"), None),
        P(("dp", "mp"), None),
        P(),
        P(),
        P(),
        P(),
        P(None, None, "mp"),
        P(None, "mp"),
        P(),
        P(),
        P(),
        P(),
        P("mp", None),
        P(),
        P(),
        P(),
        P(None, "mp"),
        P("mp"),
        P("mp", None),
        P(),
    )
    return jax.shard_map(
        per_device, mesh=mesh, in_specs=in_specs, out_specs=out_specs, check_vma=False
    )
```

```python
import functools
import math

import jax
import jax.numpy as jnp
from jax import lax
from jax.experimental import pallas as pl
from jax.experimental.pallas import tpu as pltpu
from jax.sharding import PartitionSpec as P

HEAD = 64
D = 512
EPSILON = 1e-06
SLOTS = 8
EDGE = 7
CELLS = EDGE * EDGE
ROWS = CELLS * SLOTS
SCALE = HEAD ** (-0.5)
BF16 = jnp.bfloat16
F32 = jnp.float32


def mm(left, right):
    return jnp.dot(left, right, preferred_element_type=F32)


def mm_t(left, right):
    return lax.dot_general(left, right, (((1,), (1,)), ((), ())), preferred_element_type=F32)


def t_mm(left, right):
    return lax.dot_general(left, right, (((0,), (0,)), ((), ())), preferred_element_type=F32)


def split_mm(onehot, values):
    high = values.astype(BF16)
    low = (values - high.astype(F32)).astype(BF16)
    return mm(onehot, high) + mm(onehot, low)


class Source:
    def __init__(self, ref, copy):
        self.held, self.copy, self.shape = ref, copy, ref.shape

    def ref(self):
        if self.copy is not None:
            self.copy.wait()
            self.copy = None
        return self.held

    def __getitem__(self, index):
        return self.ref()[index]


class Result:
    def __init__(self, ref, copy):
        self.held, self.copy, self.sent, self.shape = ref, copy, False, ref.shape

    def __setitem__(self, index, value):
        self.held[index] = value

    def __getitem__(self, index):
        return self.held[index]

    def send(self):
        self.copy.start()
        self.sent = True


def call(body, outs, args, scratch=(), us=3.0, smem=0, vmem=24):
    arrays = args[smem:]
    sources, results = len(arrays), len(outs)

    def kernel(*refs):
        refs = list(refs)

        def take(count):
            taken = refs[:count]
            del refs[:count]
            return taken

        scalars, far_in, far_out = take(smem), take(sources), take(results)
        near_in, near_out = take(sources), take(results)
        (in_sems,) = take(1)
        (out_sems,) = take(1)
        ins = []
        for index, (far, near) in enumerate(zip(far_in, near_in)):
            copy = pltpu.make_async_copy(far, near, in_sems.at[index])
            copy.start()
            ins.append(Source(near, copy))
        made = [
            Result(near, pltpu.make_async_copy(near, far, out_sems.at[index]))
            for index, (far, near) in enumerate(zip(far_out, near_out))
        ]
        body(scalars, ins, made, refs)
        for one in made:
            if not one.sent:
                one.send()
        for one in ins:
            one.ref()
        for one in made:
            one.copy.wait()

    shapes = [pltpu.VMEM(one.shape, one.dtype) for one in arrays]
    shapes += [pltpu.VMEM(shape, kind) for shape, kind in outs]
    shapes += [pltpu.SemaphoreType.DMA((sources,)), pltpu.SemaphoreType.DMA((results,))]
    return pl.pallas_call(
        kernel,
        out_shape=[jax.ShapeDtypeStruct(shape, kind) for shape, kind in outs],
        in_specs=[pl.BlockSpec(memory_space=pltpu.SMEM)] * smem
        + [pl.BlockSpec(memory_space=pl.ANY)] * sources,
        out_specs=[pl.BlockSpec(memory_space=pl.ANY)] * results,
        scratch_shapes=shapes + list(scratch),
        compiler_params=pltpu.CompilerParams(vmem_limit_bytes=vmem << 20),
        cost_estimate=pl.CostEstimate(
            flops=int(us * 1.0e9), bytes_accessed=1 << 18, transcendentals=0
        ),
    )(*args)


def over_lanes(width, body):
    if width % 128 == 0:

        @pl.loop(0, width // 128)
        def _(step):
            body(pl.ds(pl.multiple_of(step * 128, 128), 128))

    else:
        body(slice(0, width))


def frame_conv(source, tap, target, edge, lanes):
    half = (edge - 1) // 2
    for i in range(EDGE):
        total = [None] * EDGE
        for a in range(edge):
            row = i + a - half
            if not 0 <= row < EDGE:
                continue
            cells = [source[row * EDGE + j, :, lanes] for j in range(EDGE)]
            for b in range(edge):
                weight = tap(a, b)
                for j in range(EDGE):
                    column = j + b - half
                    if 0 <= column < EDGE:
                        term = cells[column] * weight
                        total[j] = term if total[j] is None else total[j] + term
        for j in range(EDGE):
            target[i * EDGE + j, :, lanes] = total[j]


def frame_taps(grad, source, target, edge, lanes):
    half = (edge - 1) // 2
    for a in range(edge):
        total = [None] * edge
        for i in range(EDGE):
            row = i + a - half
            if not 0 <= row < EDGE:
                continue
            cells = [source[row * EDGE + j, :, lanes] for j in range(EDGE)]
            for j in range(EDGE):
                own = grad[i * EDGE + j, :, lanes]
                for b in range(edge):
                    column = j + b - half
                    if 0 <= column < EDGE:
                        term = own * cells[column]
                        total[b] = term if total[b] is None else total[b] + term
        for b in range(edge):
            row = a * edge + b
            target[row : row + 1, lanes] = jnp.sum(total[b], axis=0, keepdims=True)


def crop_frames(kinds, base, rows):
    sub = lax.broadcasted_iota(jnp.int32, (SLOTS, rows), 0)
    lane = lax.broadcasted_iota(jnp.int32, (SLOTS, rows), 1)
    place = lax.broadcasted_iota(jnp.int32, (8, ROWS), 1)
    slot = place & (SLOTS - 1)
    cell = place >> 3
    down = (cell * 37) >> 8
    across = cell - down * EDGE
    begin = jnp.zeros((SLOTS, rows), jnp.int32)
    whole = jnp.zeros((SLOTS, rows), jnp.int32)
    begin_row = jnp.zeros((8, ROWS), jnp.int32)
    whole_row = jnp.zeros((8, ROWS), jnp.int32)
    start = jnp.int32(0)
    for s in range(SLOTS):
        large = (kinds[base + s] == 0).astype(jnp.int32)
        begin = jnp.where(sub == s, start, begin)
        whole = jnp.where(sub == s, large, whole)
        begin_row = jnp.where(slot == s, start, begin_row)
        whole_row = jnp.where(slot == s, large, whole_row)
        start = start + 9 + 40 * large
    tiles = []
    for i in range(EDGE):
        for j in range(EDGE):
            small = begin + (i * 3 + j) if i < 3 and j < 3 else jnp.full_like(begin, -1)
            token = jnp.where(whole == 1, begin + (i * EDGE + j), small)
            tiles.append(jnp.where(token == lane, 1.0, 0.0))
    to_frame = jnp.concatenate(tiles, axis=0).astype(BF16)
    corner = jnp.where((down < 3) & (across < 3), begin_row + down * 3 + across, -1)
    token_row = jnp.where(whole_row == 1, begin_row + cell, corner)
    height = lax.broadcasted_iota(jnp.int32, (rows, ROWS), 0)
    to_token = jnp.where(height == token_row[0:1], 1.0, 0.0).astype(BF16)
    return to_frame, to_token


def norm_parts(values):
    average = jnp.mean(values, axis=-1, keepdims=True)
    centred = values - average
    variance = jnp.mean(centred * centred, axis=-1, keepdims=True)
    inverse = lax.rsqrt(variance + EPSILON)
    return centred * inverse, inverse


def norm_back(grad, unit, inverse, gain):
    scaled = grad * gain
    first = jnp.mean(scaled, axis=-1, keepdims=True)
    second = jnp.mean(scaled * unit, axis=-1, keepdims=True)
    return (scaled - first - unit * second) * inverse


def column_sum(values):
    return jnp.sum(values, axis=0, keepdims=True)


def same_head(width):
    rows = lax.broadcasted_iota(jnp.int32, (width, width), 0) // HEAD
    columns = lax.broadcasted_iota(jnp.int32, (width, width), 1) // HEAD
    return rows == columns


def front_body(image, keep_grad, scalars, ins, outs, scratch):
    (kinds,) = scalars
    (
        tokens,
        position_kernel,
        position_bias,
        gain,
        shift,
        qkv_weight,
        pair_bias,
        relative_kernel,
        relative_bias,
        output_weight,
    ) = ins[:10]
    (
        residual_out,
        normed_out,
        query_out,
        weight_out,
        value_out,
        relative_out,
        context_out,
        attended_out,
        partial_out,
        to_frame_out,
        to_token_out,
    ) = outs
    grid_in, grid_out = scratch
    rows = tokens.shape[0]
    width = relative_kernel.shape[2]
    to_frame, to_token = crop_frames(kinds, image() * SLOTS, rows)
    to_frame_out[...] = to_frame
    to_frame_out.send()
    to_token_out[...] = to_token
    to_token_out.send()
    grid_in[...] = mm(to_frame, tokens[...]).reshape(CELLS, SLOTS, D)
    position_taps = position_kernel.ref()

    def position(lanes):
        frame_conv(grid_in, lambda a, b: position_taps[a, b : b + 1, lanes], grid_out, 3, lanes)

    over_lanes(D, position)
    residual = tokens[...].astype(F32) + split_mm(to_token, grid_out[...].reshape(ROWS, D))
    residual = residual + position_bias[...]
    residual_out[...] = residual
    residual_out.send()
    unit, _ = norm_parts(residual)
    normed = (unit * gain[...] + shift[...]).astype(BF16)
    normed_out[...] = normed
    normed_out.send()
    framed = mm(to_frame, normed).astype(BF16)
    valid = mm(to_frame, jnp.ones((rows, width), BF16))
    pair = pair_bias[...].astype(F32)
    query = mm(framed, qkv_weight[0]) + valid * pair[0:1]
    query_out[...] = query
    query_out.send()
    keys = mm(framed, qkv_weight[1])
    value = mm(framed, qkv_weight[2]) + valid * pair[1:2]
    keys = jnp.where(valid > 0.5, keys, -1e30)
    weight = jnp.exp(keys - jnp.max(keys, axis=0, keepdims=True))
    weight = weight / column_sum(weight)
    weight_out[...] = weight
    weight_out.send()
    value_out[...] = value.reshape(CELLS, SLOTS, width)
    value_out.send()
    context = jnp.where(same_head(width), t_mm(weight.astype(BF16), value.astype(BF16)), 0.0)
    context_out[...] = context
    context_out.send()
    relative_taps = relative_kernel.ref()

    def relative(lanes):
        frame_conv(
            value_out,
            lambda a, b: relative_taps[a, b : b + 1, lanes],
            relative_out,
            EDGE,
            lanes,
        )

    over_lanes(width, relative)
    position_term = relative_out[...].reshape(ROWS, width) + relative_bias[...]
    relative_out[...] = position_term.reshape(CELLS, SLOTS, width)
    relative_out.send()
    attended = SCALE * mm(query.astype(BF16), context.astype(BF16)) + query * position_term
    attended = mm(to_token, attended.astype(BF16)).astype(BF16)
    attended_out[...] = attended
    attended_out.send()
    partial = mm(attended, output_weight[...]).astype(BF16)
    if keep_grad:
        partial_out[0] = partial
        partial_out[1] = ins[10][...]
    else:
        partial_out[...] = partial


def mlp_body(images, scalars, ins, outs, scratch):
    output_bias, gain, shift, up_weight, up_bias, down_weight = ins[:6]
    residuals = ins[6 : 6 + len(images)]
    others = ins[6 + len(images) :]
    grad_normed_out, mlp_out, grad_bias_out = outs[:3]
    hidden_width = up_weight.shape[1]

    def pick(place):
        index, part = place
        return others[index][...] if part is None else others[index][part]

    bias_total = None
    for image, (first, second, cotangent) in enumerate(images):
        middle_out, normed_out, hidden_out, grad_pre_out = outs[3 + 4 * image : 7 + 4 * image]
        projected = pick(first).astype(F32) + pick(second).astype(F32)
        middle = residuals[image][...] + projected + output_bias[...]
        middle_out[...] = middle
        middle_out.send()
        unit, _ = norm_parts(middle)
        normed = (unit * gain[...] + shift[...]).astype(BF16)
        normed_out[...] = normed
        normed_out.send()
        out_grad = pick(cotangent)
        step = min(256, hidden_width)
        sums = []
        for begin in range(0, hidden_width, step):
            part = slice(begin, begin + step)
            pre = mm(normed, up_weight[:, part]) + up_bias[:, part]
            below = 0.5 * (1.0 + lax.erf(pre * (2.0**-0.5)))
            hidden_out[:, part] = (pre * below).astype(BF16)
            slope = below + pre * jnp.exp(-0.5 * pre * pre) * ((2.0 * math.pi) ** -0.5)
            grad = (mm_t(out_grad, down_weight[part, :]) * slope).astype(BF16)
            grad_pre_out[:, part] = grad
            sums.append(column_sum(grad.astype(F32)))
        hidden_out.send()
        grad_pre_out.send()
        sums = jnp.concatenate(sums, axis=1)
        bias_total = sums if bias_total is None else bias_total + sums
        grad_normed_out[image] = mm_t(grad_pre_out[...], up_weight[...]).astype(BF16)
        mlp_out[image] = mm(hidden_out[...], down_weight[...]).astype(BF16)
    grad_bias_out[...] = bias_total


def back_body(place, scalars, ins, outs, scratch):
    (
        mine,
        other,
        middle,
        out_grad,
        gain,
        output_weight,
        qkv_weight,
        query,
        weight,
        value,
        relative,
        context,
        relative_kernel,
        to_frame,
        to_token,
    ) = ins
    grad_middle_out, projected_out, grad_qkv_out, grad_normed_out, wide_sums, head_sums = outs
    grid_grad, grid_back = scratch
    width = relative_kernel.shape[2]
    unit, inverse = norm_parts(middle[...])
    grad = mine[place[0]].astype(F32) + other[place[1]].astype(F32)
    cotangent = out_grad[...] if len(out_grad.shape) == 2 else out_grad[1]
    cotangent = cotangent.astype(F32)
    grad_middle = cotangent + norm_back(grad, unit, inverse, gain[...])
    grad_middle_out[...] = grad_middle
    grad_middle_out.send()
    projected = grad_middle.astype(BF16)
    projected_out[...] = projected
    projected_out.send()
    wide_sums[0:1] = column_sum(projected.astype(F32))
    wide_sums[1:2] = column_sum(grad * unit)
    wide_sums[2:3] = column_sum(grad)
    wide_sums[3:4] = column_sum(cotangent)
    wide_sums[4:8] = jnp.zeros((4, D), F32)
    wide_sums.send()
    framed = mm(to_frame[...], projected).astype(BF16)
    attended = mm_t(framed, output_weight[...])
    attended_low = attended.astype(BF16)
    query_all = query[...]
    context_low = context[...].astype(BF16)
    grad_relative = attended * query_all
    grid_grad[...] = grad_relative.reshape(CELLS, SLOTS, width)
    relative_all = relative[...].reshape(ROWS, width)
    grad_query = SCALE * mm_t(attended_low, context_low) + attended * relative_all
    grad_context = SCALE * t_mm(query_all.astype(BF16), attended_low)
    grad_context = jnp.where(same_head(width), grad_context, 0.0)
    context_sum = lax.dot_general(
        jnp.ones((8, width), F32),
        grad_context * context[...],
        (((1,), (1,)), ((), ())),
        preferred_element_type=F32,
        precision=lax.Precision.HIGHEST,
    )[0:1]
    grad_context_low = grad_context.astype(BF16)
    taps, grid_value = relative_kernel.ref(), value.ref()

    def convolve(lanes):
        frame_conv(
            grid_grad,
            lambda a, b: taps[EDGE - 1 - a, EDGE - 1 - b : EDGE - b, lanes],
            grid_back,
            EDGE,
            lanes,
        )
        frame_taps(grid_grad, grid_value, head_sums, EDGE, lanes)

    over_lanes(width, convolve)
    head_sums[49:50] = column_sum(grad_relative)
    weight_all = weight[...]
    value_low = value[...].reshape(ROWS, width).astype(BF16)
    grad_value = grid_back[...].reshape(ROWS, width) + mm(weight_all.astype(BF16), grad_context_low)
    grad_key = weight_all * (mm_t(value_low, grad_context_low) - context_sum)
    parts = []
    for grad_part in (grad_query, grad_key, grad_value):
        parts.append(mm(to_token[...], grad_part.astype(BF16)))
    head_sums[50:51] = column_sum(parts[0])
    head_sums[51:52] = column_sum(parts[2])
    head_sums[52:56] = jnp.zeros((4, width), F32)
    head_sums.send()
    grad_normed = None
    for index in range(3):
        low = parts[index].astype(BF16)
        grad_qkv_out[index] = low
        term = mm_t(low, qkv_weight[index])
        grad_normed = term if grad_normed is None else grad_normed + term
    grad_qkv_out.send()
    grad_normed_out[...] = grad_normed.astype(BF16)


def last_body(scalars, ins, outs, scratch):
    (
        tokens,
        residual,
        grad_middle,
        mine,
        other,
        gain,
        position_kernel,
        to_frame,
        to_token,
        middle,
        down_bias,
    ) = ins
    block_out, token_grad, sums = outs
    grid_grad, grid_in, grid_back = scratch
    block_out[...] = (
        middle[...] + (mine[1].astype(F32) + other[1].astype(F32)) + down_bias[...]
    )
    block_out.send()
    unit, inverse = norm_parts(residual[...])
    grad = mine[0].astype(F32) + other[0].astype(F32)
    grad_residual = grad_middle[...] + norm_back(grad, unit, inverse, gain[...])
    grid_grad[...] = split_mm(to_frame[...], grad_residual).reshape(CELLS, SLOTS, D)
    grid_in[...] = mm(to_frame[...], tokens[...]).reshape(CELLS, SLOTS, D)
    taps = position_kernel.ref()

    def convolve(lanes):
        frame_conv(
            grid_grad, lambda a, b: taps[2 - a, 2 - b : 3 - b, lanes], grid_back, 3, lanes
        )
        frame_taps(grid_grad, grid_in, sums, 3, lanes)

    over_lanes(D, convolve)
    token_grad[...] = grad_residual + split_mm(to_token[...], grid_back[...].reshape(ROWS, D))
    token_grad.send()
    sums[9:10] = column_sum(grad_residual)
    sums[10:11] = column_sum(grad * unit)
    sums[11:12] = column_sum(grad)
    sums[12:16] = jnp.zeros((4, D), F32)


def turn(values, distance, axis="dp"):
    size = lax.axis_size(axis)
    return lax.ppermute(values, axis, [(i, i ^ distance) for i in range(size)])


def step_bits():
    bits = list(range(1, lax.axis_size("dp").bit_length() - 1))
    return bits, bits[1:] + bits[:1]


def step_turn(values, step):
    orders = step_bits()
    size = lax.axis_size("dp")
    return lax.ppermute(values, "dp", [(i, i ^ (1 << orders[i & 1][step])) for i in range(size)])


def step_side(step):
    first, second = step_bits()
    me = lax.axis_index("dp")
    return (me >> jnp.where(me & 1 == 0, first[step], second[step])) & 1


def rows_of(side, count):
    return pl.ds(pl.multiple_of(side * count, 16), count)


def mlp_grads(ins, images, tiles):
    normed, grad_pre = ins[:images], ins[images : 2 * images]
    hidden, out_grad = ins[2 * images : 3 * images], ins[3 * images : 4 * images]

    def cotangent(image):
        one = out_grad[image]
        return one[...] if len(one.shape) == 2 else one[1]

    def part(which, tile):
        columns = slice(tile * D, (tile + 1) * D)
        total = None
        for image in range(images):
            if which == 0:
                term = t_mm(normed[image][...], grad_pre[image][:, columns])
            else:
                term = t_mm(hidden[image][:, columns], cotangent(image))
            total = term if total is None else total + term
        return total

    return part


def mlp_grads_body(images, scalars, ins, outs, scratch):
    keep, send = outs
    tiles = keep.shape[0] // D
    part = mlp_grads(ins, images, tiles)
    for one in ins:
        one.ref()
    core = lax.axis_index("dp") & 1
    for side in range(2):

        @pl.when(core == side)
        def _():
            for tile in range(tiles):
                rows = slice(tile * D, (tile + 1) * D)
                keep[rows, :] = part(side, tile).astype(BF16)
                send[rows, :] = part(1 - side, tile).astype(BF16)


def attention_grads_body(images, scalars, ins, outs, scratch):
    keep, send = outs
    normed, grad_qkv = ins[:images], ins[images : 2 * images]
    attended, projected = ins[2 * images : 3 * images], ins[3 * images :]
    width = D // 2
    for one in ins:
        one.ref()

    def total(term):
        out = None
        for image in range(images):
            out = term(image) if out is None else out + term(image)
        return out.astype(BF16)

    def write(which, target):
        if which == 0:
            for index in range(2):
                target[:, index * width : (index + 1) * width] = total(
                    lambda image: t_mm(normed[image][...], grad_qkv[image][index])
                )
        else:
            target[0:width, :] = total(
                lambda image: t_mm(attended[image][...], projected[image][...])
            )
            for index in range(2):
                columns = slice(index * width, (index + 1) * width)
                target[width:, columns] = total(
                    lambda image: t_mm(normed[image][:, columns], grad_qkv[image][2])
                )

    core = lax.axis_index("dp") & 1
    for side in range(2):

        @pl.when(core == side)
        def _():
            write(side, keep)
            write(1 - side, send)


def halve_body(step, scalars, ins, outs, scratch):
    here, came = ins
    here.ref()
    came.ref()
    if len(outs) == 1:
        outs[0][...] = (here[...].astype(F32) + came[...].astype(F32)).astype(BF16)
        return
    stay, go = outs
    count = stay.shape[0]
    side = step_side(step)
    for target, place in ((go, 1 - side), (stay, side)):
        rows = rows_of(place, count)
        target[...] = (here[rows, :].astype(F32) + came[rows, :].astype(F32)).astype(BF16)
        target.send()


def join_body(step, scalars, ins, outs, scratch):
    here, came = ins
    side = step_side(step)
    count = here.shape[0]
    outs[0][rows_of(side, count), :] = here[...]
    outs[0][rows_of(1 - side, count), :] = came[...]


def mlp_final_body(scalars, ins, outs, scratch):
    mine, other = ins
    grad_up, grad_down = outs
    mine.ref()
    other.ref()
    core = lax.axis_index("dp") & 1
    for side in range(2):

        @pl.when(core == side)
        def _():
            up, down = (mine, other) if side == 0 else (other, mine)
            for tile in range(down.shape[0] // D):
                rows = slice(tile * D, (tile + 1) * D)
                grad_up[:, rows] = up[rows, :].astype(F32)
            grad_down[...] = down[...].astype(F32)


def attention_final_body(scalars, ins, outs, scratch):
    mine, other = ins
    grad_qkv, grad_out = outs
    width = D // 2
    mine.ref()
    other.ref()
    core = lax.axis_index("dp") & 1
    for side in range(2):

        @pl.when(core == side)
        def _():
            first, second = (mine, other) if side == 0 else (other, mine)
            for index in range(2):
                columns = slice(index * width, (index + 1) * width)
                grad_qkv[index] = first[:, columns].astype(F32)
                grad_qkv[2, columns, :] = second[width:, columns].astype(F32)
            grad_out[...] = second[0:width, :].astype(F32)


def sum_blocks(keep, send):
    steps = len(step_bits()[0])
    came = turn(send, 1)
    for step in range(steps):
        rows = keep.shape[0] // 2
        outs = [((rows, D), BF16)] * 2
        keep, send = call(functools.partial(halve_body, step), outs, (keep, came), us=0.7)
        came = step_turn(send, step)
    (keep,) = call(functools.partial(halve_body, None), [(keep.shape, BF16)], (keep, came), us=0.7)
    for step in reversed(range(steps)):
        came = step_turn(keep, step)
        outs = [((keep.shape[0] * 2, D), BF16)]
        (keep,) = call(functools.partial(join_body, step), outs, (keep, came), us=0.7)
    return keep, turn(keep, 1)


def sum_small(values):
    size = lax.axis_size("dp")
    if size & (size - 1):
        return lax.psum(values, "dp")
    for bit in range(size.bit_length() - 1):
        values = values + turn(values, 1 << bit)
    return values


def whole_body(products, scalars, ins, outs, scratch):
    for target, pairs in zip(outs, products):
        total = None
        for left, right in pairs:
            one, two = (ins[i][...] if part is None else ins[i][part] for i, part in (left, right))
            term = t_mm(one, two)
            total = term if total is None else total + term
        target[...] = total.astype(BF16)


def per_device(
    tokens,
    out_grad,
    crop_image,
    crop_res,
    position_kernel,
    position_bias,
    gain_one,
    shift_one,
    qkv_weight,
    query_value_bias,
    relative_three,
    relative_five,
    relative_seven,
    relative_bias,
    output_weight,
    output_bias,
    gain_two,
    shift_two,
    up_weight,
    up_bias,
    down_weight,
    down_bias,
):
    group = lax.axis_size("mp")
    member = lax.axis_index("mp")
    rows = tokens.shape[0]
    width = qkv_weight.shape[2]
    hidden_width = up_weight.shape[1]
    pair = group == 2
    size = lax.axis_size("dp")
    blocks = (
        size >= 8
        and size & (size - 1) == 0
        and 2 * width == D
        and hidden_width % D == 0
        and D % (size * 8) == 0
    )

    def row(vector):
        return vector.reshape(1, -1)

    full_kernel = jnp.concatenate(
        [
            jnp.pad(relative_three, ((2, 2), (2, 2), (0, 0))),
            jnp.pad(relative_five, ((1, 1), (1, 1), (0, 0))),
            relative_seven,
        ],
        axis=2,
    )
    kernel_part = lax.dynamic_slice_in_dim(full_kernel, member * width, width, 2)
    bias_part = row(lax.dynamic_slice_in_dim(relative_bias, member * width, width, 0))
    qkv_planes = jnp.transpose(qkv_weight, (1, 0, 2))

    if pair:
        token_list = [tokens, turn(tokens, 1, "mp")]
        images = [lambda: lax.axis_index("mp"), lambda: 1 - lax.axis_index("mp")]
    else:
        token_list = list(lax.all_gather(tokens, "mp", axis=0))
        grad_list = list(lax.all_gather(out_grad, "mp", axis=0))
        images = [functools.partial(int, j) for j in range(group)]

    def own(parts):
        if pair:
            return parts[0]
        return lax.dynamic_index_in_dim(jnp.stack(parts), member, 0, keepdims=False)

    fronts = []
    for index, (image, one) in enumerate(zip(images, token_list)):
        carry = pair and index == 0
        outs = [
            ((rows, D), F32),
            ((rows, D), BF16),
            ((ROWS, width), F32),
            ((ROWS, width), F32),
            ((CELLS, SLOTS, width), F32),
            ((CELLS, SLOTS, width), F32),
            ((width, width), F32),
            ((rows, width), BF16),
            ((2, rows, D) if carry else (rows, D), BF16),
            ((ROWS, rows), BF16),
            ((rows, ROWS), BF16),
        ]
        args = (
            crop_res,
            one,
            position_kernel,
            row(position_bias),
            row(gain_one),
            row(shift_one),
            qkv_planes,
            query_value_bias,
            kernel_part,
            bias_part,
            output_weight,
        )
        if carry:
            args += (out_grad,)
        scratch = [pltpu.VMEM((CELLS, SLOTS, D), F32)] * 2
        body = functools.partial(front_body, image, carry)
        fronts.append(call(body, outs, args, scratch, us=5.0, smem=1))
    residual, normed, query, weight, value, relative, context, attended, partial, to_frame, to_token = zip(
        *fronts
    )

    if pair:
        first, second = turn(partial[0], 1, "mp"), turn(partial[1], 1, "mp")
        addends = (partial[0], partial[1], first, second, out_grad)
        places = [((0, 0), (3, None), (4, None)), ((1, None), (2, 0), (2, 1))]
        grad_list = [out_grad, first]
    else:
        total = lax.psum(jnp.stack(partial), "mp")
        addends = (total, jnp.zeros_like(total[0]), *grad_list)
        places = [((0, j), (1, None), (2 + j, None)) for j in range(group)]
    outs = [((group, rows, D), BF16), ((group, rows, D), BF16), ((1, hidden_width), F32)]
    for _ in range(group):
        outs += [
            ((rows, D), F32),
            ((rows, D), BF16),
            ((rows, hidden_width), BF16),
            ((rows, hidden_width), BF16),
        ]
    args = (
        row(output_bias),
        row(gain_two),
        row(shift_two),
        up_weight,
        row(up_bias.astype(F32)),
        down_weight,
        *residual,
        *addends,
    )
    made = call(functools.partial(mlp_body, places), outs, args, us=3.0 * group, vmem=40)
    grad_two_part, mlp_part, grad_up_bias = made[:3]
    middle, normed_two, hidden, grad_pre = (made[3 + kind :: 4] for kind in range(4))

    if pair:
        grad_two_other = turn(grad_two_part, 1, "mp")
        back_places = [(0, 1), (1, 0)]
    else:
        grad_two_part = lax.psum(grad_two_part, "mp")
        grad_two_other = jnp.zeros_like(grad_two_part)
        back_places = [(j, j) for j in range(group)]

    if blocks:
        outs = [((hidden_width, D), BF16)] * 2
        args = (*normed_two, *grad_pre, *hidden, *grad_list)
        keep, send = call(functools.partial(mlp_grads_body, group), outs, args, us=3.0)
        mine, other = sum_blocks(keep, send)
        outs = [((D, hidden_width), F32), ((hidden_width, D), F32)]
        grad_up, grad_down = call(mlp_final_body, outs, (mine, other), us=2.0)

    backs = []
    for index in range(group):
        outs = [
            ((rows, D), F32),
            ((rows, D), BF16),
            ((3, rows, width), BF16),
            ((rows, D), BF16),
            ((8, D), F32),
            ((56, width), F32),
        ]
        args = (
            grad_two_part,
            grad_two_other,
            middle[index],
            grad_list[index],
            row(gain_two),
            output_weight,
            qkv_planes,
            query[index],
            weight[index],
            value[index],
            relative[index],
            context[index],
            kernel_part,
            to_frame[index],
            to_token[index],
        )
        scratch = [pltpu.VMEM((CELLS, SLOTS, width), F32)] * 2
        body = functools.partial(back_body, back_places[index])
        backs.append(call(body, outs, args, scratch, us=5.0))
    grad_middle, grad_projected, grad_qkv, grad_one_part, wide_sums, head_sums = zip(*backs)

    if blocks:
        outs = [((D, D), BF16)] * 2
        args = (*normed, *grad_qkv, *attended, *grad_projected)
        keep, send = call(functools.partial(attention_grads_body, group), outs, args, us=2.0)
        mine, other = sum_blocks(keep, send)
        outs = [((3, D, width), F32), ((width, D), F32)]
        grad_qkv_planes, grad_out = call(attention_final_body, outs, (mine, other), us=1.5)
    else:
        args = (*normed_two, *grad_pre, *hidden, *grad_list, *normed, *grad_qkv, *attended, *grad_projected)
        spot = lambda kind, image, part=None: (kind * group + image, part)
        products = [
            [(spot(0, j), spot(1, j)) for j in range(group)],
            [(spot(2, j), spot(3, j, 1 if pair and j else None)) for j in range(group)],
        ]
        products += [[(spot(4, j), spot(5, j, plane)) for j in range(group)] for plane in range(3)]
        products += [[(spot(6, j), spot(7, j)) for j in range(group)]]
        outs = [((D, hidden_width), BF16), ((hidden_width, D), BF16)]
        outs += [((D, width), BF16)] * 3 + [((width, D), BF16)]
        wholes = call(functools.partial(whole_body, products), outs, args, us=6.0, vmem=40)
        grad_up, grad_down, *planes, grad_out = (lax.psum(one, "dp").astype(F32) for one in wholes)
        grad_qkv_planes = jnp.stack(planes)

    if pair:
        mine = jnp.stack([grad_one_part[0], mlp_part[0]])
        other = turn(jnp.stack([grad_one_part[1], mlp_part[1]]), 1, "mp")
    else:
        sums = [jnp.stack(grad_one_part), mlp_part]
        mine = jnp.stack([lax.psum_scatter(one, "mp", scatter_dimension=0) for one in sums])
        other = jnp.zeros_like(mine)
    outs = [((rows, D), F32), ((rows, D), F32), ((16, D), F32)]
    args = (
        tokens,
        own(residual),
        own(grad_middle),
        mine,
        other,
        row(gain_one),
        position_kernel,
        own(to_frame),
        own(to_token),
        own(middle),
        row(down_bias),
    )
    scratch = [pltpu.VMEM((CELLS, SLOTS, D), F32)] * 3
    block_out, token_grad, own_sums = call(last_body, outs, args, scratch, us=5.0)

    head_total = functools.reduce(jnp.add, head_sums)
    wide_total = functools.reduce(jnp.add, wide_sums)
    if pair:
        mixed = jnp.concatenate([own_sums[:12], head_total[:50].reshape(-1, D)], axis=0)
        far = turn(mixed, 1, "mp")
        own_total = mixed[:12] + far[:12]
        halves = [mixed[12:].reshape(50, width), far[12:].reshape(50, width)]
        first = jnp.where(member == 0, halves[0], halves[1])
        second = jnp.where(member == 0, halves[1], halves[0])
        relative_total = jnp.concatenate([first, second], axis=1)
    else:
        own_total = lax.psum(own_sums[:12], "mp")
        relative_total = lax.all_gather(head_total[:50], "mp", axis=1, tiled=True)
    pieces = [own_total, wide_total[:4], relative_total]
    private = jnp.concatenate([grad_up_bias.reshape(-1), head_total[50:52].reshape(-1)])
    pieces.append(jnp.pad(private, (0, -private.shape[0] % D)).reshape(-1, D))
    total = sum_small(jnp.concatenate(pieces, axis=0))
    kernel_grad = total[16:65].reshape(EDGE, EDGE, D)
    tail = total[66:].reshape(-1)
    return (
        block_out,
        token_grad,
        total[:9].reshape(3, 3, D),
        total[9],
        total[10],
        total[11],
        jnp.transpose(grad_qkv_planes, (1, 0, 2)),
        tail[hidden_width : hidden_width + 2 * width].reshape(2, width),
        kernel_grad[2:5, 2:5, : 2 * HEAD],
        kernel_grad[1:6, 1:6, 2 * HEAD : 5 * HEAD],
        kernel_grad[:, :, 5 * HEAD :],
        total[65],
        grad_out,
        total[12],
        total[13],
        total[14],
        grad_up,
        tail[:hidden_width],
        grad_down,
        total[15],
    )


def solution(mesh):
    in_specs = (
        P(("dp", "mp"), None),
        P(("dp", "mp"), None),
        P("dp"),
        P("dp"),
        P(),
        P(),
        P(),
        P(),
        P(None, None, "mp"),
        P(None, "mp"),
        P(),
        P(),
        P(),
        P(),
        P("mp", None),
        P(),
        P(),
        P(),
        P(None, "mp"),
        P("mp"),
        P("mp", None),
        P(),
    )
    out_specs = (
        P(("dp", "mp"), None),
        P(("dp", "mp"), None),
        P(),
        P(),
        P(),
        P(),
        P(None, None, "mp"),
        P(None, "mp"),
        P(),
        P(),
        P(),
        P(),
        P("mp", None),
        P(),
        P(),
        P(),
        P(None, "mp"),
        P("mp"),
        P("mp", None),
        P(),
    )
    return jax.shard_map(
        per_device, mesh=mesh, in_specs=in_specs, out_specs=out_specs, check_vma=False
    )
```

```python
import functools
import math

import jax
import jax.numpy as jnp
from jax import lax
from jax.experimental import pallas as pl
from jax.experimental.pallas import tpu as pltpu
from jax.sharding import PartitionSpec as P

HEAD = 64
D = 512
EPSILON = 1e-06
SLOTS = 8
EDGE = 7
CELLS = EDGE * EDGE
ROWS = CELLS * SLOTS
SCALE = HEAD ** (-0.5)
SMALL = 80
BF16 = jnp.bfloat16
F32 = jnp.float32


def mm(left, right):
    return jnp.dot(left, right, preferred_element_type=F32)


def mm_t(left, right):
    return lax.dot_general(left, right, (((1,), (1,)), ((), ())), preferred_element_type=F32)


def t_mm(left, right):
    return lax.dot_general(left, right, (((0,), (0,)), ((), ())), preferred_element_type=F32)


def split_mm(onehot, values):
    high = values.astype(BF16)
    low = (values - high.astype(F32)).astype(BF16)
    return mm(onehot, high) + mm(onehot, low)


class Source:
    def __init__(self, ref, copy=None):
        self.held, self.copy, self.shape = ref, copy, ref.shape

    def ref(self):
        if self.copy is not None:
            self.copy.wait()
            self.copy = None
        return self.held

    def __getitem__(self, index):
        return self.ref()[index]


class Result:
    def __init__(self, ref, copy=None):
        self.held, self.copy, self.sent, self.shape = ref, copy, copy is None, ref.shape

    def __setitem__(self, index, value):
        self.held[index] = value

    def __getitem__(self, index):
        return self.held[index]

    def send(self):
        if not self.sent:
            self.copy.start()
            self.sent = True


class Far:
    def __init__(self, *what):
        self.what = what


def call(body, outs, args, scratch=(), us=3.0, smem=0, vmem=24, after=()):
    far_in = [isinstance(one, Far) for one in args[smem:]]
    far_out = [isinstance(one, Far) for one in outs]
    arrays = [one.what[0] if isinstance(one, Far) else one for one in args[smem:]]
    outs = [one.what if isinstance(one, Far) else one for one in outs]

    def kernel(*refs):
        refs = list(refs)

        def take(count):
            taken = refs[:count]
            del refs[:count]
            return taken

        scalars, given = take(smem), take(len(arrays))
        take(len(after))
        places = take(len(outs))
        near_in, near_out = take(sum(far_in)), take(sum(far_out))
        in_sems = take(1)[0] if any(far_in) else None
        out_sems = take(1)[0] if any(far_out) else None
        ins, made = [], []
        for ref, far in zip(given, far_in):
            if far:
                index = sum(one.copy is not None for one in ins)
                copy = pltpu.make_async_copy(ref, near_in[index], in_sems.at[index])
                copy.start()
                ins.append(Source(near_in[index], copy))
            else:
                ins.append(Source(ref))
        for ref, far in zip(places, far_out):
            if far:
                index = sum(one.copy is not None for one in made)
                copy = pltpu.make_async_copy(near_out[index], ref, out_sems.at[index])
                made.append(Result(near_out[index], copy))
            else:
                made.append(Result(ref))
        body(scalars, ins, made, refs)
        for one in made:
            one.send()
        for one in ins:
            one.ref()
        for one in made:
            if one.copy is not None:
                one.copy.wait()

    shapes = [pltpu.VMEM(one.shape, one.dtype) for one, far in zip(arrays, far_in) if far]
    shapes += [pltpu.VMEM(*one) for one, far in zip(outs, far_out) if far]
    if any(far_in):
        shapes.append(pltpu.SemaphoreType.DMA((sum(far_in),)))
    if any(far_out):
        shapes.append(pltpu.SemaphoreType.DMA((sum(far_out),)))
    near, far = pl.BlockSpec(memory_space=pltpu.VMEM), pl.BlockSpec(memory_space=pltpu.HBM)
    operands = [
        pltpu.with_memory_space_constraint(one, pltpu.HBM) if away else one
        for one, away in zip(arrays, far_in)
    ]
    return pl.pallas_call(
        kernel,
        out_shape=[
            pltpu.HBM(*one) if away else jax.ShapeDtypeStruct(*one)
            for one, away in zip(outs, far_out)
        ],
        in_specs=[pl.BlockSpec(memory_space=pltpu.SMEM)] * smem
        + [far if away else near for away in far_in]
        + [pl.BlockSpec(memory_space=pl.ANY)] * len(after),
        out_specs=[far if away else near for away in far_out],
        scratch_shapes=shapes + list(scratch),
        compiler_params=pltpu.CompilerParams(vmem_limit_bytes=vmem << 20),
        cost_estimate=pl.CostEstimate(
            flops=int(us * 1.0e8), bytes_accessed=1 << 12, transcendentals=0
        ),
    )(*args[:smem], *operands, *after)


def over_lanes(width, body):
    if width % 128 == 0:

        @pl.loop(0, width // 128)
        def _(step):
            body(pl.ds(pl.multiple_of(step * 128, 128), 128))

    else:
        body(slice(0, width))


def frame_conv(source, tap, target, edge, lanes):
    half = (edge - 1) // 2
    for i in range(EDGE):
        total = [None] * EDGE
        for a in range(edge):
            row = i + a - half
            if not 0 <= row < EDGE:
                continue
            cells = [source[row * EDGE + j, :, lanes] for j in range(EDGE)]
            for b in range(edge):
                weight = tap(a, b)
                for j in range(EDGE):
                    column = j + b - half
                    if 0 <= column < EDGE:
                        term = cells[column] * weight
                        total[j] = term if total[j] is None else total[j] + term
        for j in range(EDGE):
            target[i * EDGE + j, :, lanes] = total[j]


def frame_taps(grad, source, target, edge, lanes):
    half = (edge - 1) // 2
    for a in range(edge):
        total = [None] * edge
        for i in range(EDGE):
            row = i + a - half
            if not 0 <= row < EDGE:
                continue
            cells = [source[row * EDGE + j, :, lanes] for j in range(EDGE)]
            for j in range(EDGE):
                own = grad[i * EDGE + j, :, lanes]
                for b in range(edge):
                    column = j + b - half
                    if 0 <= column < EDGE:
                        term = own * cells[column]
                        total[b] = term if total[b] is None else total[b] + term
        for b in range(edge):
            row = a * edge + b
            target[row : row + 1, lanes] = jnp.sum(total[b], axis=0, keepdims=True)


def crop_frames(kinds, base, rows):
    sub = lax.broadcasted_iota(jnp.int32, (SLOTS, rows), 0)
    lane = lax.broadcasted_iota(jnp.int32, (SLOTS, rows), 1)
    place = lax.broadcasted_iota(jnp.int32, (8, ROWS), 1)
    slot = place & (SLOTS - 1)
    cell = place >> 3
    down = (cell * 37) >> 8
    across = cell - down * EDGE
    begin = jnp.zeros((SLOTS, rows), jnp.int32)
    whole = jnp.zeros((SLOTS, rows), jnp.int32)
    begin_row = jnp.zeros((8, ROWS), jnp.int32)
    whole_row = jnp.zeros((8, ROWS), jnp.int32)
    start = jnp.int32(0)
    for s in range(SLOTS):
        large = (kinds[base + s] == 0).astype(jnp.int32)
        begin = jnp.where(sub == s, start, begin)
        whole = jnp.where(sub == s, large, whole)
        begin_row = jnp.where(slot == s, start, begin_row)
        whole_row = jnp.where(slot == s, large, whole_row)
        start = start + 9 + 40 * large
    tiles = []
    for i in range(EDGE):
        for j in range(EDGE):
            small = begin + (i * 3 + j) if i < 3 and j < 3 else jnp.full_like(begin, -1)
            token = jnp.where(whole == 1, begin + (i * EDGE + j), small)
            tiles.append(jnp.where(token == lane, 1.0, 0.0))
    to_frame = jnp.concatenate(tiles, axis=0).astype(BF16)
    corner = jnp.where((down < 3) & (across < 3), begin_row + down * 3 + across, -1)
    token_row = jnp.where(whole_row == 1, begin_row + cell, corner)
    height = lax.broadcasted_iota(jnp.int32, (rows, ROWS), 0)
    to_token = jnp.where(height == token_row[0:1], 1.0, 0.0).astype(BF16)
    return to_frame, to_token


def norm_parts(values):
    average = jnp.mean(values, axis=-1, keepdims=True)
    centred = values - average
    variance = jnp.mean(centred * centred, axis=-1, keepdims=True)
    inverse = lax.rsqrt(variance + EPSILON)
    return centred * inverse, inverse


def norm_back(grad, unit, inverse, gain):
    scaled = grad * gain
    first = jnp.mean(scaled, axis=-1, keepdims=True)
    second = jnp.mean(scaled * unit, axis=-1, keepdims=True)
    return (scaled - first - unit * second) * inverse


def column_sum(values):
    return jnp.sum(values, axis=0, keepdims=True)


def same_head(width):
    rows = lax.broadcasted_iota(jnp.int32, (width, width), 0) // HEAD
    columns = lax.broadcasted_iota(jnp.int32, (width, width), 1) // HEAD
    return rows == columns


def tap_table(member, three, five, seven, table):
    table[...] = jnp.zeros(table.shape, F32)

    @pl.when(member == 0)
    def _():
        table[2:5, 2:5, 0:128] = three[...]
        for row in range(5):
            table[1 + row, 1:6, 128:256] = five[row, :, 0:128]

    @pl.when(member == 1)
    def _():
        for row in range(5):
            table[1 + row, 1:6, 0:64] = five[row, :, 128:192]
        lane = lax.broadcasted_iota(jnp.int32, (EDGE, 128), 1)
        for row in range(EDGE):
            near = pltpu.roll(seven[row, :, 0:128], 64, 1)
            wide = jnp.concatenate([seven[row, :, 128:192], jnp.zeros((EDGE, 64), F32)], axis=1)
            far = pltpu.roll(wide, 64, 1)
            table[row, :, 0:128] = jnp.where(lane < 64, table[row, :, 0:128], near)
            table[row, :, 128:256] = jnp.where(lane < 64, near, far)


def front_body(image, table, scalars, ins, outs, scratch):
    (kinds,) = scalars
    (
        tokens,
        position_kernel,
        position_bias,
        gain,
        shift,
        qkv_weight,
        pair_bias,
        relative_bias,
        output_weight,
    ) = ins[:9]
    (
        residual_out,
        normed_out,
        query_out,
        weight_out,
        value_out,
        relative_out,
        context_out,
        attended_out,
        partial_out,
        to_frame_out,
        to_token_out,
    ) = outs[:11]
    width = output_weight.shape[0]
    member = lax.axis_index("mp")
    if table:
        three, five, seven = ins[9:12]
        for one in ins[9:12]:
            one.ref()
        relative_kernel = outs[11]
        tap_table(member, three, five, seven, relative_kernel.held)
        relative_kernel.send()
        relative_taps = relative_kernel.held
    else:
        relative_taps = None
    if relative_bias.shape[1] == width:
        bias_row = relative_bias[...]
    else:
        bias_row = relative_bias[:, pl.ds(pl.multiple_of(member * width, 128), width)]
    grid_in, grid_out = scratch
    rows = tokens.shape[0]
    to_frame, to_token = crop_frames(kinds, image() * SLOTS, rows)
    to_frame_out[...] = to_frame
    to_frame_out.send()
    to_token_out[...] = to_token
    to_token_out.send()
    grid_in[...] = mm(to_frame, tokens[...]).reshape(CELLS, SLOTS, D)
    position_taps = position_kernel.ref()

    def position(lanes):
        frame_conv(grid_in, lambda a, b: position_taps[a, b : b + 1, lanes], grid_out, 3, lanes)

    over_lanes(D, position)
    residual = tokens[...].astype(F32) + split_mm(to_token, grid_out[...].reshape(ROWS, D))
    residual = residual + position_bias[...]
    residual_out[...] = residual
    residual_out.send()
    unit, _ = norm_parts(residual)
    normed = (unit * gain[...] + shift[...]).astype(BF16)
    normed_out[...] = normed
    normed_out.send()
    framed = mm(to_frame, normed).astype(BF16)
    valid = mm(to_frame, jnp.ones((rows, width), BF16))
    pair = pair_bias[...].astype(F32)
    query = mm(framed, qkv_weight[0]) + valid * pair[0:1]
    query_out[...] = query
    query_out.send()
    keys = mm(framed, qkv_weight[1])
    value = mm(framed, qkv_weight[2]) + valid * pair[1:2]
    keys = jnp.where(valid > 0.5, keys, -1e30)
    weight = jnp.exp(keys - jnp.max(keys, axis=0, keepdims=True))
    weight = weight / column_sum(weight)
    weight_out[...] = weight
    weight_out.send()
    value_out[...] = value.reshape(CELLS, SLOTS, width)
    value_out.send()
    context = jnp.where(same_head(width), t_mm(weight.astype(BF16), value.astype(BF16)), 0.0)
    context_out[...] = context
    context_out.send()
    if not table:
        relative_taps = ins[9].ref()

    def relative(lanes):
        frame_conv(
            value_out,
            lambda a, b: relative_taps[a, b : b + 1, lanes],
            relative_out,
            EDGE,
            lanes,
        )

    over_lanes(width, relative)
    position_term = relative_out[...].reshape(ROWS, width) + bias_row
    relative_out[...] = position_term.reshape(CELLS, SLOTS, width)
    relative_out.send()
    attended = SCALE * mm(query.astype(BF16), context.astype(BF16)) + query * position_term
    attended = mm(to_token, attended.astype(BF16)).astype(BF16)
    attended_out[...] = attended
    attended_out.send()
    partial = mm(attended, output_weight[...]).astype(BF16)
    partial_out[...] = partial


def pair_body(scalars, ins, outs, scratch):
    for index, one in enumerate(ins):
        outs[0][index] = one[...]


def picked(source, part):
    return source[...] if part is None else source[part]


def mlp_body(parts, scalars, ins, outs, scratch):
    (
        residual,
        first,
        second,
        cotangent,
        output_bias,
        gain,
        shift,
        up_weight,
        up_bias,
        down_weight,
    ) = ins
    middle_out, normed_out, hidden_out, grad_pre_out, grad_normed_out, mlp_out, grad_bias_out = outs
    hidden_width = up_weight.shape[1]
    projected = picked(first, parts[0]).astype(F32) + picked(second, parts[1]).astype(F32)
    middle = residual[...] + projected + output_bias[...]
    middle_out[...] = middle
    middle_out.send()
    unit, _ = norm_parts(middle)
    normed = (unit * gain[...] + shift[...]).astype(BF16)
    normed_out[...] = normed
    out_grad = picked(cotangent, parts[2])
    step = min(256, hidden_width)
    for begin in range(0, hidden_width, step):
        part = slice(begin, begin + step)
        pre = mm(normed, up_weight[:, part]) + up_bias[:, part]
        below = 0.5 * (1.0 + lax.erf(pre * (2.0**-0.5)))
        hidden_out[:, part] = (pre * below).astype(BF16)
        slope = below + pre * jnp.exp(-0.5 * pre * pre) * ((2.0 * math.pi) ** -0.5)
        grad = (mm_t(out_grad, down_weight[part, :]) * slope).astype(BF16)
        grad_pre_out[:, part] = grad
        grad_bias_out[:, part] = column_sum(grad.astype(F32))
    grad_bias_out.send()
    mlp_out[...] = mm(hidden_out[...], down_weight[...]).astype(BF16)
    mlp_out.send()
    grad_normed_out[...] = mm_t(grad_pre_out[...], up_weight[...]).astype(BF16)


def back_body(parts, scalars, ins, outs, scratch):
    (
        mine,
        other,
        middle,
        out_grad,
        gain,
        output_weight,
        qkv_weight,
        query,
        weight,
        value,
        relative,
        context,
        relative_kernel,
        to_frame,
        to_token,
    ) = ins[:15]
    grad_middle_out, projected_out, grad_qkv_out, grad_normed_out, wide_sums, head_sums = outs
    grid_grad, grid_back = scratch
    width = relative_kernel.shape[2]
    unit, inverse = norm_parts(middle[...])
    grad = picked(mine, parts[0]).astype(F32) + picked(other, parts[1]).astype(F32)
    cotangent = picked(out_grad, parts[2]).astype(F32)
    grad_middle = cotangent + norm_back(grad, unit, inverse, gain[...])
    grad_middle_out[...] = grad_middle
    grad_middle_out.send()
    projected = grad_middle.astype(BF16)
    projected_out[...] = projected
    wide_sums[0:1] = column_sum(projected.astype(F32))
    wide_sums[1:2] = column_sum(grad * unit)
    wide_sums[2:3] = column_sum(grad)
    wide_sums[3:4] = column_sum(cotangent)
    wide_sums[4:8] = jnp.zeros((4, D), F32)
    wide_sums.send()
    framed = mm(to_frame[...], projected).astype(BF16)
    attended = mm_t(framed, output_weight[...])
    attended_low = attended.astype(BF16)
    query_all = query[...]
    context_low = context[...].astype(BF16)
    grad_relative = attended * query_all
    grid_grad[...] = grad_relative.reshape(CELLS, SLOTS, width)
    relative_all = relative[...].reshape(ROWS, width)
    grad_query = SCALE * mm_t(attended_low, context_low) + attended * relative_all
    grad_context = SCALE * t_mm(query_all.astype(BF16), attended_low)
    grad_context = jnp.where(same_head(width), grad_context, 0.0)
    context_sum = lax.dot_general(
        jnp.ones((8, width), F32),
        grad_context * context[...],
        (((1,), (1,)), ((), ())),
        preferred_element_type=F32,
        precision=lax.Precision.HIGHEST,
    )[0:1]
    grad_context_low = grad_context.astype(BF16)
    taps, grid_value = relative_kernel.ref(), value.ref()

    def convolve(lanes):
        frame_conv(
            grid_grad,
            lambda a, b: taps[EDGE - 1 - a, EDGE - 1 - b : EDGE - b, lanes],
            grid_back,
            EDGE,
            lanes,
        )
        frame_taps(grid_grad, grid_value, head_sums, EDGE, lanes)

    over_lanes(width, convolve)
    head_sums[49:50] = column_sum(grad_relative)
    weight_all = weight[...]
    value_low = value[...].reshape(ROWS, width).astype(BF16)
    grad_value = grid_back[...].reshape(ROWS, width) + mm(weight_all.astype(BF16), grad_context_low)
    grad_key = weight_all * (mm_t(value_low, grad_context_low) - context_sum)
    parts = []
    for grad_part in (grad_query, grad_key, grad_value):
        parts.append(mm(to_token[...], grad_part.astype(BF16)))
    head_sums[50:51] = column_sum(parts[0])
    head_sums[51:52] = column_sum(parts[2])
    head_sums[52:56] = jnp.zeros((4, width), F32)
    head_sums.send()
    grad_normed = None
    for index in range(3):
        low = parts[index].astype(BF16)
        grad_qkv_out[index] = low
        term = mm_t(low, qkv_weight[index])
        grad_normed = term if grad_normed is None else grad_normed + term
    if len(ins) > 15:
        grad_normed_out[0] = grad_normed.astype(BF16)
        grad_normed_out[1] = ins[15][...]
    else:
        grad_normed_out[...] = grad_normed.astype(BF16)


def last_body(scalars, ins, outs, scratch):
    (
        tokens,
        residual,
        grad_middle,
        mine,
        mlp_mine,
        other,
        gain,
        position_kernel,
        to_frame,
        to_token,
        middle,
        down_bias,
    ) = ins[:12]
    block_out, token_grad, sums_out = outs
    grid_grad, grid_in, grid_back, sums = scratch
    block_out[...] = (
        middle[...] + (mlp_mine[...].astype(F32) + other[1].astype(F32)) + down_bias[...]
    )
    block_out.send()
    unit, inverse = norm_parts(residual[...])
    grad = mine[...].astype(F32) + other[0].astype(F32)
    grad_residual = grad_middle[...] + norm_back(grad, unit, inverse, gain[...])
    grid_grad[...] = split_mm(to_frame[...], grad_residual).reshape(CELLS, SLOTS, D)
    grid_in[...] = mm(to_frame[...], tokens[...]).reshape(CELLS, SLOTS, D)
    taps = position_kernel.ref()

    def convolve(lanes):
        frame_conv(
            grid_grad, lambda a, b: taps[2 - a, 2 - b : 3 - b, lanes], grid_back, 3, lanes
        )
        frame_taps(grid_grad, grid_in, sums, 3, lanes)

    over_lanes(D, convolve)
    token_grad[...] = grad_residual + split_mm(to_token[...], grid_back[...].reshape(ROWS, D))
    token_grad.send()
    sums[9:10] = column_sum(grad_residual)
    sums[10:11] = column_sum(grad * unit)
    sums[11:12] = column_sum(grad)
    if len(ins) > 12:
        first, second = ins[12:]
        width = first.shape[1]
        sums[12:62, 0:width] = first[0:50] + second[0:50]
        sums[12:62, width:] = jnp.zeros((50, D - width), F32)
        sums[62:64] = jnp.zeros((2, D), F32)
    else:
        sums[12:16] = jnp.zeros((4, D), F32)
    sums_out[...] = sums[...].astype(sums_out.held.dtype)


def turn(values, distance, axis="dp"):
    size = lax.axis_size(axis)
    return lax.ppermute(values, axis, [(i, i ^ distance) for i in range(size)])


def step_bits():
    bits = list(range(1, lax.axis_size("dp").bit_length() - 1))
    return bits, bits[1:] + bits[:1]


def step_turn(values, step):
    orders = step_bits()
    size = lax.axis_size("dp")
    return lax.ppermute(values, "dp", [(i, i ^ (1 << orders[i & 1][step])) for i in range(size)])


def step_side(step):
    first, second = step_bits()
    me = lax.axis_index("dp")
    return (me >> jnp.where(me & 1 == 0, first[step], second[step])) & 1


def rows_of(side, count):
    return pl.ds(pl.multiple_of(side * count, 16), count)


def mlp_grads(ins, images, tiles):
    normed, grad_pre = ins[:images], ins[images : 2 * images]
    hidden, out_grad = ins[2 * images : 3 * images], ins[3 * images : 4 * images]

    def cotangent(image):
        one = out_grad[image]
        return one[...] if len(one.shape) == 2 else one[1]

    def part(which, tile):
        columns = slice(tile * D, (tile + 1) * D)
        total = None
        for image in range(images):
            if which == 0:
                term = t_mm(normed[image][...], grad_pre[image][:, columns])
            else:
                term = t_mm(hidden[image][:, columns], cotangent(image))
            total = term if total is None else total + term
        return total

    return part


def mlp_grads_body(images, scalars, ins, outs, scratch):
    keep, send = outs
    tiles = keep.shape[0] // D
    part = mlp_grads(ins, images, tiles)
    for one in ins:
        one.ref()
    core = lax.axis_index("dp") & 1
    for side in range(2):

        @pl.when(core == side)
        def _():
            for tile in range(tiles):
                rows = slice(tile * D, (tile + 1) * D)
                keep[rows, :] = part(side, tile).astype(BF16)
                send[rows, :] = part(1 - side, tile).astype(BF16)


def attention_grads_body(images, scalars, ins, outs, scratch):
    keep, send = outs
    normed, grad_qkv = ins[:images], ins[images : 2 * images]
    attended, projected = ins[2 * images : 3 * images], ins[3 * images :]
    width = D // 2
    for one in ins:
        one.ref()

    def total(term):
        out = None
        for image in range(images):
            out = term(image) if out is None else out + term(image)
        return out.astype(BF16)

    def write(which, target):
        if which == 0:
            for index in range(2):
                target[:, index * width : (index + 1) * width] = total(
                    lambda image: t_mm(normed[image][...], grad_qkv[image][index])
                )
        else:
            target[0:width, :] = total(
                lambda image: t_mm(attended[image][...], projected[image][...])
            )
            for index in range(2):
                columns = slice(index * width, (index + 1) * width)
                target[width:, columns] = total(
                    lambda image: t_mm(normed[image][:, columns], grad_qkv[image][2])
                )

    core = lax.axis_index("dp") & 1
    for side in range(2):

        @pl.when(core == side)
        def _():
            write(side, keep)
            write(1 - side, send)


def halve_body(step, scalars, ins, outs, scratch):
    here, came = ins
    here.ref()
    came.ref()
    if len(outs) == 1:
        outs[0][...] = (here[...].astype(F32) + came[...].astype(F32)).astype(BF16)
        return
    stay, go = outs
    count = stay.shape[0]
    side = step_side(step)
    for target, place in ((go, 1 - side), (stay, side)):
        rows = rows_of(place, count)
        target[...] = (here[rows, :].astype(F32) + came[rows, :].astype(F32)).astype(BF16)
        target.send()


def join_body(step, extra, scalars, ins, outs, scratch):
    here, came = ins
    side = step_side(step)
    count = here.shape[0] - extra
    outs[0].held[rows_of(side, count), :] = here[0:count, :]
    outs[0].held[rows_of(1 - side, count), :] = came[0:count, :]
    if extra:
        total = here[count:, :].astype(F32) + came[count:, :].astype(F32)
        outs[0][2 * count :, :] = total.astype(BF16)


def pack_body(scalars, ins, outs, scratch):
    here, came, mine, far, wide_one, wide_two, bias_one, bias_two, head_one, head_two = ins
    (rows,) = scratch
    count = here.shape[0]
    outs[0][0:count, :] = (here[...].astype(F32) + came[...].astype(F32)).astype(BF16)
    own, others = mine[...].astype(F32), far[...].astype(F32)
    width = D // 2
    rows[0:12] = own[0:12] + others[0:12]
    rows[12:16] = wide_one[0:4] + wide_two[0:4]
    member = lax.axis_index("mp")
    low = jnp.where(member == 0, own[:, 0:width], others[:, 0:width])
    high = jnp.where(member == 0, others[:, 0:width], own[:, 0:width])
    rows[16:66, 0:width] = low[12:62]
    rows[16:66, width:] = high[12:62]
    bias = bias_one[...] + bias_two[...]
    rows[66:67] = bias[:, 0:D]
    rows[67:68] = bias[:, D:]
    rows[68:69, 0:width] = head_one[50:51] + head_two[50:51]
    rows[68:69, width:] = head_one[51:52] + head_two[51:52]
    rows[69:SMALL] = jnp.zeros((SMALL - 69, D), F32)
    outs[0][count:, :] = rows[...].astype(BF16)


def mlp_final_body(scalars, ins, outs, scratch):
    mine, other = ins
    grad_up, grad_down = outs
    mine.ref()
    other.ref()
    core = lax.axis_index("dp") & 1
    for side in range(2):

        @pl.when(core == side)
        def _():
            up, down = (mine, other) if side == 0 else (other, mine)
            for tile in range(down.shape[0] // D):
                rows = slice(tile * D, (tile + 1) * D)
                grad_up[:, rows] = up[rows, :].astype(F32)
            grad_down[...] = down[...].astype(F32)


def attention_final_body(scalars, ins, outs, scratch):
    mine, other = ins
    grad_qkv, grad_out, position, up_bias, pair_bias, three, five, seven = outs[:8]
    vectors = outs[8:]
    (small,) = scratch
    width = D // 2
    core = lax.axis_index("dp") & 1
    small[...] = mine[D:, :].astype(F32) + other[D:, :].astype(F32)
    for row in range(3):
        position[row] = small[3 * row : 3 * row + 3]
    position.send()
    for place, vector in zip((9, 10, 11, 65, 12, 13, 14, 15), vectors):
        vector[...] = small[place : place + 1]
        vector.send()
    up_bias[:, 0:D] = small[66:67]
    up_bias[:, D:] = small[67:68]
    up_bias.send()
    pair_bias[0:1] = small[68:69, 0:width]
    pair_bias[1:2] = small[68:69, width:]
    pair_bias.send()
    for row in range(3):
        begin = 16 + EDGE * (row + 2) + 2
        three[row] = small[begin : begin + 3, 0:128]
    three.send()
    for row in range(5):
        begin = 16 + EDGE * (row + 1) + 1
        five[row] = small[begin : begin + 5, 128:320]
    five.send()
    for row in range(EDGE):
        begin = 16 + EDGE * row
        seven[row] = pltpu.roll(small[begin : begin + EDGE, 256:512], 192, 1)[:, 0:192]
    seven.send()
    for side in range(2):

        @pl.when(core == side)
        def _():
            first, second = (mine, other) if side == 0 else (other, mine)
            for index in range(2):
                columns = slice(index * width, (index + 1) * width)
                grad_qkv[index] = first[0:D, columns].astype(F32)
                grad_qkv[2, columns, :] = second[width:D, columns].astype(F32)
            grad_out[...] = second[0:width, :].astype(F32)


def halve(keep, came, step, after=()):
    outs = [((keep.shape[0] // 2, D), BF16)] * 2
    body = functools.partial(halve_body, step)
    keep, send = call(body, outs, (keep, came), us=0.3, after=after)
    return keep, step_turn(send, step)


def join(keep, came, step, extra=0, after=()):
    outs = [(((keep.shape[0] - extra) * 2 + extra, D), BF16)]
    body = functools.partial(join_body, step, extra)
    return call(body, outs, (keep, came), us=0.3, after=after)[0]


def sum_small(values):
    size = lax.axis_size("dp")
    if size & (size - 1):
        return lax.psum(values, "dp")
    for bit in range(size.bit_length() - 1):
        values = values + turn(values, 1 << bit)
    return values


def whole_body(products, scalars, ins, outs, scratch):
    for target, pairs in zip(outs, products):
        total = None
        for left, right in pairs:
            one, two = (ins[i][...] if part is None else ins[i][part] for i, part in (left, right))
            term = t_mm(one, two)
            total = term if total is None else total + term
        target[...] = total.astype(BF16)


def per_device(
    tokens,
    out_grad,
    crop_image,
    crop_res,
    position_kernel,
    position_bias,
    gain_one,
    shift_one,
    qkv_weight,
    query_value_bias,
    relative_three,
    relative_five,
    relative_seven,
    relative_bias,
    output_weight,
    output_bias,
    gain_two,
    shift_two,
    up_weight,
    up_bias,
    down_weight,
    down_bias,
):
    group = lax.axis_size("mp")
    member = lax.axis_index("mp")
    rows = tokens.shape[0]
    width = qkv_weight.shape[2]
    hidden_width = up_weight.shape[1]
    pair = group == 2
    size = lax.axis_size("dp")
    blocks = (
        pair
        and size >= 4
        and size & (size - 1) == 0
        and 2 * width == D
        and hidden_width == 2 * D
        and D % (size * 8) == 0
    )

    def row(vector):
        return vector.reshape(1, -1)

    if not blocks:
        full_kernel = jnp.concatenate(
            [
                jnp.pad(relative_three, ((2, 2), (2, 2), (0, 0))),
                jnp.pad(relative_five, ((1, 1), (1, 1), (0, 0))),
                relative_seven,
            ],
            axis=2,
        )
        kernel_part = lax.dynamic_slice_in_dim(full_kernel, member * width, width, 2)
        bias_part = row(lax.dynamic_slice_in_dim(relative_bias, member * width, width, 0))
    else:
        kernel_part, bias_part = None, row(relative_bias)
    qkv_planes = jnp.transpose(qkv_weight, (1, 0, 2))

    if pair:
        token_list = [tokens, turn(tokens, 1, "mp")]
        images = [lambda: lax.axis_index("mp"), lambda: 1 - lax.axis_index("mp")]
    else:
        token_list = list(lax.all_gather(tokens, "mp", axis=0))
        grad_list = list(lax.all_gather(out_grad, "mp", axis=0))
        images = [functools.partial(int, j) for j in range(group)]

    def own(parts):
        if pair:
            return parts[0]
        return lax.dynamic_index_in_dim(jnp.stack(parts), member, 0, keepdims=False)

    fronts = []
    for index, (image, one) in enumerate(zip(images, token_list)):
        table = blocks and index == 0
        outs = [
            Far((rows, D), F32),
            Far((rows, D), BF16),
            Far((ROWS, width), F32),
            Far((ROWS, width), F32),
            Far((CELLS, SLOTS, width), F32),
            Far((CELLS, SLOTS, width), F32),
            Far((width, width), F32),
            Far((rows, width), BF16),
            ((rows, D), BF16),
            Far((ROWS, rows), BF16),
            Far((rows, ROWS), BF16),
        ]
        args = [
            crop_res,
            Far(one) if index == 0 else one,
            Far(position_kernel),
            Far(row(position_bias)),
            Far(row(gain_one)),
            Far(row(shift_one)),
            Far(qkv_planes),
            Far(query_value_bias),
            Far(bias_part),
            Far(output_weight),
        ]
        if table:
            outs.append(Far((EDGE, EDGE, width), F32))
            args += [Far(relative_three), Far(relative_five), Far(relative_seven)]
        else:
            args.append(Far(kernel_part))
        scratch = [pltpu.VMEM((CELLS, SLOTS, D), F32)] * 2
        body = functools.partial(front_body, image, table)
        made = call(body, outs, args, scratch, us=50.0 if index == 0 else 5.0, smem=1)
        if table:
            kernel_part = made[11]
        fronts.append(made[:11])
    residual, normed, query, weight, value, relative, context, attended, partial, to_frame, to_token = zip(
        *fronts
    )

    if pair:
        args = (partial[0], out_grad)
        (both,) = call(pair_body, [((2, rows, D), BF16)], args, us=0.3, after=[token_list[1]])
        first, second = turn(both, 1, "mp"), turn(partial[1], 1, "mp")
        grad_list, grad_parts = [out_grad, first], [None, 1]
        addends = [(partial[0], second), (partial[1], first)]
        places = [(None, None), (None, 0)]
        order = (1, 0)
    else:
        total = lax.psum(jnp.stack(partial), "mp")
        grad_parts = [None] * group
        addends = [(one, jnp.zeros_like(one)) for one in total]
        places = [(None, None)] * group
        order = range(group)
    mlps = [None] * group
    for index in order:
        outs = [
            Far((rows, D), F32),
            ((rows, D), BF16),
            ((rows, hidden_width), BF16),
            ((rows, hidden_width), BF16),
            ((rows, D), BF16),
            Far((rows, D), BF16),
            Far((1, hidden_width), F32),
        ]
        args = (
            Far(residual[index]),
            *addends[index],
            grad_list[index],
            Far(row(output_bias)),
            Far(row(gain_two)),
            Far(row(shift_two)),
            up_weight,
            row(up_bias.astype(F32)),
            down_weight,
        )
        body = functools.partial(mlp_body, (*places[index], grad_parts[index]))
        after = [mlps[1][4]] if pair and index == 0 else []
        mlps[index] = call(body, outs, args, us=2.5, after=after)
    middle, normed_two, hidden, grad_pre, grad_two_part, mlp_part, grad_up_bias = zip(*mlps)

    if pair:
        back_addends = [
            (grad_two_part[0], turn(grad_two_part[1], 1, "mp")),
            (grad_two_part[1], turn(grad_two_part[0], 1, "mp")),
        ]
    else:
        total = lax.psum(jnp.stack(grad_two_part), "mp")
        back_addends = [(one, jnp.zeros_like(one)) for one in total]

    steps = len(step_bits()[0])
    if blocks:
        outs = [((hidden_width, D), BF16)] * 2
        args = (*normed_two, *grad_pre, *hidden, *grad_list)
        body = functools.partial(mlp_grads_body, group)
        mlp_keep, mlp_send = call(body, outs, args, us=2.0, after=[back_addends[0][1]])
        mlp_came = turn(mlp_send, 1)

    backs = []
    for index in range(group):
        carry = pair and index == 1
        outs = [
            Far((rows, D), F32),
            ((rows, D), BF16),
            ((3, rows, width), BF16),
            ((2, rows, D) if carry else (rows, D), BF16),
            Far((8, D), F32),
            Far((56, width), F32),
        ]
        args = [
            *back_addends[index],
            Far(middle[index]),
            grad_list[index],
            Far(row(gain_two)),
            Far(output_weight),
            Far(qkv_planes),
            Far(query[index]),
            Far(weight[index]),
            Far(value[index]),
            Far(relative[index]),
            Far(context[index]),
            Far(kernel_part),
            Far(to_frame[index]),
            Far(to_token[index]),
        ]
        if carry:
            args.append(Far(mlp_part[1]))
        scratch = [pltpu.VMEM((CELLS, SLOTS, width), F32)] * 2
        body = functools.partial(back_body, (None, None, grad_parts[index]))
        after = [mlp_keep] if blocks else []
        backs.append(call(body, outs, args, scratch, us=5.0, after=after))
        if blocks and index == 0:
            mlp_keep, mlp_came = halve(mlp_keep, mlp_came, 0, after=[backs[0][3]])
    grad_middle, grad_projected, grad_qkv, grad_one_part, wide_sums, head_sums = zip(*backs)

    if blocks:
        outs = [((D, D), BF16)] * 2
        args = (*map(Far, normed), *grad_qkv, *map(Far, attended), *grad_projected)
        body = functools.partial(attention_grads_body, group)
        keep, send = call(body, outs, args, us=2.0)
        came = turn(send, 1)
        for step in range(1, steps + 1):
            if step < steps:
                mlp_keep, mlp_came = halve(mlp_keep, mlp_came, step, after=[keep])
            else:
                outs = [(mlp_keep.shape, BF16)]
                body = functools.partial(halve_body, None)
                (mlp_keep,) = call(body, outs, (mlp_keep, mlp_came), us=0.3, after=[keep])
                mlp_came = step_turn(mlp_keep, steps - 1)
            keep, came = halve(keep, came, step - 1)
    if not blocks:
        args = (*normed_two, *grad_pre, *hidden, *grad_list)
        args += (*normed, *grad_qkv, *attended, *grad_projected)

        def spot(kind, image, part=None):
            return kind * group + image, part

        each = range(group)
        products = [
            [(spot(0, j), spot(1, j)) for j in each],
            [(spot(2, j), spot(3, j, grad_parts[j])) for j in each],
        ]
        products += [[(spot(4, j), spot(5, j, plane)) for j in each] for plane in range(3)]
        products += [[(spot(6, j), spot(7, j)) for j in each]]
        outs = [((D, hidden_width), BF16), ((hidden_width, D), BF16)]
        outs += [((D, width), BF16)] * 3 + [((width, D), BF16)]
        wholes = call(functools.partial(whole_body, products), outs, args, us=6.0, vmem=40)
        grad_up, grad_down, *planes, grad_out = (lax.psum(one, "dp").astype(F32) for one in wholes)
        grad_qkv_planes = jnp.stack(planes)

    if pair:
        mine, mlp_mine = grad_one_part[0], mlp_part[0]
        other = turn(grad_one_part[1], 1, "mp")
    else:
        sums = [jnp.stack(grad_one_part), jnp.stack(mlp_part)]
        mine, mlp_mine = (lax.psum_scatter(one, "mp", scatter_dimension=0) for one in sums)
        other = jnp.zeros((2, rows, D), BF16)
    outs = [Far((rows, D), F32), Far((rows, D), F32)]
    outs.append(((64, D), BF16) if blocks else ((16, D), F32))
    args = [
        Far(tokens),
        Far(own(residual)),
        Far(own(grad_middle)),
        mine,
        Far(mlp_mine),
        other,
        Far(row(gain_one)),
        Far(position_kernel),
        Far(own(to_frame)),
        Far(own(to_token)),
        Far(own(middle)),
        Far(row(down_bias)),
    ]
    if blocks:
        args += [Far(head_sums[0]), Far(head_sums[1])]
    scratch = [pltpu.VMEM((CELLS, SLOTS, D), F32)] * 3
    scratch.append(pltpu.VMEM((64 if blocks else 16, D), F32))
    block_out, token_grad, own_sums = call(last_body, outs, args, scratch, us=5.0)

    if blocks:
        args = (keep, came, own_sums, turn(own_sums, 1, "mp"))
        args += tuple(map(Far, (*wide_sums, *grad_up_bias, *head_sums)))
        outs = [((keep.shape[0] + SMALL, D), BF16)]
        (keep,) = call(pack_body, outs, args, [pltpu.VMEM((SMALL, D), F32)], us=1.0)
        for step in reversed(range(steps)):
            came = step_turn(keep, step)
            mlp_keep = join(mlp_keep, mlp_came, step, after=[keep])
            mlp_came = step_turn(mlp_keep, step - 1) if step else turn(mlp_keep, 1)
            keep = join(keep, came, step, SMALL)
        came = turn(keep, 1)
        outs = [Far((D, hidden_width), F32), Far((hidden_width, D), F32)]
        grad_up, grad_down = call(mlp_final_body, outs, (mlp_keep, mlp_came), us=2.0, after=[keep])
        shapes = [(3, D, width), (width, D), (3, 3, D), (1, hidden_width), (2, width)]
        shapes += [relative_three.shape, relative_five.shape, relative_seven.shape]
        outs = [Far(shape, F32) for shape in shapes + [(1, D)] * 8]
        scratch = [pltpu.VMEM((SMALL, D), F32)]
        made = call(attention_final_body, outs, (keep, came), scratch, us=2.0, after=[grad_up])
        grad_qkv_planes, grad_out, position, up_sum, pair_sum, three, five, seven = made[:8]
        vectors = [one.reshape(D) for one in made[8:]]
        return (
            block_out,
            token_grad,
            position,
            *vectors[0:3],
            jnp.transpose(grad_qkv_planes, (1, 0, 2)),
            pair_sum,
            three,
            five,
            seven,
            vectors[3],
            grad_out,
            *vectors[4:7],
            grad_up,
            up_sum.reshape(hidden_width),
            grad_down,
            vectors[7],
        )

    head_total = functools.reduce(jnp.add, head_sums)
    wide_total = functools.reduce(jnp.add, wide_sums)
    own_total = lax.psum(own_sums[:12], "mp")
    relative_total = lax.all_gather(head_total[:50], "mp", axis=1, tiled=True)
    bias_total = functools.reduce(jnp.add, grad_up_bias)
    pieces = [own_total, wide_total[:4], relative_total]
    private = jnp.concatenate([bias_total.reshape(-1), head_total[50:52].reshape(-1)])
    pieces.append(jnp.pad(private, (0, -private.shape[0] % D)).reshape(-1, D))
    total = sum_small(jnp.concatenate(pieces, axis=0))
    kernel_grad = total[16:65].reshape(EDGE, EDGE, D)
    tail = total[66:].reshape(-1)
    return (
        block_out,
        token_grad,
        total[:9].reshape(3, 3, D),
        total[9],
        total[10],
        total[11],
        jnp.transpose(grad_qkv_planes, (1, 0, 2)),
        tail[hidden_width : hidden_width + 2 * width].reshape(2, width),
        kernel_grad[2:5, 2:5, : 2 * HEAD],
        kernel_grad[1:6, 1:6, 2 * HEAD : 5 * HEAD],
        kernel_grad[:, :, 5 * HEAD :],
        total[65],
        grad_out,
        total[12],
        total[13],
        total[14],
        grad_up,
        tail[:hidden_width],
        grad_down,
        total[15],
    )


def solution(mesh):
    in_specs = (
        P(("dp", "mp"), None),
        P(("dp", "mp"), None),
        P("dp"),
        P("dp"),
        P(),
        P(),
        P(),
        P(),
        P(None, None, "mp"),
        P(None, "mp"),
        P(),
        P(),
        P(),
        P(),
        P("mp", None),
        P(),
        P(),
        P(),
        P(None, "mp"),
        P("mp"),
        P("mp", None),
        P(),
    )
    out_specs = (
        P(("dp", "mp"), None),
        P(("dp", "mp"), None),
        P(),
        P(),
        P(),
        P(),
        P(None, None, "mp"),
        P(None, "mp"),
        P(),
        P(),
        P(),
        P(),
        P("mp", None),
        P(),
        P(),
        P(),
        P(None, "mp"),
        P("mp"),
        P("mp", None),
        P(),
    )
    return jax.shard_map(
        per_device, mesh=mesh, in_specs=in_specs, out_specs=out_specs, check_vma=False
    )
```

```python
import functools
import math

import jax
import jax.numpy as jnp
from jax import lax
from jax.experimental import pallas as pl
from jax.experimental.pallas import tpu as pltpu
from jax.sharding import PartitionSpec as P

HEAD = 64
D = 512
EPSILON = 1e-06
SLOTS = 8
EDGE = 7
CELLS = EDGE * EDGE
ROWS = CELLS * SLOTS
SCALE = HEAD ** (-0.5)
SMALL = 80
WEIGH = 40.0
BF16 = jnp.bfloat16
F32 = jnp.float32


def mm(left, right):
    return jnp.dot(left, right, preferred_element_type=F32)


def mm_t(left, right):
    return lax.dot_general(left, right, (((1,), (1,)), ((), ())), preferred_element_type=F32)


def t_mm(left, right):
    return lax.dot_general(left, right, (((0,), (0,)), ((), ())), preferred_element_type=F32)


def split_mm(onehot, values):
    high = values.astype(BF16)
    low = (values - high.astype(F32)).astype(BF16)
    return mm(onehot, high) + mm(onehot, low)


class Source:
    def __init__(self, ref, copy=None):
        self.held, self.copy, self.shape = ref, copy, ref.shape

    def ref(self):
        if self.copy is not None:
            self.copy.wait()
            self.copy = None
        return self.held

    def __getitem__(self, index):
        return self.ref()[index]


class Result:
    def __init__(self, ref, copy=None):
        self.held, self.copy, self.sent, self.shape = ref, copy, copy is None, ref.shape

    def __setitem__(self, index, value):
        self.held[index] = value

    def __getitem__(self, index):
        return self.held[index]

    def send(self):
        if not self.sent:
            self.copy.start()
            self.sent = True


class Far:
    def __init__(self, *what):
        self.what = what


def call(body, outs, args, scratch=(), us=3.0, smem=0, vmem=24, after=()):
    far_in = [isinstance(one, Far) for one in args[smem:]]
    far_out = [isinstance(one, Far) for one in outs]
    arrays = [one.what[0] if isinstance(one, Far) else one for one in args[smem:]]
    outs = [one.what if isinstance(one, Far) else one for one in outs]

    def kernel(*refs):
        refs = list(refs)

        def take(count):
            taken = refs[:count]
            del refs[:count]
            return taken

        scalars, given = take(smem), take(len(arrays))
        take(len(after))
        places = take(len(outs))
        near_in, near_out = take(sum(far_in)), take(sum(far_out))
        in_sems = take(1)[0] if any(far_in) else None
        out_sems = take(1)[0] if any(far_out) else None
        ins, made = [], []
        for ref, far in zip(given, far_in):
            if far:
                index = sum(one.copy is not None for one in ins)
                copy = pltpu.make_async_copy(ref, near_in[index], in_sems.at[index])
                copy.start()
                ins.append(Source(near_in[index], copy))
            else:
                ins.append(Source(ref))
        for ref, far in zip(places, far_out):
            if far:
                index = sum(one.copy is not None for one in made)
                copy = pltpu.make_async_copy(near_out[index], ref, out_sems.at[index])
                made.append(Result(near_out[index], copy))
            else:
                made.append(Result(ref))
        body(scalars, ins, made, refs)
        for one in made:
            one.send()
        for one in ins:
            one.ref()
        for one in made:
            if one.copy is not None:
                one.copy.wait()

    shapes = [pltpu.VMEM(one.shape, one.dtype) for one, far in zip(arrays, far_in) if far]
    shapes += [pltpu.VMEM(*one) for one, far in zip(outs, far_out) if far]
    if any(far_in):
        shapes.append(pltpu.SemaphoreType.DMA((sum(far_in),)))
    if any(far_out):
        shapes.append(pltpu.SemaphoreType.DMA((sum(far_out),)))
    near, far = pl.BlockSpec(memory_space=pltpu.VMEM), pl.BlockSpec(memory_space=pltpu.HBM)
    operands = [
        pltpu.with_memory_space_constraint(one, pltpu.HBM) if away else one
        for one, away in zip(arrays, far_in)
    ]
    return pl.pallas_call(
        kernel,
        out_shape=[
            pltpu.HBM(*one) if away else jax.ShapeDtypeStruct(*one)
            for one, away in zip(outs, far_out)
        ],
        in_specs=[pl.BlockSpec(memory_space=pltpu.SMEM)] * smem
        + [far if away else near for away in far_in]
        + [pl.BlockSpec(memory_space=pl.ANY)] * len(after),
        out_specs=[far if away else near for away in far_out],
        scratch_shapes=shapes + list(scratch),
        compiler_params=pltpu.CompilerParams(vmem_limit_bytes=vmem << 20),
        cost_estimate=pl.CostEstimate(
            flops=int(us * 1.0e8), bytes_accessed=1 << 12, transcendentals=0
        ),
    )(*args[:smem], *operands, *after)


def over_lanes(width, body):
    if width % 128 == 0:

        @pl.loop(0, width // 128)
        def _(step):
            body(pl.ds(pl.multiple_of(step * 128, 128), 128))

    else:
        body(slice(0, width))


def frame_conv(source, tap, target, edge, lanes):
    half = (edge - 1) // 2
    for i in range(EDGE):
        total = [None] * EDGE
        for a in range(edge):
            row = i + a - half
            if not 0 <= row < EDGE:
                continue
            cells = [source[row * EDGE + j, :, lanes] for j in range(EDGE)]
            for b in range(edge):
                weight = tap(a, b)
                for j in range(EDGE):
                    column = j + b - half
                    if 0 <= column < EDGE:
                        term = cells[column] * weight
                        total[j] = term if total[j] is None else total[j] + term
        for j in range(EDGE):
            target[i * EDGE + j, :, lanes] = total[j]


def frame_taps(grad, source, target, edge, lanes):
    half = (edge - 1) // 2
    for a in range(edge):
        total = [None] * edge
        for i in range(EDGE):
            row = i + a - half
            if not 0 <= row < EDGE:
                continue
            cells = [source[row * EDGE + j, :, lanes] for j in range(EDGE)]
            for j in range(EDGE):
                own = grad[i * EDGE + j, :, lanes]
                for b in range(edge):
                    column = j + b - half
                    if 0 <= column < EDGE:
                        term = own * cells[column]
                        total[b] = term if total[b] is None else total[b] + term
        for b in range(edge):
            row = a * edge + b
            target[row : row + 1, lanes] = jnp.sum(total[b], axis=0, keepdims=True)


def crop_frames(kinds, base, rows):
    sub = lax.broadcasted_iota(jnp.int32, (SLOTS, rows), 0)
    lane = lax.broadcasted_iota(jnp.int32, (SLOTS, rows), 1)
    place = lax.broadcasted_iota(jnp.int32, (8, ROWS), 1)
    slot = place & (SLOTS - 1)
    cell = place >> 3
    down = (cell * 37) >> 8
    across = cell - down * EDGE
    begin = jnp.zeros((SLOTS, rows), jnp.int32)
    whole = jnp.zeros((SLOTS, rows), jnp.int32)
    begin_row = jnp.zeros((8, ROWS), jnp.int32)
    whole_row = jnp.zeros((8, ROWS), jnp.int32)
    start = jnp.int32(0)
    for s in range(SLOTS):
        large = (kinds[base + s] == 0).astype(jnp.int32)
        begin = jnp.where(sub == s, start, begin)
        whole = jnp.where(sub == s, large, whole)
        begin_row = jnp.where(slot == s, start, begin_row)
        whole_row = jnp.where(slot == s, large, whole_row)
        start = start + 9 + 40 * large
    tiles = []
    for i in range(EDGE):
        for j in range(EDGE):
            small = begin + (i * 3 + j) if i < 3 and j < 3 else jnp.full_like(begin, -1)
            token = jnp.where(whole == 1, begin + (i * EDGE + j), small)
            tiles.append(jnp.where(token == lane, 1.0, 0.0))
    to_frame = jnp.concatenate(tiles, axis=0).astype(BF16)
    corner = jnp.where((down < 3) & (across < 3), begin_row + down * 3 + across, -1)
    token_row = jnp.where(whole_row == 1, begin_row + cell, corner)
    height = lax.broadcasted_iota(jnp.int32, (rows, ROWS), 0)
    to_token = jnp.where(height == token_row[0:1], 1.0, 0.0).astype(BF16)
    return to_frame, to_token


def norm_parts(values):
    average = jnp.mean(values, axis=-1, keepdims=True)
    centred = values - average
    variance = jnp.mean(centred * centred, axis=-1, keepdims=True)
    inverse = lax.rsqrt(variance + EPSILON)
    return centred * inverse, inverse


def norm_back(grad, unit, inverse, gain):
    scaled = grad * gain
    first = jnp.mean(scaled, axis=-1, keepdims=True)
    second = jnp.mean(scaled * unit, axis=-1, keepdims=True)
    return (scaled - first - unit * second) * inverse


def column_sum(values):
    return jnp.sum(values, axis=0, keepdims=True)


def same_head(width):
    rows = lax.broadcasted_iota(jnp.int32, (width, width), 0) // HEAD
    columns = lax.broadcasted_iota(jnp.int32, (width, width), 1) // HEAD
    return rows == columns


def tap_table(member, three, five, seven, table):
    table[...] = jnp.zeros(table.shape, F32)

    @pl.when(member == 0)
    def _():
        table[2:5, 2:5, 0:128] = three[...]
        for row in range(5):
            table[1 + row, 1:6, 128:256] = five[row, :, 0:128]

    @pl.when(member == 1)
    def _():
        for row in range(5):
            table[1 + row, 1:6, 0:64] = five[row, :, 128:192]
        lane = lax.broadcasted_iota(jnp.int32, (EDGE, 128), 1)
        for row in range(EDGE):
            near = pltpu.roll(seven[row, :, 0:128], 64, 1)
            wide = jnp.concatenate([seven[row, :, 128:192], jnp.zeros((EDGE, 64), F32)], axis=1)
            far = pltpu.roll(wide, 64, 1)
            table[row, :, 0:128] = jnp.where(lane < 64, table[row, :, 0:128], near)
            table[row, :, 128:256] = jnp.where(lane < 64, near, far)


def front_body(image, table, early, scalars, ins, outs, scratch):
    (kinds,) = scalars
    tokens, position_kernel, position_bias, gain, shift, qkv_weight, pair_bias = ins[:7]
    relative_bias, output_weight = ins[-2:]
    (
        to_frame_out,
        to_token_out,
        residual_out,
        normed_out,
        query_out,
        value_out,
        weight_out,
        context_out,
        relative_out,
        attended_out,
        partial_out,
    ) = outs[:11]
    grid_in, grid_out = scratch
    rows = tokens.shape[0]
    width = output_weight.shape[0]
    member = lax.axis_index("mp")
    to_frame, to_token = crop_frames(kinds, image() * SLOTS, rows)
    to_frame_out[...] = to_frame
    to_frame_out.send()
    to_token_out[...] = to_token
    to_token_out.send()
    grid_in[...] = mm(to_frame, tokens[...]).reshape(CELLS, SLOTS, D)
    position_taps = position_kernel.ref()

    def position(lanes):
        frame_conv(grid_in, lambda a, b: position_taps[a, b : b + 1, lanes], grid_out, 3, lanes)

    over_lanes(D, position)
    residual = tokens[...].astype(F32) + split_mm(to_token, grid_out[...].reshape(ROWS, D))
    residual = residual + position_bias[...]
    residual_out[...] = residual
    if table:
        outs[13][...] = residual
        outs[13].send()
    unit, _ = norm_parts(residual)
    normed = (unit * gain[...] + shift[...]).astype(BF16)
    normed_out[...] = normed
    normed_out.send()
    pair = pair_bias[...].astype(F32)
    value = (mm(normed, qkv_weight[2]) + pair[1:2]).astype(BF16)
    value_out[...] = value
    value_out.send()
    grid_in[:, :, 0:width] = mm(to_frame, value).reshape(CELLS, SLOTS, width)
    query = mm(normed, qkv_weight[0]) + pair[0:1]
    query_out[...] = query
    query_out.send()
    keys = mm(normed, qkv_weight[1])
    weight = jnp.exp(keys - jnp.max(keys, axis=0, keepdims=True))
    weight = weight / column_sum(weight)
    weight_out[...] = weight
    weight_out.send()
    context = jnp.where(same_head(width), t_mm(weight.astype(BF16), value), 0.0).astype(BF16)
    context_out[...] = context
    context_out.send()
    if table:
        relative_kernel = outs[12]
        for one in ins[7:10]:
            one.ref()
        tap_table(member, *ins[7:10], relative_kernel.held)
        relative_kernel.send()
        relative_taps = relative_kernel.held
    else:
        relative_taps = ins[7].ref()

    def relative(lanes):
        frame_conv(
            grid_in, lambda a, b: relative_taps[a, b : b + 1, lanes], grid_out, EDGE, lanes
        )

    over_lanes(width, relative)
    if relative_bias.shape[1] == width:
        bias_row = relative_bias[...]
    else:
        bias_row = relative_bias[:, pl.ds(pl.multiple_of(member * width, 128), width)]
    framed = grid_out[:, :, 0:width].reshape(ROWS, width).astype(BF16)
    position_term = mm(to_token, framed) + bias_row
    relative_out[...] = position_term
    relative_out.send()
    attended = SCALE * mm(query.astype(BF16), context) + query * position_term
    attended = attended.astype(BF16)
    attended_out[...] = attended
    attended_out.send()
    if early:
        outs[11][:, 0:D] = normed
        outs[11][:, D:] = attended
    partial_out[...] = mm(attended, output_weight[...]).astype(BF16)


def mark(array, us):
    def body(scalars, ins, outs, scratch):
        outs[0][...] = jnp.zeros((8, 128), F32)

    return call(body, [((8, 128), F32)], (), us=us, after=[array])[0]


def pair_body(scalars, ins, outs, scratch):
    for index, one in enumerate(ins):
        outs[0][index] = one[...]


def picked(source, part):
    return source[...] if part is None else source[part]


def mlp_body(parts, split, scalars, ins, outs, scratch):
    (
        residual,
        first,
        second,
        cotangent,
        output_bias,
        gain,
        shift,
        up_weight,
        up_bias,
        down_weight,
    ) = ins
    middle_out, grad_normed_out, mlp_out, grad_bias_out = outs[:4]
    hidden_out, grad_pre_out = scratch if split else outs[4:6]
    hidden_width = up_weight.shape[1]
    projected = picked(first, parts[0]).astype(F32) + picked(second, parts[1]).astype(F32)
    middle = residual[...] + projected + output_bias[...]
    middle_out[...] = middle
    middle_out.send()
    unit, _ = norm_parts(middle)
    normed = (unit * gain[...] + shift[...]).astype(BF16)
    out_grad = picked(cotangent, parts[2])
    step = min(256, hidden_width)
    for begin in range(0, hidden_width, step):
        part = slice(begin, begin + step)
        pre = mm(normed, up_weight[:, part]) + up_bias[:, part]
        below = 0.5 * (1.0 + lax.erf(pre * (2.0**-0.5)))
        hidden_out[:, part] = (pre * below).astype(BF16)
        slope = below + pre * jnp.exp(-0.5 * pre * pre) * ((2.0 * math.pi) ** -0.5)
        grad = (mm_t(out_grad, down_weight[part, :]) * slope).astype(BF16)
        grad_pre_out[:, part] = grad
        grad_bias_out[:, part] = column_sum(grad.astype(F32))
    grad_bias_out.send()
    mlp_out[...] = mm(hidden_out[...], down_weight[...]).astype(BF16)
    mlp_out.send()
    grad_normed_out[...] = mm_t(grad_pre_out[...], up_weight[...]).astype(BF16)
    if not split:
        outs[6][...] = normed
        return
    keep, send = outs[4:6]
    core = lax.axis_index("dp") & 1
    for side in range(2):

        @pl.when(core == side)
        def _():
            up, down = (keep, send) if side == 0 else (send, keep)
            up[:, 0:hidden_width] = grad_pre_out[...]
            up[:, hidden_width:] = normed
            down[:, 0:hidden_width] = hidden_out[...]
            down[:, hidden_width:] = out_grad


def back_body(parts, split, scalars, ins, outs, scratch):
    (
        mine,
        other,
        out_grad,
        middle,
        gain,
        output_weight,
        query,
        to_frame,
        value,
        relative_kernel,
        context,
        relative,
        weight,
        to_token,
        qkv_weight,
    ) = ins[:15]
    grad_middle_out, grad_normed_out, wide_sums, head_sums = outs[:4]
    grid_grad, grid_value, grid_back = scratch
    width = relative_kernel.shape[2]
    unit, inverse = norm_parts(middle[...])
    grad = picked(mine, parts[0]).astype(F32) + picked(other, parts[1]).astype(F32)
    cotangent = picked(out_grad, parts[2]).astype(F32)
    grad_middle = cotangent + norm_back(grad, unit, inverse, gain[...])
    grad_middle_out[...] = grad_middle
    grad_middle_out.send()
    projected = grad_middle.astype(BF16)
    attended = mm_t(projected, output_weight[...])
    attended_low = attended.astype(BF16)
    query_all = query[...]
    grad_relative = attended * query_all
    shape = (CELLS, SLOTS, width)
    grid_grad[...] = mm(to_frame[...], grad_relative.astype(BF16)).reshape(shape)
    grid_value[...] = mm(to_frame[...], value[...]).reshape(shape)
    taps = relative_kernel.ref()

    def convolve(lanes):
        frame_conv(
            grid_grad,
            lambda a, b: taps[EDGE - 1 - a, EDGE - 1 - b : EDGE - b, lanes],
            grid_back,
            EDGE,
            lanes,
        )
        frame_taps(grid_grad, grid_value, head_sums, EDGE, lanes)

    over_lanes(width, convolve)
    wide_sums[0:1] = column_sum(projected.astype(F32))
    wide_sums[1:2] = column_sum(grad * unit)
    wide_sums[2:3] = column_sum(grad)
    wide_sums[3:4] = column_sum(cotangent)
    wide_sums[4:8] = jnp.zeros((4, D), F32)
    wide_sums.send()
    grad_query = SCALE * mm_t(attended_low, context[...]) + attended * relative[...]
    grad_context = SCALE * t_mm(query_all.astype(BF16), attended_low)
    grad_context = jnp.where(same_head(width), grad_context, 0.0)
    context_sum = lax.dot_general(
        jnp.ones((8, width), F32),
        grad_context * context[...].astype(F32),
        (((1,), (1,)), ((), ())),
        preferred_element_type=F32,
        precision=lax.Precision.HIGHEST,
    )[0:1]
    grad_context_low = grad_context.astype(BF16)
    weight_all = weight[...]
    grad_key = weight_all * (mm_t(value[...], grad_context_low) - context_sum)
    framed = grid_back[...].reshape(ROWS, width).astype(BF16)
    grad_value = mm(to_token[...], framed) + mm(weight_all.astype(BF16), grad_context_low)
    grad_query = grad_query.astype(BF16)
    grad_value = grad_value.astype(BF16)
    head_sums[49:50] = column_sum(grad_relative)
    head_sums[50:51] = column_sum(grad_query.astype(F32))
    head_sums[51:52] = column_sum(grad_value.astype(F32))
    head_sums[52:56] = jnp.zeros((4, width), F32)
    head_sums.send()
    grad_key = grad_key.astype(BF16)
    if split:
        keep, send = outs[4:]
        core = lax.axis_index("dp") & 1
        for which in range(2):

            @pl.when(core == which)
            def _():
                first, second = (keep, send) if which == 0 else (send, keep)
                first[:, 0:width] = grad_query
                first[:, width:D] = grad_key
                first[:, D:] = jnp.zeros_like(grad_value)
                second[:, 0:D] = projected
                second[:, D:] = grad_value

    else:
        outs[4][...] = projected
    grad_normed = None
    for index, low in enumerate((grad_query, grad_key, grad_value)):
        if not split:
            outs[5][index] = low
        term = mm_t(low, qkv_weight[index])
        grad_normed = term if grad_normed is None else grad_normed + term
    if len(ins) > 15:
        grad_normed_out[0] = grad_normed.astype(BF16)
        grad_normed_out[1] = ins[15][...]
    else:
        grad_normed_out[...] = grad_normed.astype(BF16)


def last_body(scalars, ins, outs, scratch):
    (
        mine,
        other,
        residual,
        gain,
        grad_middle,
        to_frame,
        tokens,
        position_kernel,
        to_token,
        middle,
        mlp_mine,
        down_bias,
    ) = ins[:12]
    block_out, token_grad, sums_out = outs
    grid_grad, grid_in, grid_back, sums = scratch
    unit, inverse = norm_parts(residual[...])
    grad = mine[...].astype(F32) + other[0].astype(F32)
    grad_residual = grad_middle[...] + norm_back(grad, unit, inverse, gain[...])
    grid_grad[...] = mm(to_frame[...], grad_residual.astype(BF16)).reshape(CELLS, SLOTS, D)
    grid_in[...] = mm(to_frame[...], tokens[...]).reshape(CELLS, SLOTS, D)
    taps = position_kernel.ref()
    block_out[...] = (
        middle[...] + (mlp_mine[...].astype(F32) + other[1].astype(F32)) + down_bias[...]
    )
    block_out.send()

    def convolve(lanes):
        frame_conv(
            grid_grad, lambda a, b: taps[2 - a, 2 - b : 3 - b, lanes], grid_back, 3, lanes
        )
        frame_taps(grid_grad, grid_in, sums, 3, lanes)

    over_lanes(D, convolve)
    framed = grid_back[...].reshape(ROWS, D).astype(BF16)
    token_grad[...] = grad_residual + mm(to_token[...], framed)
    token_grad.send()
    sums[9:10] = column_sum(grad_residual)
    sums[10:11] = column_sum(grad * unit)
    sums[11:12] = column_sum(grad)
    if len(ins) > 12:
        first, second = ins[12:]
        width = first.shape[1]
        sums[12:62, 0:width] = first[0:50] + second[0:50]
        sums[12:62, width:] = jnp.zeros((50, D - width), F32)
        sums[62:64] = jnp.zeros((2, D), F32)
    else:
        sums[12:16] = jnp.zeros((4, D), F32)
    sums_out[...] = sums[...].astype(sums_out.held.dtype)


def turn(values, distance, axis="dp"):
    size = lax.axis_size(axis)
    return lax.ppermute(values, axis, [(i, i ^ distance) for i in range(size)])


def step_bits():
    bits = list(range(1, lax.axis_size("dp").bit_length() - 1))
    return bits, bits[1::-1] + bits[2:]


def step_turn(values, step):
    orders = step_bits()
    size = lax.axis_size("dp")
    return lax.ppermute(values, "dp", [(i, i ^ (1 << orders[i & 1][step])) for i in range(size)])


def step_side(step):
    first, second = step_bits()
    me = lax.axis_index("dp")
    return (me >> jnp.where(me & 1 == 0, first[step], second[step])) & 1


def rows_of(side, count):
    return pl.ds(pl.multiple_of(side * count, 16), count)


def mlp_grads_body(scalars, ins, outs, scratch):
    hidden_width = ins[0].shape[1] - D
    core, side = lax.axis_index("dp") & 1, step_side(0)
    for which in range(2):

        @pl.when(core == which)
        def _():
            for target, place in ((outs[1], 1 - side), (outs[0], side)):
                columns = pl.ds(pl.multiple_of(place * D, 128), D)
                total = None
                for one in ins:
                    wide, narrow = one[:, columns], one[:, hidden_width:]
                    term = t_mm(narrow, wide) if which == 0 else t_mm(wide, narrow)
                    total = term if total is None else total + term
                target[...] = total.astype(BF16)


def attention_grads_body(images, scalars, ins, outs, scratch):
    stay, go = outs
    normed, attended = ins[:images], ins[images : 2 * images]
    far_early = ins[2 * images : 3 * images]
    late = ins[3 * images :]
    normed = [*normed, *far_early]
    width = D // 2

    def attended_of(place):
        return attended[place][...] if place < images else far_early[place - images][:, D:]

    def total(term):
        out = None
        for place in range(2 * images):
            out = term(place) if out is None else out + term(place)
        return out.astype(BF16)

    core, side = lax.axis_index("dp") & 1, step_side(0)

    @pl.when(core == 0)
    def _():
        for target, half in ((go, 1 - side), (stay, side)):
            columns = pl.ds(pl.multiple_of(half * width, 128), width)
            target[...] = total(lambda place: t_mm(normed[place][:, columns], late[place][:, 0:D]))

    for which in range(2):

        @pl.when((core == 1) & (side == which))
        def _():
            first, second = (stay, go) if which == 0 else (go, stay)
            first[...] = total(lambda place: t_mm(attended_of(place), late[place][:, 0:D]))
            for index in range(2):
                columns = slice(index * width, (index + 1) * width)
                second[:, columns] = total(
                    lambda place: t_mm(normed[place][:, columns], late[place][:, D:])
                )


def halve_body(step, scalars, ins, outs, scratch):
    here, came = ins
    here.ref()
    came.ref()
    if len(outs) == 1:
        outs[0][...] = (here[...].astype(F32) + came[...].astype(F32)).astype(BF16)
        return
    stay, go = outs
    count = stay.shape[0]
    side = step_side(step)
    for target, place in ((go, 1 - side), (stay, side)):
        rows = rows_of(place, count)
        target[...] = (here[rows, :].astype(F32) + came[rows, :].astype(F32)).astype(BF16)
        target.send()


def join_body(step, extra, scalars, ins, outs, scratch):
    here, came = ins
    side = step_side(step)
    count = here.shape[0] - extra
    outs[0].held[rows_of(side, count), :] = here[0:count, :]
    outs[0].held[rows_of(1 - side, count), :] = came[0:count, :]
    if extra:
        total = here[count:, :].astype(F32) + came[count:, :].astype(F32)
        outs[0][2 * count :, :] = total.astype(BF16)


def pack_body(scalars, ins, outs, scratch):
    here, came, mine, far, wide_one, wide_two, bias_one, bias_two, head_one, head_two = ins
    (rows,) = scratch
    count = here.shape[0]
    outs[0][0:count, :] = (here[...].astype(F32) + came[...].astype(F32)).astype(BF16)
    own, others = mine[...].astype(F32), far[...].astype(F32)
    width = D // 2
    rows[0:12] = own[0:12] + others[0:12]
    rows[12:16] = wide_one[0:4] + wide_two[0:4]
    member = lax.axis_index("mp")
    low = jnp.where(member == 0, own[:, 0:width], others[:, 0:width])
    high = jnp.where(member == 0, others[:, 0:width], own[:, 0:width])
    rows[16:66, 0:width] = low[12:62]
    rows[16:66, width:] = high[12:62]
    bias = bias_one[...] + bias_two[...]
    rows[66:67] = bias[:, 0:D]
    rows[67:68] = bias[:, D:]
    rows[68:69, 0:width] = head_one[50:51] + head_two[50:51]
    rows[68:69, width:] = head_one[51:52] + head_two[51:52]
    rows[69:SMALL] = jnp.zeros((SMALL - 69, D), F32)
    outs[0][count:, :] = rows[...].astype(BF16)


def mlp_final_body(scalars, ins, outs, scratch):
    mine, other = ins
    grad_up, grad_down, finished = outs
    finished[...] = jnp.zeros((8, 128), F32)
    mine.ref()
    other.ref()
    core = lax.axis_index("dp") & 1
    for side in range(2):

        @pl.when(core == side)
        def _():
            up, down = (mine, other) if side == 0 else (other, mine)
            for tile in range(down.shape[0] // D):
                rows = slice(tile * D, (tile + 1) * D)
                grad_up[:, rows] = up[rows, :].astype(F32)
            grad_down[...] = down[...].astype(F32)


def attention_final_body(scalars, ins, outs, scratch):
    mine, other = ins
    grad_qkv, grad_out, position, up_bias, pair_bias, three, five, seven = outs[:8]
    vectors = outs[8:]
    (small,) = scratch
    width = D // 2
    core = lax.axis_index("dp") & 1
    small[...] = mine[D:, :].astype(F32) + other[D:, :].astype(F32)
    for row in range(3):
        position[row] = small[3 * row : 3 * row + 3]
    position.send()
    for place, vector in zip((9, 10, 11, 65, 12, 13, 14, 15), vectors):
        vector[...] = small[place : place + 1]
        vector.send()
    up_bias[:, 0:D] = small[66:67]
    up_bias[:, D:] = small[67:68]
    up_bias.send()
    pair_bias[0:1] = small[68:69, 0:width]
    pair_bias[1:2] = small[68:69, width:]
    pair_bias.send()
    for row in range(3):
        begin = 16 + EDGE * (row + 2) + 2
        three[row] = small[begin : begin + 3, 0:128]
    three.send()
    for row in range(5):
        begin = 16 + EDGE * (row + 1) + 1
        five[row] = small[begin : begin + 5, 128:320]
    five.send()
    for row in range(EDGE):
        begin = 16 + EDGE * row
        seven[row] = pltpu.roll(small[begin : begin + EDGE, 256:512], 192, 1)[:, 0:192]
    seven.send()
    for side in range(2):

        @pl.when(core == side)
        def _():
            first, second = (mine, other) if side == 0 else (other, mine)
            for index in range(2):
                columns = slice(index * width, (index + 1) * width)
                grad_qkv[index] = first[0:D, columns].astype(F32)
                grad_qkv[2, columns, :] = second[width:D, columns].astype(F32)
            grad_out[...] = second[0:width, :].astype(F32)


def halve(keep, came, step, after=(), us=0.0):
    outs = [((keep.shape[0] // 2, D), BF16)] * 2
    body = functools.partial(halve_body, step)
    keep, send = call(body, outs, (keep, came), us=us, after=after)
    return keep, step_turn(send, step)


def join(keep, came, step, extra=0, after=(), us=0.0):
    outs = [(((keep.shape[0] - extra) * 2 + extra, D), BF16)]
    body = functools.partial(join_body, step, extra)
    return call(body, outs, (keep, came), us=us, after=after)[0]


def sum_small(values):
    size = lax.axis_size("dp")
    if size & (size - 1):
        return lax.psum(values, "dp")
    for bit in range(size.bit_length() - 1):
        values = values + turn(values, 1 << bit)
    return values


def whole_body(products, scalars, ins, outs, scratch):
    for target, pairs in zip(outs, products):
        total = None
        for left, right in pairs:
            one, two = (ins[i][...] if part is None else ins[i][part] for i, part in (left, right))
            term = t_mm(one, two)
            total = term if total is None else total + term
        target[...] = total.astype(BF16)


def per_device(
    tokens,
    out_grad,
    crop_image,
    crop_res,
    position_kernel,
    position_bias,
    gain_one,
    shift_one,
    qkv_weight,
    query_value_bias,
    relative_three,
    relative_five,
    relative_seven,
    relative_bias,
    output_weight,
    output_bias,
    gain_two,
    shift_two,
    up_weight,
    up_bias,
    down_weight,
    down_bias,
):
    group = lax.axis_size("mp")
    member = lax.axis_index("mp")
    rows = tokens.shape[0]
    width = qkv_weight.shape[2]
    hidden_width = up_weight.shape[1]
    pair = group == 2
    size = lax.axis_size("dp")
    blocks = (
        pair
        and size >= 4
        and size & (size - 1) == 0
        and 2 * width == D
        and hidden_width == 2 * D
        and D % (size * 8) == 0
    )

    def row(vector):
        return vector.reshape(1, -1)

    if not blocks:
        full_kernel = jnp.concatenate(
            [
                jnp.pad(relative_three, ((2, 2), (2, 2), (0, 0))),
                jnp.pad(relative_five, ((1, 1), (1, 1), (0, 0))),
                relative_seven,
            ],
            axis=2,
        )
        kernel_part = lax.dynamic_slice_in_dim(full_kernel, member * width, width, 2)
        bias_part = row(lax.dynamic_slice_in_dim(relative_bias, member * width, width, 0))
    else:
        kernel_part, bias_part = None, row(relative_bias)
    qkv_planes = jnp.transpose(qkv_weight, (1, 0, 2))

    if pair:
        token_list = [tokens, turn(tokens, 1, "mp")]
        images = [lambda: lax.axis_index("mp"), lambda: 1 - lax.axis_index("mp")]
    else:
        token_list = list(lax.all_gather(tokens, "mp", axis=0))
        grad_list = list(lax.all_gather(out_grad, "mp", axis=0))
        images = [functools.partial(int, j) for j in range(group)]

    def own(parts):
        if pair:
            return parts[0]
        return lax.dynamic_index_in_dim(jnp.stack(parts), member, 0, keepdims=False)

    fronts = []
    for index, (image, one) in enumerate(zip(images, token_list)):
        table = blocks and index == 0
        outs = [
            Far((ROWS, rows), BF16),
            Far((rows, ROWS), BF16),
            ((rows, D), F32),
            Far((rows, D), BF16),
            Far((rows, width), F32),
            Far((rows, width), BF16),
            Far((rows, width), F32),
            Far((width, width), BF16),
            Far((rows, width), F32),
            Far((rows, width), BF16),
            ((rows, D), BF16),
        ]
        if blocks:
            outs.append(((rows, D + width), BF16))
        args = [
            crop_res,
            Far(one) if index == 0 else one,
            Far(position_kernel),
            Far(row(position_bias)),
            Far(row(gain_one)),
            Far(row(shift_one)),
            Far(qkv_planes),
            Far(query_value_bias),
        ]
        if table:
            outs += [Far((EDGE, EDGE, width), F32), Far((rows, D), F32)]
            args += [Far(relative_three), Far(relative_five), Far(relative_seven)]
        else:
            args.append(Far(kernel_part))
        args += [Far(bias_part), Far(output_weight)]
        scratch = [pltpu.VMEM((CELLS, SLOTS, D), F32)] * 2
        body = functools.partial(front_body, image, table, blocks)
        if index:
            args = [one.what[0] if isinstance(one, Far) and one.what[0] is not kernel_part else one for one in args]
        made = call(body, outs, args, scratch, us=50.0 if index == 0 else 5.0, smem=1)
        if table:
            kernel_part, kept_residual = made[12:14]
        fronts.append(made[: 12 if blocks else 11])
    to_frame, to_token, residual, normed, query, value, weight, context = tuple(zip(*fronts))[:8]
    relative, attended, partial, *early = tuple(zip(*fronts))[8:]

    if pair:
        args = (partial[0], out_grad)
        (both,) = call(pair_body, [((2, rows, D), BF16)], args, us=0.3, after=[token_list[1]])
        first, second = turn(both, 1, "mp"), turn(partial[1], 1, "mp")
        grad_list, grad_parts = [out_grad, first], [None, 1]
        addends = [(partial[0], second), (partial[1], first)]
        places = [(None, None), (None, 0)]
        order = (1, 0)
    else:
        total = lax.psum(jnp.stack(partial), "mp")
        grad_parts = [None] * group
        addends = [(one, jnp.zeros_like(one)) for one in total]
        places = [(None, None)] * group
        order = range(group)
    mlps = [None] * group
    for index in order:
        outs = [Far((rows, D), F32), ((rows, D), BF16), Far((rows, D), BF16)]
        outs.append(Far((1, hidden_width), F32))
        scratch = []
        if blocks:
            outs += [((rows, hidden_width + D), BF16)] * 2
            scratch = [pltpu.VMEM((rows, hidden_width), BF16)] * 2
        else:
            outs += [((rows, hidden_width), BF16)] * 2 + [((rows, D), BF16)]
        args = (
            residual[index],
            *addends[index],
            grad_list[index],
            row(output_bias),
            row(gain_two),
            row(shift_two),
            up_weight,
            row(up_bias.astype(F32)),
            down_weight,
        )
        body = functools.partial(mlp_body, (*places[index], grad_parts[index]), blocks)
        after = [mlps[1][1]] if pair and index == 0 else []
        mlps[index] = call(body, outs, args, scratch, us=2.5, after=after)
    middle, grad_two_part, mlp_part, grad_up_bias, *mlp_rows = zip(*mlps)

    if pair:
        back_addends = [
            (grad_two_part[0], turn(grad_two_part[1], 1, "mp")),
            (grad_two_part[1], turn(grad_two_part[0], 1, "mp")),
        ]
    else:
        total = lax.psum(jnp.stack(grad_two_part), "mp")
        back_addends = [(one, jnp.zeros_like(one)) for one in total]

    steps = len(step_bits()[0])
    if blocks:
        args = (*mlp_rows[0], *(turn(one, 1) for one in mlp_rows[1]))
        after = [mark(back_addends[0][1], 60.0)]
        mlp_keep, mlp_send = call(mlp_grads_body, [((D, D), BF16)] * 2, args, us=2.0, after=after)
        mlp_came = step_turn(mlp_send, 0)

    backs = []
    for index in range(group):
        carry = pair and index == 1
        outs = [
            Far((rows, D), F32),
            ((2, rows, D) if carry else (rows, D), BF16),
            Far((8, D), F32),
            Far((56, width), F32),
        ]
        if blocks:
            outs += [((rows, D + width), BF16)] * 2
        else:
            outs += [((rows, D), BF16), ((3, rows, width), BF16)]
        args = [
            *back_addends[index],
            grad_list[index],
            middle[index],
            row(gain_two),
            output_weight,
            query[index],
            to_frame[index],
            value[index],
            kernel_part,
            context[index],
            relative[index],
            weight[index],
            to_token[index],
            qkv_planes,
        ]
        if carry:
            args.append(mlp_part[1])
        scratch = [pltpu.VMEM((CELLS, SLOTS, width), F32)] * 3
        body = functools.partial(back_body, (None, None, grad_parts[index]), blocks)
        after = [mlp_keep] if blocks else []
        if pair and index:
            after.append(backs[0][1])
        backs.append(call(body, outs, args, scratch, us=5.0, after=after))
    grad_middle, grad_one_part, wide_sums, head_sums, *late = zip(*backs)

    if blocks:
        mlp_keep, mlp_came = halve(mlp_keep, mlp_came, 1, after=[backs[1][1]])
        outs = [((width, D), BF16)] * 2
        args = (*normed, *attended, *(turn(one, 1) for one in early[0]))
        args += (*late[0], *(turn(one, 1) for one in late[1]))
        body = functools.partial(attention_grads_body, group)
        keep, send = call(body, outs, args, us=2.0, after=[mlp_keep])
        came = step_turn(send, 0)
    if not blocks:
        hidden, grad_pre, normed_two = mlp_rows
        grad_projected, grad_qkv = late
        args = (*normed_two, *grad_pre, *hidden, *grad_list)
        args += (*normed, *grad_qkv, *attended, *grad_projected)

        def spot(kind, image, part=None):
            return kind * group + image, part

        each = range(group)
        products = [
            [(spot(0, j), spot(1, j)) for j in each],
            [(spot(2, j), spot(3, j, grad_parts[j])) for j in each],
        ]
        products += [[(spot(4, j), spot(5, j, plane)) for j in each] for plane in range(3)]
        products += [[(spot(6, j), spot(7, j)) for j in each]]
        outs = [((D, hidden_width), BF16), ((hidden_width, D), BF16)]
        outs += [((D, width), BF16)] * 3 + [((width, D), BF16)]
        wholes = call(functools.partial(whole_body, products), outs, args, us=6.0, vmem=40)
        grad_up, grad_down, *planes, grad_out = (lax.psum(one, "dp").astype(F32) for one in wholes)
        grad_qkv_planes = jnp.stack(planes)

    if pair:
        mine, mlp_mine = grad_one_part[0], mlp_part[0]
        other = turn(grad_one_part[1], 1, "mp")
    else:
        sums = [jnp.stack(grad_one_part), jnp.stack(mlp_part)]
        mine, mlp_mine = (lax.psum_scatter(one, "mp", scatter_dimension=0) for one in sums)
        other = jnp.zeros((2, rows, D), BF16)
    outs = [Far((rows, D), F32), Far((rows, D), F32)]
    outs.append(((64, D), BF16) if blocks else ((16, D), F32))
    args = [
        mine,
        other,
        kept_residual if blocks else own(residual),
        row(gain_one),
        own(grad_middle),
        own(to_frame),
        tokens,
        position_kernel,
        own(to_token),
        own(middle),
        mlp_mine,
        row(down_bias),
    ]
    if blocks:
        args += [*head_sums]
    scratch = [pltpu.VMEM((CELLS, SLOTS, D), F32)] * 3
    scratch.append(pltpu.VMEM((64 if blocks else 16, D), F32))
    after = []
    if blocks:
        keep, came = halve(keep, came, 1, after=[mlp_keep], us=WEIGH)
        after = [keep]
    block_out, token_grad, own_sums = call(last_body, outs, args, scratch, us=5.0, after=after)

    if blocks:
        far_sums = turn(own_sums, 1, "mp")
        for step in range(2, steps):
            mlp_keep, mlp_came = halve(mlp_keep, mlp_came, step, after=[own_sums])
            keep, came = halve(keep, came, step, after=[mlp_keep], us=WEIGH)
        outs = [(mlp_keep.shape, BF16)]
        body = functools.partial(halve_body, None)
        (mlp_keep,) = call(body, outs, (mlp_keep, mlp_came), us=0.0, after=[keep])
        mlp_came = step_turn(mlp_keep, steps - 1)
        args = (keep, came, own_sums, far_sums)
        args += (*wide_sums, *grad_up_bias, *head_sums)
        outs = [((keep.shape[0] + SMALL, D), BF16)]
        scratch = [pltpu.VMEM((SMALL, D), F32)]
        (keep,) = call(pack_body, outs, args, scratch, us=WEIGH, after=[mlp_keep])
        for step in reversed(range(steps)):
            came = step_turn(keep, step)
            mlp_keep = join(mlp_keep, mlp_came, step, after=[keep])
            mlp_came = step_turn(mlp_keep, step - 1) if step else turn(mlp_keep, 1)
            keep = join(keep, came, step, SMALL, after=[mlp_keep], us=WEIGH)
        came = turn(keep, 1)
        outs = [Far((D, hidden_width), F32), Far((hidden_width, D), F32), ((8, 128), F32)]
        args = (mlp_keep, mlp_came)
        grad_up, grad_down, finished = call(mlp_final_body, outs, args, us=2.0, after=[keep])
        shapes = [(3, D, width), (width, D), (3, 3, D), (1, hidden_width), (2, width)]
        shapes += [relative_three.shape, relative_five.shape, relative_seven.shape]
        outs = [Far(shape, F32) for shape in shapes + [(1, D)] * 8]
        scratch = [pltpu.VMEM((SMALL, D), F32)]
        made = call(attention_final_body, outs, (keep, came), scratch, us=2.0, after=[finished])
        grad_qkv_planes, grad_out, position, up_sum, pair_sum, three, five, seven = made[:8]
        vectors = [one.reshape(D) for one in made[8:]]
        return (
            block_out,
            token_grad,
            position,
            *vectors[0:3],
            jnp.transpose(grad_qkv_planes, (1, 0, 2)),
            pair_sum,
            three,
            five,
            seven,
            vectors[3],
            grad_out,
            *vectors[4:7],
            grad_up,
            up_sum.reshape(hidden_width),
            grad_down,
            vectors[7],
        )

    head_total = functools.reduce(jnp.add, head_sums)
    wide_total = functools.reduce(jnp.add, wide_sums)
    own_total = lax.psum(own_sums[:12], "mp")
    relative_total = lax.all_gather(head_total[:50], "mp", axis=1, tiled=True)
    bias_total = functools.reduce(jnp.add, grad_up_bias)
    pieces = [own_total, wide_total[:4], relative_total]
    private = jnp.concatenate([bias_total.reshape(-1), head_total[50:52].reshape(-1)])
    pieces.append(jnp.pad(private, (0, -private.shape[0] % D)).reshape(-1, D))
    total = sum_small(jnp.concatenate(pieces, axis=0))
    kernel_grad = total[16:65].reshape(EDGE, EDGE, D)
    tail = total[66:].reshape(-1)
    return (
        block_out,
        token_grad,
        total[:9].reshape(3, 3, D),
        total[9],
        total[10],
        total[11],
        jnp.transpose(grad_qkv_planes, (1, 0, 2)),
        tail[hidden_width : hidden_width + 2 * width].reshape(2, width),
        kernel_grad[2:5, 2:5, : 2 * HEAD],
        kernel_grad[1:6, 1:6, 2 * HEAD : 5 * HEAD],
        kernel_grad[:, :, 5 * HEAD :],
        total[65],
        grad_out,
        total[12],
        total[13],
        total[14],
        grad_up,
        tail[:hidden_width],
        grad_down,
        total[15],
    )


def solution(mesh):
    in_specs = (
        P(("dp", "mp"), None),
        P(("dp", "mp"), None),
        P("dp"),
        P("dp"),
        P(),
        P(),
        P(),
        P(),
        P(None, None, "mp"),
        P(None, "mp"),
        P(),
        P(),
        P(),
        P(),
        P("mp", None),
        P(),
        P(),
        P(),
        P(None, "mp"),
        P("mp"),
        P("mp", None),
        P(),
    )
    out_specs = (
        P(("dp", "mp"), None),
        P(("dp", "mp"), None),
        P(),
        P(),
        P(),
        P(),
        P(None, None, "mp"),
        P(None, "mp"),
        P(),
        P(),
        P(),
        P(),
        P("mp", None),
        P(),
        P(),
        P(),
        P(None, "mp"),
        P("mp"),
        P("mp", None),
        P(),
    )
    return jax.shard_map(
        per_device, mesh=mesh, in_specs=in_specs, out_specs=out_specs, check_vma=False
    )
```

```python
import functools
import math

import jax
import jax.numpy as jnp
from jax import lax
from jax.experimental import pallas as pl
from jax.experimental.pallas import tpu as pltpu
from jax.sharding import PartitionSpec as P

HEAD = 64
D = 512
EPSILON = 1e-06
SLOTS = 8
EDGE = 7
CELLS = EDGE * EDGE
ROWS = CELLS * SLOTS
SCALE = HEAD ** (-0.5)
SMALL = 64
FREE = [7 * i + j for i in range(7) for j in range(7) if i in (0, 6) or j in (0, 6)]
WEIGHTS = dict(
    h1=0.0, h2=0.0, p1=40.0, last=0.0, p2=0.0, total=0.0, pack=0.0, j2=0.0, a2=0.0, j1=0.0, a1=40.0, j0=0.0, a0=40.0
)
BF16 = jnp.bfloat16
F32 = jnp.float32


def mm(left, right):
    return jnp.dot(left, right, preferred_element_type=F32)


def mm_t(left, right):
    return lax.dot_general(left, right, (((1,), (1,)), ((), ())), preferred_element_type=F32)


def t_mm(left, right):
    return lax.dot_general(left, right, (((0,), (0,)), ((), ())), preferred_element_type=F32)


def split_mm(onehot, values):
    high = values.astype(BF16)
    low = (values - high.astype(F32)).astype(BF16)
    return mm(onehot, high) + mm(onehot, low)


class Source:
    def __init__(self, ref, copy=None):
        self.held, self.copy, self.shape = ref, copy, ref.shape

    def ref(self):
        if self.copy is not None:
            self.copy.wait()
            self.copy = None
        return self.held

    def __getitem__(self, index):
        return self.ref()[index]


class Result:
    def __init__(self, ref, copy=None):
        self.held, self.copy, self.sent, self.shape = ref, copy, copy is None, ref.shape

    def __setitem__(self, index, value):
        self.held[index] = value

    def __getitem__(self, index):
        return self.held[index]

    def send(self):
        if not self.sent:
            self.copy.start()
            self.sent = True


class Far:
    def __init__(self, *what):
        self.what = what


def call(body, outs, args, scratch=(), us=3.0, smem=0, vmem=24, after=()):
    far_in = [isinstance(one, Far) for one in args[smem:]]
    far_out = [isinstance(one, Far) for one in outs]
    arrays = [one.what[0] if isinstance(one, Far) else one for one in args[smem:]]
    outs = [one.what if isinstance(one, Far) else one for one in outs]

    def kernel(*refs):
        refs = list(refs)

        def take(count):
            taken = refs[:count]
            del refs[:count]
            return taken

        far_scalars, given = take(smem), take(len(arrays))
        take(len(after))
        places = take(len(outs))
        near_scalars = take(smem)
        scalar_sems = take(1)[0] if smem else None
        near_in, near_out = take(sum(far_in)), take(sum(far_out))
        scalars = []
        for index, (away, near) in enumerate(zip(far_scalars, near_scalars)):
            copy = pltpu.make_async_copy(away, near, scalar_sems.at[index])
            copy.start()
            scalars.append(Source(near, copy))
        in_sems = take(1)[0] if any(far_in) else None
        out_sems = take(1)[0] if any(far_out) else None
        ins, made = [], []
        for ref, far in zip(given, far_in):
            if far:
                index = sum(one.copy is not None for one in ins)
                copy = pltpu.make_async_copy(ref, near_in[index], in_sems.at[index])
                copy.start()
                ins.append(Source(near_in[index], copy))
            else:
                ins.append(Source(ref))
        for ref, far in zip(places, far_out):
            if far:
                index = sum(one.copy is not None for one in made)
                copy = pltpu.make_async_copy(near_out[index], ref, out_sems.at[index])
                made.append(Result(near_out[index], copy))
            else:
                made.append(Result(ref))
        body(scalars, ins, made, refs)
        for one in made:
            one.send()
        for one in scalars + ins:
            one.ref()
        for one in made:
            if one.copy is not None:
                one.copy.wait()

    shapes = [pltpu.SMEM(one.shape, one.dtype) for one in args[:smem]]
    if smem:
        shapes.append(pltpu.SemaphoreType.DMA((smem,)))
    shapes += [pltpu.VMEM(one.shape, one.dtype) for one, far in zip(arrays, far_in) if far]
    shapes += [pltpu.VMEM(*one) for one, far in zip(outs, far_out) if far]
    if any(far_in):
        shapes.append(pltpu.SemaphoreType.DMA((sum(far_in),)))
    if any(far_out):
        shapes.append(pltpu.SemaphoreType.DMA((sum(far_out),)))
    near, far = pl.BlockSpec(memory_space=pltpu.VMEM), pl.BlockSpec(memory_space=pltpu.HBM)
    operands = [
        pltpu.with_memory_space_constraint(one, pltpu.HBM) if away else one
        for one, away in zip(arrays, far_in)
    ]
    scalars_far = [pltpu.with_memory_space_constraint(one, pltpu.HBM) for one in args[:smem]]
    return pl.pallas_call(
        kernel,
        out_shape=[
            pltpu.HBM(*one) if away else jax.ShapeDtypeStruct(*one)
            for one, away in zip(outs, far_out)
        ],
        in_specs=[far] * smem
        + [far if away else near for away in far_in]
        + [pl.BlockSpec(memory_space=pl.ANY)] * len(after),
        out_specs=[far if away else near for away in far_out],
        scratch_shapes=shapes + list(scratch),
        compiler_params=pltpu.CompilerParams(vmem_limit_bytes=vmem << 20),
        cost_estimate=pl.CostEstimate(
            flops=int(us * 1.0e8), bytes_accessed=1 << 12, transcendentals=0
        ),
    )(*scalars_far, *operands, *after)


def over_lanes(width, body):
    if width % 128 == 0:

        @pl.loop(0, width // 128)
        def _(step):
            body(pl.ds(pl.multiple_of(step * 128, 128), 128))

    else:
        body(slice(0, width))


def frame_conv(source, tap, target, edge, lanes):
    half = (edge - 1) // 2
    for i in range(EDGE):
        total = [None] * EDGE
        for a in range(edge):
            row = i + a - half
            if not 0 <= row < EDGE:
                continue
            cells = [source[row * EDGE + j, :, lanes] for j in range(EDGE)]
            for b in range(edge):
                weight = tap(a, b)
                for j in range(EDGE):
                    column = j + b - half
                    if 0 <= column < EDGE:
                        term = cells[column] * weight
                        total[j] = term if total[j] is None else total[j] + term
        for j in range(EDGE):
            target[i * EDGE + j, :, lanes] = total[j]


def frame_taps(grad, source, target, edge, lanes):
    half = (edge - 1) // 2
    for a in range(edge):
        total = [None] * edge
        for i in range(EDGE):
            row = i + a - half
            if not 0 <= row < EDGE:
                continue
            cells = [source[row * EDGE + j, :, lanes] for j in range(EDGE)]
            for j in range(EDGE):
                own = grad[i * EDGE + j, :, lanes]
                for b in range(edge):
                    column = j + b - half
                    if 0 <= column < EDGE:
                        term = own * cells[column]
                        total[b] = term if total[b] is None else total[b] + term
        for b in range(edge):
            row = a * edge + b
            target[row : row + 1, lanes] = jnp.sum(total[b], axis=0, keepdims=True)


def crop_frames(kinds, base, rows):
    sub = lax.broadcasted_iota(jnp.int32, (SLOTS, rows), 0)
    lane = lax.broadcasted_iota(jnp.int32, (SLOTS, rows), 1)
    place = lax.broadcasted_iota(jnp.int32, (8, ROWS), 1)
    slot = place & (SLOTS - 1)
    cell = place >> 3
    down = (cell * 37) >> 8
    across = cell - down * EDGE
    begin = jnp.zeros((SLOTS, rows), jnp.int32)
    whole = jnp.zeros((SLOTS, rows), jnp.int32)
    begin_row = jnp.zeros((8, ROWS), jnp.int32)
    whole_row = jnp.zeros((8, ROWS), jnp.int32)
    start = jnp.int32(0)
    for s in range(SLOTS):
        large = (kinds[base + s] == 0).astype(jnp.int32)
        begin = jnp.where(sub == s, start, begin)
        whole = jnp.where(sub == s, large, whole)
        begin_row = jnp.where(slot == s, start, begin_row)
        whole_row = jnp.where(slot == s, large, whole_row)
        start = start + 9 + 40 * large
    tiles = []
    for i in range(EDGE):
        for j in range(EDGE):
            small = begin + (i * 3 + j) if i < 3 and j < 3 else jnp.full_like(begin, -1)
            token = jnp.where(whole == 1, begin + (i * EDGE + j), small)
            tiles.append(jnp.where(token == lane, 1.0, 0.0))
    to_frame = jnp.concatenate(tiles, axis=0).astype(BF16)
    corner = jnp.where((down < 3) & (across < 3), begin_row + down * 3 + across, -1)
    token_row = jnp.where(whole_row == 1, begin_row + cell, corner)
    height = lax.broadcasted_iota(jnp.int32, (rows, ROWS), 0)
    to_token = jnp.where(height == token_row[0:1], 1.0, 0.0).astype(BF16)
    return to_frame, to_token


def norm_parts(values):
    average = jnp.mean(values, axis=-1, keepdims=True)
    centred = values - average
    variance = jnp.mean(centred * centred, axis=-1, keepdims=True)
    inverse = lax.rsqrt(variance + EPSILON)
    return centred * inverse, inverse


def norm_back(grad, unit, inverse, gain):
    scaled = grad * gain
    first = jnp.mean(scaled, axis=-1, keepdims=True)
    second = jnp.mean(scaled * unit, axis=-1, keepdims=True)
    return (scaled - first - unit * second) * inverse


def column_sum(values):
    return jnp.sum(values, axis=0, keepdims=True)


def same_head(width):
    rows = lax.broadcasted_iota(jnp.int32, (width, width), 0) // HEAD
    columns = lax.broadcasted_iota(jnp.int32, (width, width), 1) // HEAD
    return rows == columns


def tap_table(member, three, five, seven, table):
    table[...] = jnp.zeros(table.shape, F32)

    @pl.when(member == 0)
    def _():
        table[2:5, 2:5, 0:128] = three[...]
        for row in range(5):
            table[1 + row, 1:6, 128:256] = five[row, :, 0:128]

    @pl.when(member == 1)
    def _():
        for row in range(5):
            table[1 + row, 1:6, 0:64] = five[row, :, 128:192]
        lane = lax.broadcasted_iota(jnp.int32, (EDGE, 128), 1)
        for row in range(EDGE):
            near = pltpu.roll(seven[row, :, 0:128], 64, 1)
            wide = jnp.concatenate([seven[row, :, 128:192], jnp.zeros((EDGE, 64), F32)], axis=1)
            far = pltpu.roll(wide, 64, 1)
            table[row, :, 0:128] = jnp.where(lane < 64, table[row, :, 0:128], near)
            table[row, :, 128:256] = jnp.where(lane < 64, near, far)


def front_body(image, table, early, scalars, ins, outs, scratch):
    (kinds,) = scalars
    tokens, position_kernel, position_bias, gain, shift, qkv_weight, pair_bias = ins[:7]
    relative_bias, output_weight = ins[-2:]
    (
        to_frame_out,
        to_token_out,
        residual_out,
        normed_out,
        query_out,
        value_out,
        weight_out,
        context_out,
        relative_out,
        attended_out,
        partial_out,
    ) = outs[:11]
    grid_in, grid_out = scratch
    rows = tokens.shape[0]
    width = output_weight.shape[0]
    member = lax.axis_index("mp")
    to_frame, to_token = crop_frames(kinds, image() * SLOTS, rows)
    to_frame_out[...] = to_frame
    to_frame_out.send()
    to_token_out[...] = to_token
    to_token_out.send()
    grid_in[...] = mm(to_frame, tokens[...]).reshape(CELLS, SLOTS, D)
    position_taps = position_kernel.ref()

    def position(lanes):
        frame_conv(grid_in, lambda a, b: position_taps[a, b : b + 1, lanes], grid_out, 3, lanes)

    over_lanes(D, position)
    residual = tokens[...].astype(F32) + split_mm(to_token, grid_out[...].reshape(ROWS, D))
    residual = residual + position_bias[...]
    residual_out[...] = residual
    if table:
        outs[13][...] = residual
        outs[13].send()
    unit, _ = norm_parts(residual)
    normed = (unit * gain[...] + shift[...]).astype(BF16)
    normed_out[...] = normed
    normed_out.send()
    pair = pair_bias[...].astype(F32)
    value = (mm(normed, qkv_weight[2]) + pair[1:2]).astype(BF16)
    value_out[...] = value
    value_out.send()
    grid_in[:, :, 0:width] = mm(to_frame, value).reshape(CELLS, SLOTS, width)
    query = mm(normed, qkv_weight[0]) + pair[0:1]
    query_out[...] = query
    query_out.send()
    keys = mm(normed, qkv_weight[1])
    weight = jnp.exp(keys - jnp.max(keys, axis=0, keepdims=True))
    weight = weight / column_sum(weight)
    weight_out[...] = weight
    weight_out.send()
    context = jnp.where(same_head(width), t_mm(weight.astype(BF16), value), 0.0).astype(BF16)
    context_out[...] = context
    context_out.send()
    if table:
        relative_kernel = outs[12]
        for one in ins[7:10]:
            one.ref()
        tap_table(member, *ins[7:10], relative_kernel.held)
        relative_kernel.send()
        relative_taps = relative_kernel.held
    else:
        relative_taps = ins[7].ref()

    def relative(lanes):
        frame_conv(
            grid_in, lambda a, b: relative_taps[a, b : b + 1, lanes], grid_out, EDGE, lanes
        )

    over_lanes(width, relative)
    if relative_bias.shape[1] == width:
        bias_row = relative_bias[...]
    else:
        bias_row = relative_bias[:, pl.ds(pl.multiple_of(member * width, 128), width)]
    framed = grid_out[:, :, 0:width].reshape(ROWS, width).astype(BF16)
    position_term = mm(to_token, framed) + bias_row
    relative_out[...] = position_term
    relative_out.send()
    attended = SCALE * mm(query.astype(BF16), context) + query * position_term
    attended = attended.astype(BF16)
    attended_out[...] = attended
    attended_out.send()
    if early:
        outs[11][:, 0:D] = normed
        outs[11][:, D:] = attended
    partial_out[...] = mm(attended, output_weight[...]).astype(BF16)


def mark(array, us):
    def body(scalars, ins, outs, scratch):
        outs[0][...] = jnp.zeros((8, 128), F32)

    return call(body, [((8, 128), F32)], (), us=us, after=[array])[0]


def pair_body(scalars, ins, outs, scratch):
    for index, one in enumerate(ins):
        outs[0][index] = one[...]


def picked(source, part):
    return source[...] if part is None else source[part]


def mlp_body(parts, split, scalars, ins, outs, scratch):
    (
        residual,
        first,
        second,
        cotangent,
        output_bias,
        gain,
        shift,
        up_weight,
        up_bias,
        down_weight,
    ) = ins
    middle_out, grad_normed_out, mlp_out, grad_bias_out = outs[:4]
    hidden_out, grad_pre_out = scratch if split else outs[4:6]
    hidden_width = up_weight.shape[1]
    projected = picked(first, parts[0]).astype(F32) + picked(second, parts[1]).astype(F32)
    middle = residual[...] + projected + output_bias[...]
    middle_out[...] = middle
    middle_out.send()
    unit, _ = norm_parts(middle)
    normed = (unit * gain[...] + shift[...]).astype(BF16)
    out_grad = picked(cotangent, parts[2])
    step = min(256, hidden_width)
    for begin in range(0, hidden_width, step):
        part = slice(begin, begin + step)
        pre = mm(normed, up_weight[:, part]) + up_bias[:, part]
        below = 0.5 * (1.0 + lax.erf(pre * (2.0**-0.5)))
        hidden_out[:, part] = (pre * below).astype(BF16)
        slope = below + pre * jnp.exp(-0.5 * pre * pre) * ((2.0 * math.pi) ** -0.5)
        grad = (mm_t(out_grad, down_weight[part, :]) * slope).astype(BF16)
        grad_pre_out[:, part] = grad
        grad_bias_out[:, part] = column_sum(grad.astype(F32))
    grad_bias_out.send()
    mlp_out[...] = mm(hidden_out[...], down_weight[...]).astype(BF16)
    mlp_out.send()
    grad_normed_out[...] = mm_t(grad_pre_out[...], up_weight[...]).astype(BF16)
    if not split:
        outs[6][...] = normed
        return
    keep, send = outs[4:6]
    core = lax.axis_index("dp") & 1
    for side in range(2):

        @pl.when(core == side)
        def _():
            up, down = (keep, send) if side == 0 else (send, keep)
            up[:, 0:hidden_width] = grad_pre_out[...]
            up[:, hidden_width:] = normed
            down[:, 0:hidden_width] = hidden_out[...]
            down[:, hidden_width:] = out_grad


def back_body(parts, split, scalars, ins, outs, scratch):
    (
        mine,
        other,
        out_grad,
        middle,
        gain,
        output_weight,
        query,
        to_frame,
        value,
        relative_kernel,
        context,
        relative,
        weight,
        to_token,
        qkv_weight,
    ) = ins[:15]
    grad_middle_out, grad_normed_out, wide_sums, head_sums = outs[:4]
    grid_grad, grid_value, grid_back = scratch
    width = relative_kernel.shape[2]
    unit, inverse = norm_parts(middle[...])
    grad = picked(mine, parts[0]).astype(F32) + picked(other, parts[1]).astype(F32)
    cotangent = picked(out_grad, parts[2]).astype(F32)
    grad_middle = cotangent + norm_back(grad, unit, inverse, gain[...])
    grad_middle_out[...] = grad_middle
    grad_middle_out.send()
    projected = grad_middle.astype(BF16)
    attended = mm_t(projected, output_weight[...])
    attended_low = attended.astype(BF16)
    query_all = query[...]
    grad_relative = attended * query_all
    shape = (CELLS, SLOTS, width)
    grid_grad[...] = mm(to_frame[...], grad_relative.astype(BF16)).reshape(shape)
    grid_value[...] = mm(to_frame[...], value[...]).reshape(shape)
    taps = relative_kernel.ref()

    def convolve(lanes):
        frame_conv(
            grid_grad,
            lambda a, b: taps[EDGE - 1 - a, EDGE - 1 - b : EDGE - b, lanes],
            grid_back,
            EDGE,
            lanes,
        )
        frame_taps(grid_grad, grid_value, head_sums, EDGE, lanes)

    over_lanes(width, convolve)
    wide_sums[0:1] = column_sum(projected.astype(F32))
    wide_sums[1:2] = column_sum(grad * unit)
    wide_sums[2:3] = column_sum(grad)
    wide_sums[3:4] = column_sum(cotangent)
    wide_sums[4:8] = jnp.zeros((4, D), F32)
    wide_sums.send()
    grad_query = SCALE * mm_t(attended_low, context[...]) + attended * relative[...]
    grad_context = SCALE * t_mm(query_all.astype(BF16), attended_low)
    grad_context = jnp.where(same_head(width), grad_context, 0.0)
    context_sum = lax.dot_general(
        jnp.ones((8, width), F32),
        grad_context * context[...].astype(F32),
        (((1,), (1,)), ((), ())),
        preferred_element_type=F32,
        precision=lax.Precision.HIGHEST,
    )[0:1]
    grad_context_low = grad_context.astype(BF16)
    weight_all = weight[...]
    grad_key = weight_all * (mm_t(value[...], grad_context_low) - context_sum)
    framed = grid_back[...].reshape(ROWS, width).astype(BF16)
    grad_value = mm(to_token[...], framed) + mm(weight_all.astype(BF16), grad_context_low)
    grad_query = grad_query.astype(BF16)
    grad_value = grad_value.astype(BF16)
    head_sums[49:50] = column_sum(grad_relative)
    head_sums[50:51] = column_sum(grad_query.astype(F32))
    head_sums[51:52] = column_sum(grad_value.astype(F32))
    head_sums[52:56] = jnp.zeros((4, width), F32)
    head_sums.send()
    grad_key = grad_key.astype(BF16)
    if split:
        keep, send = outs[4:]
        core = lax.axis_index("dp") & 1
        for which in range(2):

            @pl.when(core == which)
            def _():
                first, second = (keep, send) if which == 0 else (send, keep)
                first[:, 0:width] = grad_query
                first[:, width:D] = grad_key
                first[:, D:] = jnp.zeros_like(grad_value)
                second[:, 0:D] = projected
                second[:, D:] = grad_value

    else:
        outs[4][...] = projected
    grad_normed = None
    for index, low in enumerate((grad_query, grad_key, grad_value)):
        if not split:
            outs[5][index] = low
        term = mm_t(low, qkv_weight[index])
        grad_normed = term if grad_normed is None else grad_normed + term
    if len(ins) > 15:
        grad_normed_out[0] = grad_normed.astype(BF16)
        grad_normed_out[1] = ins[15][...]
    else:
        grad_normed_out[...] = grad_normed.astype(BF16)


def last_body(scalars, ins, outs, scratch):
    (
        mine,
        other,
        residual,
        gain,
        grad_middle,
        to_frame,
        tokens,
        position_kernel,
        to_token,
        middle,
        mlp_mine,
        down_bias,
    ) = ins[:12]
    block_out, token_grad, sums_out = outs
    grid_grad, grid_in, grid_back, sums = scratch
    unit, inverse = norm_parts(residual[...])
    grad = mine[...].astype(F32) + other[0].astype(F32)
    grad_residual = grad_middle[...] + norm_back(grad, unit, inverse, gain[...])
    grid_grad[...] = mm(to_frame[...], grad_residual.astype(BF16)).reshape(CELLS, SLOTS, D)
    grid_in[...] = mm(to_frame[...], tokens[...]).reshape(CELLS, SLOTS, D)
    taps = position_kernel.ref()
    block_out[...] = (
        middle[...] + (mlp_mine[...].astype(F32) + other[1].astype(F32)) + down_bias[...]
    )
    block_out.send()

    def convolve(lanes):
        frame_conv(
            grid_grad, lambda a, b: taps[2 - a, 2 - b : 3 - b, lanes], grid_back, 3, lanes
        )
        frame_taps(grid_grad, grid_in, sums, 3, lanes)

    over_lanes(D, convolve)
    framed = grid_back[...].reshape(ROWS, D).astype(BF16)
    token_grad[...] = grad_residual + mm(to_token[...], framed)
    token_grad.send()
    sums[9:10] = column_sum(grad_residual)
    sums[10:11] = column_sum(grad * unit)
    sums[11:12] = column_sum(grad)
    if len(ins) > 12:
        first, second = ins[12:]
        width = first.shape[1]
        sums[12:62, 0:width] = first[0:50] + second[0:50]
        sums[12:62, width:] = jnp.zeros((50, D - width), F32)
        sums[62:64] = jnp.zeros((2, D), F32)
    else:
        sums[12:16] = jnp.zeros((4, D), F32)
    sums_out[...] = sums[...].astype(sums_out.held.dtype)


def turn(values, distance, axis="dp"):
    size = lax.axis_size(axis)
    return lax.ppermute(values, axis, [(i, i ^ distance) for i in range(size)])


def step_bits():
    bits = list(range(1, lax.axis_size("dp").bit_length() - 1))
    return bits, bits[1::-1] + bits[2:]


def step_turn(values, step):
    orders = step_bits()
    size = lax.axis_size("dp")
    return lax.ppermute(values, "dp", [(i, i ^ (1 << orders[i & 1][step])) for i in range(size)])


def step_side(step):
    first, second = step_bits()
    me = lax.axis_index("dp")
    return (me >> jnp.where(me & 1 == 0, first[step], second[step])) & 1


def rows_of(side, count):
    return pl.ds(pl.multiple_of(side * count, 16), count)


def mlp_grads_body(scalars, ins, outs, scratch):
    hidden_width = ins[0].shape[1] - D
    core, side = lax.axis_index("dp") & 1, step_side(0)
    for which in range(2):

        @pl.when(core == which)
        def _():
            for target, place in ((outs[1], 1 - side), (outs[0], side)):
                columns = pl.ds(pl.multiple_of(place * D, 128), D)
                total = None
                for one in ins:
                    wide, narrow = one[:, columns], one[:, hidden_width:]
                    term = t_mm(narrow, wide) if which == 0 else t_mm(wide, narrow)
                    total = term if total is None else total + term
                target[...] = total.astype(BF16)


def attention_grads_body(images, scalars, ins, outs, scratch):
    stay, go = outs
    normed, attended = ins[:images], ins[images : 2 * images]
    far_early = ins[2 * images : 3 * images]
    late = ins[3 * images :]
    normed = [*normed, *far_early]
    width = D // 2

    def attended_of(place):
        return attended[place][...] if place < images else far_early[place - images][:, D:]

    def total(term):
        out = None
        for place in range(2 * images):
            out = term(place) if out is None else out + term(place)
        return out.astype(BF16)

    core, side = lax.axis_index("dp") & 1, step_side(0)

    @pl.when(core == 0)
    def _():
        for target, half in ((go, 1 - side), (stay, side)):
            columns = pl.ds(pl.multiple_of(half * width, 128), width)
            target[...] = total(lambda place: t_mm(normed[place][:, columns], late[place][:, 0:D]))

    for which in range(2):

        @pl.when((core == 1) & (side == which))
        def _():
            first, second = (stay, go) if which == 0 else (go, stay)
            first[...] = total(lambda place: t_mm(attended_of(place), late[place][:, 0:D]))
            for index in range(2):
                columns = slice(index * width, (index + 1) * width)
                second[:, columns] = total(
                    lambda place: t_mm(normed[place][:, columns], late[place][:, D:])
                )


def halve_body(step, scalars, ins, outs, scratch):
    here, came = ins
    here.ref()
    came.ref()
    if len(outs) == 1:
        outs[0][...] = (here[...].astype(F32) + came[...].astype(F32)).astype(BF16)
        return
    stay, go = outs
    count = stay.shape[0]
    side = step_side(step)
    for target, place in ((go, 1 - side), (stay, side)):
        rows = rows_of(place, count)
        target[...] = (here[rows, :].astype(F32) + came[rows, :].astype(F32)).astype(BF16)
        target.send()


def join_body(step, extra, scalars, ins, outs, scratch):
    here, came = ins
    side = step_side(step)
    count = here.shape[0] - extra
    outs[0].held[rows_of(side, count), :] = here[0:count, :]
    outs[0].held[rows_of(1 - side, count), :] = came[0:count, :]
    if extra:
        total = here[count:, :].astype(F32) + came[count:, :].astype(F32)
        outs[0][2 * count :, :] = total.astype(BF16)


def pack_body(scalars, ins, outs, scratch):
    here, came, mine, far, wide_one, wide_two, bias_one, bias_two, head_one, head_two = ins
    (rows,) = scratch
    count = here.shape[0]
    outs[0][0:count, :] = (here[...].astype(F32) + came[...].astype(F32)).astype(BF16)
    own, others = mine[...].astype(F32), far[...].astype(F32)
    width = D // 2
    first = own[0:12] + others[0:12]
    member = lax.axis_index("mp")
    low = jnp.where(member == 0, own[:, 0:width], others[:, 0:width])
    high = jnp.where(member == 0, others[:, 0:width], own[:, 0:width])
    rows[0:50, 0:width] = low[12:62]
    rows[0:50, width:] = high[12:62]
    for index, place in enumerate(FREE):
        row, part = index // 2, slice(index % 2 * width, index % 2 * width + width)
        rows[place : place + 1, 0:width] = first[row : row + 1, part]
    rows[50:54] = wide_one[0:4] + wide_two[0:4]
    bias = bias_one[...] + bias_two[...]
    rows[54:55] = bias[:, 0:D]
    rows[55:56] = bias[:, D:]
    rows[56:57, 0:width] = head_one[50:51] + head_two[50:51]
    rows[56:57, width:] = head_one[51:52] + head_two[51:52]
    rows[57:SMALL] = jnp.zeros((SMALL - 57, D), F32)
    outs[0][count:, :] = rows[...].astype(BF16)


def mlp_final_body(scalars, ins, outs, scratch):
    mine, other = ins
    grad_up, grad_down, finished = outs
    finished[...] = jnp.zeros((8, 128), F32)
    mine.ref()
    other.ref()
    core = lax.axis_index("dp") & 1
    for side in range(2):

        @pl.when(core == side)
        def _():
            up, down = (mine, other) if side == 0 else (other, mine)
            for tile in range(down.shape[0] // D):
                rows = slice(tile * D, (tile + 1) * D)
                grad_up[:, rows] = up[rows, :].astype(F32)
            grad_down[...] = down[...].astype(F32)


def attention_final_body(scalars, ins, outs, scratch):
    mine, other = ins
    grad_qkv, grad_out, position, up_bias, pair_bias, three, five, seven = outs[:8]
    vectors = outs[8:]
    (small,) = scratch
    width = D // 2
    core = lax.axis_index("dp") & 1
    small[...] = mine[D:, :].astype(F32) + other[D:, :].astype(F32)
    for index, place in enumerate(FREE):
        row, part = index // 2, slice(index % 2 * width, index % 2 * width + width)
        if row < 9:
            position[row // 3, row % 3 : row % 3 + 1, part] = small[place : place + 1, 0:width]
        else:
            vectors[row - 9][:, part] = small[place : place + 1, 0:width]
    position.send()
    for place, vector in zip((49, 50, 51, 52, 53), vectors[3:]):
        vector[...] = small[place : place + 1]
    for vector in vectors:
        vector.send()
    up_bias[:, 0:D] = small[54:55]
    up_bias[:, D:] = small[55:56]
    up_bias.send()
    pair_bias[0:1] = small[56:57, 0:width]
    pair_bias[1:2] = small[56:57, width:]
    pair_bias.send()
    for row in range(3):
        begin = EDGE * (row + 2) + 2
        three[row] = small[begin : begin + 3, 0:128]
    three.send()
    for row in range(5):
        begin = EDGE * (row + 1) + 1
        five[row] = small[begin : begin + 5, 128:320]
    five.send()
    for row in range(EDGE):
        begin = EDGE * row
        seven[row] = pltpu.roll(small[begin : begin + EDGE, 256:512], 192, 1)[:, 0:192]
    seven.send()
    for side in range(2):

        @pl.when(core == side)
        def _():
            first, second = (mine, other) if side == 0 else (other, mine)
            for index in range(2):
                columns = slice(index * width, (index + 1) * width)
                grad_qkv[index] = first[0:D, columns].astype(F32)
                grad_qkv[2, columns, :] = second[width:D, columns].astype(F32)
            grad_out[...] = second[0:width, :].astype(F32)


def halve(keep, came, step, after=(), us=0.0):
    outs = [((keep.shape[0] // 2, D), BF16)] * 2
    body = functools.partial(halve_body, step)
    keep, send = call(body, outs, (keep, came), us=us, after=after)
    return keep, step_turn(send, step)


def join(keep, came, step, extra=0, after=(), us=0.0):
    outs = [(((keep.shape[0] - extra) * 2 + extra, D), BF16)]
    body = functools.partial(join_body, step, extra)
    return call(body, outs, (keep, came), us=us, after=after)[0]


def sum_small(values):
    size = lax.axis_size("dp")
    if size & (size - 1):
        return lax.psum(values, "dp")
    for bit in range(size.bit_length() - 1):
        values = values + turn(values, 1 << bit)
    return values


def whole_body(products, scalars, ins, outs, scratch):
    for target, pairs in zip(outs, products):
        total = None
        for left, right in pairs:
            one, two = (ins[i][...] if part is None else ins[i][part] for i, part in (left, right))
            term = t_mm(one, two)
            total = term if total is None else total + term
        target[...] = total.astype(BF16)


def per_device(
    tokens,
    out_grad,
    crop_image,
    crop_res,
    position_kernel,
    position_bias,
    gain_one,
    shift_one,
    qkv_weight,
    query_value_bias,
    relative_three,
    relative_five,
    relative_seven,
    relative_bias,
    output_weight,
    output_bias,
    gain_two,
    shift_two,
    up_weight,
    up_bias,
    down_weight,
    down_bias,
):
    group = lax.axis_size("mp")
    member = lax.axis_index("mp")
    rows = tokens.shape[0]
    width = qkv_weight.shape[2]
    hidden_width = up_weight.shape[1]
    pair = group == 2
    size = lax.axis_size("dp")
    blocks = (
        pair
        and size >= 4
        and size & (size - 1) == 0
        and 2 * width == D
        and hidden_width == 2 * D
        and D % (size * 8) == 0
    )

    def row(vector):
        return vector.reshape(1, -1)

    if not blocks:
        full_kernel = jnp.concatenate(
            [
                jnp.pad(relative_three, ((2, 2), (2, 2), (0, 0))),
                jnp.pad(relative_five, ((1, 1), (1, 1), (0, 0))),
                relative_seven,
            ],
            axis=2,
        )
        kernel_part = lax.dynamic_slice_in_dim(full_kernel, member * width, width, 2)
        bias_part = row(lax.dynamic_slice_in_dim(relative_bias, member * width, width, 0))
    else:
        kernel_part, bias_part = None, row(relative_bias)
    qkv_planes = jnp.transpose(qkv_weight, (1, 0, 2))

    if pair:
        token_list = [tokens, turn(tokens, 1, "mp")]
        images = [lambda: lax.axis_index("mp"), lambda: 1 - lax.axis_index("mp")]
    else:
        token_list = list(lax.all_gather(tokens, "mp", axis=0))
        grad_list = list(lax.all_gather(out_grad, "mp", axis=0))
        images = [functools.partial(int, j) for j in range(group)]

    def own(parts):
        if pair:
            return parts[0]
        return lax.dynamic_index_in_dim(jnp.stack(parts), member, 0, keepdims=False)

    fronts = []
    for index, (image, one) in enumerate(zip(images, token_list)):
        table = blocks and index == 0
        outs = [
            Far((ROWS, rows), BF16),
            Far((rows, ROWS), BF16),
            ((rows, D), F32),
            Far((rows, D), BF16),
            Far((rows, width), F32),
            Far((rows, width), BF16),
            Far((rows, width), F32),
            Far((width, width), BF16),
            Far((rows, width), F32),
            Far((rows, width), BF16),
            ((rows, D), BF16),
        ]
        if blocks:
            outs.append(((rows, D + width), BF16))
        args = [
            crop_res,
            Far(one) if index == 0 else one,
            Far(position_kernel),
            Far(row(position_bias)),
            Far(row(gain_one)),
            Far(row(shift_one)),
            Far(qkv_planes),
            Far(query_value_bias),
        ]
        if table:
            outs += [Far((EDGE, EDGE, width), F32), Far((rows, D), F32)]
            args += [Far(relative_three), Far(relative_five), Far(relative_seven)]
        else:
            args.append(Far(kernel_part))
        args += [Far(bias_part), Far(output_weight)]
        scratch = [pltpu.VMEM((CELLS, SLOTS, D), F32)] * 2
        body = functools.partial(front_body, image, table, blocks)
        if index:
            args = [one.what[0] if isinstance(one, Far) and one.what[0] is not kernel_part else one for one in args]
        made = call(body, outs, args, scratch, us=50.0 if index == 0 else 5.0, smem=1)
        if table:
            kernel_part, kept_residual = made[12:14]
        fronts.append(made[: 12 if blocks else 11])
    to_frame, to_token, residual, normed, query, value, weight, context = tuple(zip(*fronts))[:8]
    relative, attended, partial, *early = tuple(zip(*fronts))[8:]

    if pair:
        args = (partial[0], out_grad)
        (both,) = call(pair_body, [((2, rows, D), BF16)], args, us=0.3, after=[token_list[1]])
        first, second = turn(both, 1, "mp"), turn(partial[1], 1, "mp")
        grad_list, grad_parts = [out_grad, first], [None, 1]
        addends = [(partial[0], second), (partial[1], first)]
        places = [(None, None), (None, 0)]
        order = (1, 0)
    else:
        total = lax.psum(jnp.stack(partial), "mp")
        grad_parts = [None] * group
        addends = [(one, jnp.zeros_like(one)) for one in total]
        places = [(None, None)] * group
        order = range(group)
    mlps = [None] * group
    for index in order:
        outs = [Far((rows, D), F32), ((rows, D), BF16), Far((rows, D), BF16)]
        outs.append(Far((1, hidden_width), F32))
        scratch = []
        if blocks:
            outs += [((rows, hidden_width + D), BF16)] * 2
            scratch = [pltpu.VMEM((rows, hidden_width), BF16)] * 2
        else:
            outs += [((rows, hidden_width), BF16)] * 2 + [((rows, D), BF16)]
        args = (
            residual[index],
            *addends[index],
            grad_list[index],
            row(output_bias),
            row(gain_two),
            row(shift_two),
            up_weight,
            row(up_bias.astype(F32)),
            down_weight,
        )
        body = functools.partial(mlp_body, (*places[index], grad_parts[index]), blocks)
        after = [mlps[1][1]] if pair and index == 0 else []
        mlps[index] = call(body, outs, args, scratch, us=2.5, after=after)
    middle, grad_two_part, mlp_part, grad_up_bias, *mlp_rows = zip(*mlps)

    if pair:
        back_addends = [
            (grad_two_part[0], turn(grad_two_part[1], 1, "mp")),
            (grad_two_part[1], turn(grad_two_part[0], 1, "mp")),
        ]
    else:
        total = lax.psum(jnp.stack(grad_two_part), "mp")
        back_addends = [(one, jnp.zeros_like(one)) for one in total]

    steps = len(step_bits()[0])
    if blocks:
        args = (*mlp_rows[0], *(turn(one, 1) for one in mlp_rows[1]))
        after = [mark(back_addends[0][1], 46.0)]
        mlp_keep, mlp_send = call(mlp_grads_body, [((D, D), BF16)] * 2, args, us=2.0, after=after)
        mlp_came = step_turn(mlp_send, 0)

    backs = []
    for index in range(group):
        carry = pair and index == 1
        outs = [
            Far((rows, D), F32),
            ((2, rows, D) if carry else (rows, D), BF16),
            Far((8, D), F32),
            Far((56, width), F32),
        ]
        if blocks:
            outs += [((rows, D + width), BF16)] * 2
        else:
            outs += [((rows, D), BF16), ((3, rows, width), BF16)]
        args = [
            *back_addends[index],
            grad_list[index],
            middle[index],
            row(gain_two),
            output_weight,
            query[index],
            to_frame[index],
            value[index],
            kernel_part,
            context[index],
            relative[index],
            weight[index],
            to_token[index],
            qkv_planes,
        ]
        if carry:
            args.append(mlp_part[1])
        scratch = [pltpu.VMEM((CELLS, SLOTS, width), F32)] * 3
        body = functools.partial(back_body, (None, None, grad_parts[index]), blocks)
        after = [mlp_keep] if blocks else []
        if pair and index:
            after.append(backs[0][1])
        backs.append(call(body, outs, args, scratch, us=25.0 if index else 0.0, after=after))
    grad_middle, grad_one_part, wide_sums, head_sums, *late = zip(*backs)

    if blocks:
        mlp_keep, mlp_came = halve(mlp_keep, mlp_came, 1, after=[backs[1][1]], us=WEIGHTS["h1"])
        outs = [((width, D), BF16)] * 2
        args = (*normed, *attended, *(turn(one, 1) for one in early[0]))
        args += (*late[0], *(turn(one, 1) for one in late[1]))
        body = functools.partial(attention_grads_body, group)
        keep, send = call(body, outs, args, us=2.0, after=[mlp_keep])
        came = step_turn(send, 0)
    if not blocks:
        hidden, grad_pre, normed_two = mlp_rows
        grad_projected, grad_qkv = late
        args = (*normed_two, *grad_pre, *hidden, *grad_list)
        args += (*normed, *grad_qkv, *attended, *grad_projected)

        def spot(kind, image, part=None):
            return kind * group + image, part

        each = range(group)
        products = [
            [(spot(0, j), spot(1, j)) for j in each],
            [(spot(2, j), spot(3, j, grad_parts[j])) for j in each],
        ]
        products += [[(spot(4, j), spot(5, j, plane)) for j in each] for plane in range(3)]
        products += [[(spot(6, j), spot(7, j)) for j in each]]
        outs = [((D, hidden_width), BF16), ((hidden_width, D), BF16)]
        outs += [((D, width), BF16)] * 3 + [((width, D), BF16)]
        wholes = call(functools.partial(whole_body, products), outs, args, us=6.0, vmem=40)
        grad_up, grad_down, *planes, grad_out = (lax.psum(one, "dp").astype(F32) for one in wholes)
        grad_qkv_planes = jnp.stack(planes)

    if pair:
        mine, mlp_mine = grad_one_part[0], mlp_part[0]
        other = turn(grad_one_part[1], 1, "mp")
    else:
        sums = [jnp.stack(grad_one_part), jnp.stack(mlp_part)]
        mine, mlp_mine = (lax.psum_scatter(one, "mp", scatter_dimension=0) for one in sums)
        other = jnp.zeros((2, rows, D), BF16)
    outs = [Far((rows, D), F32), Far((rows, D), F32)]
    outs.append(((64, D), BF16) if blocks else ((16, D), F32))
    args = [
        mine,
        other,
        kept_residual if blocks else own(residual),
        row(gain_one),
        own(grad_middle),
        own(to_frame),
        tokens,
        position_kernel,
        own(to_token),
        own(middle),
        mlp_mine,
        row(down_bias),
    ]
    if blocks:
        args += [*head_sums]
    scratch = [pltpu.VMEM((CELLS, SLOTS, D), F32)] * 3
    scratch.append(pltpu.VMEM((64 if blocks else 16, D), F32))
    after = []
    if blocks:
        for step in range(2, steps):
            us = WEIGHTS["h2"]
            mlp_keep, mlp_came = halve(mlp_keep, mlp_came, step, after=[keep], us=us)
        keep, came = halve(keep, came, 1, after=[mlp_keep], us=WEIGHTS["p1"])
        after = [keep]
    block_out, token_grad, own_sums = call(
        last_body, outs, args, scratch, us=WEIGHTS["last"], after=after
    )

    if blocks:
        far_sums = turn(own_sums, 1, "mp")
        mark_last = own_sums
        for step in range(2, steps):
            keep, came = halve(keep, came, step, after=[mark_last], us=WEIGHTS["p2"])
            mark_last = keep
        outs = [(mlp_keep.shape, BF16)]
        body = functools.partial(halve_body, None)
        args = (mlp_keep, mlp_came)
        (mlp_keep,) = call(body, outs, args, us=WEIGHTS["total"], after=[mark_last])
        mlp_came = step_turn(mlp_keep, steps - 1)
        args = (keep, came, own_sums, far_sums)
        args += (*wide_sums, *grad_up_bias, *head_sums)
        outs = [((keep.shape[0] + SMALL, D), BF16)]
        scratch = [pltpu.VMEM((SMALL, D), F32)]
        (keep,) = call(pack_body, outs, args, scratch, us=WEIGHTS["pack"], after=[mlp_keep])
        for step in reversed(range(steps)):
            came = step_turn(keep, step)
            us = WEIGHTS.get(f"j{step}", 0.0)
            mlp_keep = join(mlp_keep, mlp_came, step, after=[keep], us=us)
            mlp_came = step_turn(mlp_keep, step - 1) if step else turn(mlp_keep, 1)
            us = WEIGHTS.get(f"a{step}", 0.0)
            keep = join(keep, came, step, SMALL, after=[mlp_keep], us=us)
        came = turn(keep, 1)
        outs = [Far((D, hidden_width), F32), Far((hidden_width, D), F32), ((8, 128), F32)]
        args = (mlp_keep, mlp_came)
        grad_up, grad_down, finished = call(mlp_final_body, outs, args, us=2.0, after=[keep])
        shapes = [(3, D, width), (width, D), (3, 3, D), (1, hidden_width), (2, width)]
        shapes += [relative_three.shape, relative_five.shape, relative_seven.shape]
        outs = [Far(shape, F32) for shape in shapes + [(1, D)] * 8]
        scratch = [pltpu.VMEM((SMALL, D), F32)]
        made = call(attention_final_body, outs, (keep, came), scratch, us=2.0, after=[finished])
        grad_qkv_planes, grad_out, position, up_sum, pair_sum, three, five, seven = made[:8]
        vectors = [one.reshape(D) for one in made[8:]]
        return (
            block_out,
            token_grad,
            position,
            *vectors[0:3],
            jnp.transpose(grad_qkv_planes, (1, 0, 2)),
            pair_sum,
            three,
            five,
            seven,
            vectors[3],
            grad_out,
            *vectors[4:7],
            grad_up,
            up_sum.reshape(hidden_width),
            grad_down,
            vectors[7],
        )

    head_total = functools.reduce(jnp.add, head_sums)
    wide_total = functools.reduce(jnp.add, wide_sums)
    own_total = lax.psum(own_sums[:12], "mp")
    relative_total = lax.all_gather(head_total[:50], "mp", axis=1, tiled=True)
    bias_total = functools.reduce(jnp.add, grad_up_bias)
    pieces = [own_total, wide_total[:4], relative_total]
    private = jnp.concatenate([bias_total.reshape(-1), head_total[50:52].reshape(-1)])
    pieces.append(jnp.pad(private, (0, -private.shape[0] % D)).reshape(-1, D))
    total = sum_small(jnp.concatenate(pieces, axis=0))
    kernel_grad = total[16:65].reshape(EDGE, EDGE, D)
    tail = total[66:].reshape(-1)
    return (
        block_out,
        token_grad,
        total[:9].reshape(3, 3, D),
        total[9],
        total[10],
        total[11],
        jnp.transpose(grad_qkv_planes, (1, 0, 2)),
        tail[hidden_width : hidden_width + 2 * width].reshape(2, width),
        kernel_grad[2:5, 2:5, : 2 * HEAD],
        kernel_grad[1:6, 1:6, 2 * HEAD : 5 * HEAD],
        kernel_grad[:, :, 5 * HEAD :],
        total[65],
        grad_out,
        total[12],
        total[13],
        total[14],
        grad_up,
        tail[:hidden_width],
        grad_down,
        total[15],
    )


def solution(mesh):
    in_specs = (
        P(("dp", "mp"), None),
        P(("dp", "mp"), None),
        P("dp"),
        P("dp"),
        P(),
        P(),
        P(),
        P(),
        P(None, None, "mp"),
        P(None, "mp"),
        P(),
        P(),
        P(),
        P(),
        P("mp", None),
        P(),
        P(),
        P(),
        P(None, "mp"),
        P("mp"),
        P("mp", None),
        P(),
    )
    out_specs = (
        P(("dp", "mp"), None),
        P(("dp", "mp"), None),
        P(),
        P(),
        P(),
        P(),
        P(None, None, "mp"),
        P(None, "mp"),
        P(),
        P(),
        P(),
        P(),
        P("mp", None),
        P(),
        P(),
        P(),
        P(None, "mp"),
        P("mp"),
        P("mp", None),
        P(),
    )
    return jax.shard_map(
        per_device, mesh=mesh, in_specs=in_specs, out_specs=out_specs, check_vma=False
    )
```

```python
import functools
import math

import jax
import jax.numpy as jnp
from jax import lax
from jax.experimental import pallas as pl
from jax.experimental.pallas import tpu as pltpu
from jax.sharding import PartitionSpec as P

HEAD = 64
D = 512
EPSILON = 1e-06
SLOTS = 8
EDGE = 7
CELLS = EDGE * EDGE
ROWS = CELLS * SLOTS
SCALE = HEAD ** (-0.5)
SMALL = 64
EXTRA = 16
HELD = 60.0
ARRIVED = 46.0
WEIGHTS = dict(
    h1=0.0, h2=0.0, p1=40.0, last=0.0, p2=0.0, total=0.0, pack=40.0, j2=0.0, a2=0.0, j1=0.0, a1=40.0, j0=0.0, a0=40.0
)
BF16 = jnp.bfloat16
F32 = jnp.float32


def mm(left, right):
    return jnp.dot(left, right, preferred_element_type=F32)


def mm_t(left, right):
    return lax.dot_general(left, right, (((1,), (1,)), ((), ())), preferred_element_type=F32)


def t_mm(left, right):
    return lax.dot_general(left, right, (((0,), (0,)), ((), ())), preferred_element_type=F32)


def split_mm(onehot, values):
    high = values.astype(BF16)
    low = (values - high.astype(F32)).astype(BF16)
    return mm(onehot, high) + mm(onehot, low)


class Source:
    def __init__(self, ref, copy=None):
        self.held, self.copy, self.shape = ref, copy, ref.shape

    def ref(self):
        if self.copy is not None:
            self.copy.wait()
            self.copy = None
        return self.held

    def __getitem__(self, index):
        return self.ref()[index]


class Result:
    def __init__(self, ref, copy=None):
        self.held, self.copy, self.sent, self.shape = ref, copy, copy is None, ref.shape

    def __setitem__(self, index, value):
        self.held[index] = value

    def __getitem__(self, index):
        return self.held[index]

    def send(self):
        if not self.sent:
            self.copy.start()
            self.sent = True


class Far:
    def __init__(self, *what):
        self.what = what


def call(body, outs, args, scratch=(), us=3.0, smem=0, vmem=24, after=(), bring=(), fill=()):
    far_in = [isinstance(one, Far) for one in args[smem:]]
    far_out = [isinstance(one, Far) for one in outs]
    arrays = [one.what[0] if isinstance(one, Far) else one for one in args[smem:]]
    outs = [one.what if isinstance(one, Far) else one for one in outs]
    filled_in = [one for one in fill if not isinstance(one, jax.ShapeDtypeStruct)]

    def kernel(*refs):
        refs = list(refs)

        def take(count):
            taken = refs[:count]
            del refs[:count]
            return taken

        far_scalars, given = take(smem), take(len(arrays))
        distant, _ = take(len(bring)), take(len(after) + len(filled_in))
        places, brought, filled = take(len(outs)), take(len(bring)), take(len(fill))
        near_scalars = take(smem)
        scalar_sems = take(1)[0] if smem else None
        near_in, near_out = take(sum(far_in)), take(sum(far_out))
        scalars = []
        for index, (away, near) in enumerate(zip(far_scalars, near_scalars)):
            copy = pltpu.make_async_copy(away, near, scalar_sems.at[index])
            copy.start()
            scalars.append(Source(near, copy))
        in_sems = take(1)[0] if any(far_in) else None
        out_sems = take(1)[0] if any(far_out) else None
        bring_sems = take(1)[0] if bring else None
        ins, made, moves = [], [], []
        for ref, far in zip(given, far_in):
            if far:
                index = sum(one.copy is not None for one in ins)
                copy = pltpu.make_async_copy(ref, near_in[index], in_sems.at[index])
                copy.start()
                ins.append(Source(near_in[index], copy))
            else:
                ins.append(Source(ref))
        for index, (source, target) in enumerate(zip(distant, brought)):
            moves.append(pltpu.make_async_copy(source, target, bring_sems.at[index]))
            moves[-1].start()
        for ref, far in zip(places, far_out):
            if far:
                index = sum(one.copy is not None for one in made)
                copy = pltpu.make_async_copy(near_out[index], ref, out_sems.at[index])
                made.append(Result(near_out[index], copy))
            else:
                made.append(Result(ref))
        body(scalars, ins, made, filled + refs)
        for one in made:
            one.send()
        for one in scalars + ins:
            one.ref()
        for one in made:
            if one.copy is not None:
                one.copy.wait()
        for copy in moves:
            copy.wait()

    shapes = [pltpu.SMEM(one.shape, one.dtype) for one in args[:smem]]
    if smem:
        shapes.append(pltpu.SemaphoreType.DMA((smem,)))
    shapes += [pltpu.VMEM(one.shape, one.dtype) for one, far in zip(arrays, far_in) if far]
    shapes += [pltpu.VMEM(*one) for one, far in zip(outs, far_out) if far]
    if any(far_in):
        shapes.append(pltpu.SemaphoreType.DMA((sum(far_in),)))
    if any(far_out):
        shapes.append(pltpu.SemaphoreType.DMA((sum(far_out),)))
    if bring:
        shapes.append(pltpu.SemaphoreType.DMA((len(bring),)))
    near, far = pl.BlockSpec(memory_space=pltpu.VMEM), pl.BlockSpec(memory_space=pltpu.HBM)
    operands = [
        pltpu.with_memory_space_constraint(one, pltpu.HBM) if away else one
        for one, away in zip(arrays, far_in)
    ]
    brought_far = [pltpu.with_memory_space_constraint(one, pltpu.HBM) for one in bring]
    scalars_far = [pltpu.with_memory_space_constraint(one, pltpu.HBM) for one in args[:smem]]
    return pl.pallas_call(
        kernel,
        out_shape=[
            pltpu.HBM(*one) if away else jax.ShapeDtypeStruct(*one)
            for one, away in zip(outs, far_out)
        ]
        + [jax.ShapeDtypeStruct(one.shape, one.dtype) for one in bring]
        + [pltpu.HBM(one.shape, one.dtype) for one in fill],
        in_specs=[far] * smem
        + [far if away else near for away in far_in]
        + [far] * len(bring)
        + [pl.BlockSpec(memory_space=pl.ANY)] * len(after)
        + [far] * len(filled_in),
        out_specs=[far if away else near for away in far_out]
        + [near] * len(bring)
        + [far] * len(fill),
        input_output_aliases={
            len(args) + len(bring) + len(after) + index: len(outs) + len(bring) + index
            for index in range(len(filled_in))
        },
        scratch_shapes=shapes + list(scratch),
        compiler_params=pltpu.CompilerParams(vmem_limit_bytes=vmem << 20),
        cost_estimate=pl.CostEstimate(
            flops=int(us * 1.0e8), bytes_accessed=1 << 12, transcendentals=0
        ),
    )(*scalars_far, *operands, *brought_far, *after, *filled_in)


def over_lanes(width, body):
    if width % 128 == 0:

        @pl.loop(0, width // 128)
        def _(step):
            body(pl.ds(pl.multiple_of(step * 128, 128), 128))

    else:
        body(slice(0, width))


def frame_conv(source, tap, target, edge, lanes):
    half = (edge - 1) // 2
    for i in range(EDGE):
        total = [None] * EDGE
        for a in range(edge):
            row = i + a - half
            if not 0 <= row < EDGE:
                continue
            cells = [source[row * EDGE + j, :, lanes] for j in range(EDGE)]
            for b in range(edge):
                weight = tap(a, b)
                for j in range(EDGE):
                    column = j + b - half
                    if 0 <= column < EDGE:
                        term = cells[column] * weight
                        total[j] = term if total[j] is None else total[j] + term
        for j in range(EDGE):
            target[i * EDGE + j, :, lanes] = total[j]


def frame_taps(grad, source, target, edge, lanes):
    half = (edge - 1) // 2
    for a in range(edge):
        total = [None] * edge
        for i in range(EDGE):
            row = i + a - half
            if not 0 <= row < EDGE:
                continue
            cells = [source[row * EDGE + j, :, lanes] for j in range(EDGE)]
            for j in range(EDGE):
                own = grad[i * EDGE + j, :, lanes]
                for b in range(edge):
                    column = j + b - half
                    if 0 <= column < EDGE:
                        term = own * cells[column]
                        total[b] = term if total[b] is None else total[b] + term
        for b in range(edge):
            row = a * edge + b
            target[row : row + 1, lanes] = jnp.sum(total[b], axis=0, keepdims=True)


def crop_frames(kinds, base, rows):
    sub = lax.broadcasted_iota(jnp.int32, (SLOTS, rows), 0)
    lane = lax.broadcasted_iota(jnp.int32, (SLOTS, rows), 1)
    place = lax.broadcasted_iota(jnp.int32, (8, ROWS), 1)
    slot = place & (SLOTS - 1)
    cell = place >> 3
    down = (cell * 37) >> 8
    across = cell - down * EDGE
    begin = jnp.zeros((SLOTS, rows), jnp.int32)
    whole = jnp.zeros((SLOTS, rows), jnp.int32)
    begin_row = jnp.zeros((8, ROWS), jnp.int32)
    whole_row = jnp.zeros((8, ROWS), jnp.int32)
    start = jnp.int32(0)
    for s in range(SLOTS):
        large = (kinds[base + s] == 0).astype(jnp.int32)
        begin = jnp.where(sub == s, start, begin)
        whole = jnp.where(sub == s, large, whole)
        begin_row = jnp.where(slot == s, start, begin_row)
        whole_row = jnp.where(slot == s, large, whole_row)
        start = start + 9 + 40 * large
    tiles = []
    for i in range(EDGE):
        for j in range(EDGE):
            small = begin + (i * 3 + j) if i < 3 and j < 3 else jnp.full_like(begin, -1)
            token = jnp.where(whole == 1, begin + (i * EDGE + j), small)
            tiles.append(jnp.where(token == lane, 1.0, 0.0))
    to_frame = jnp.concatenate(tiles, axis=0).astype(BF16)
    corner = jnp.where((down < 3) & (across < 3), begin_row + down * 3 + across, -1)
    token_row = jnp.where(whole_row == 1, begin_row + cell, corner)
    height = lax.broadcasted_iota(jnp.int32, (rows, ROWS), 0)
    to_token = jnp.where(height == token_row[0:1], 1.0, 0.0).astype(BF16)
    return to_frame, to_token


def norm_parts(values):
    average = jnp.mean(values, axis=-1, keepdims=True)
    centred = values - average
    variance = jnp.mean(centred * centred, axis=-1, keepdims=True)
    inverse = lax.rsqrt(variance + EPSILON)
    return centred * inverse, inverse


def norm_back(grad, unit, inverse, gain):
    scaled = grad * gain
    first = jnp.mean(scaled, axis=-1, keepdims=True)
    second = jnp.mean(scaled * unit, axis=-1, keepdims=True)
    return (scaled - first - unit * second) * inverse


def column_sum(values):
    return jnp.sum(values, axis=0, keepdims=True)


def same_head(width):
    rows = lax.broadcasted_iota(jnp.int32, (width, width), 0) // HEAD
    columns = lax.broadcasted_iota(jnp.int32, (width, width), 1) // HEAD
    return rows == columns


def tap_table(member, three, five, seven, table):
    table[...] = jnp.zeros(table.shape, F32)

    @pl.when(member == 0)
    def _():
        table[2:5, 2:5, 0:128] = three[...]
        for row in range(5):
            table[1 + row, 1:6, 128:256] = five[row, :, 0:128]

    @pl.when(member == 1)
    def _():
        for row in range(5):
            table[1 + row, 1:6, 0:64] = five[row, :, 128:192]
        lane = lax.broadcasted_iota(jnp.int32, (EDGE, 128), 1)
        for row in range(EDGE):
            near = pltpu.roll(seven[row, :, 0:128], 64, 1)
            wide = jnp.concatenate([seven[row, :, 128:192], jnp.zeros((EDGE, 64), F32)], axis=1)
            far = pltpu.roll(wide, 64, 1)
            table[row, :, 0:128] = jnp.where(lane < 64, table[row, :, 0:128], near)
            table[row, :, 128:256] = jnp.where(lane < 64, near, far)


def front_body(image, table, early, scalars, ins, outs, scratch):
    (kinds,) = scalars
    tokens, position_kernel, position_bias, gain, shift, qkv_weight, pair_bias = ins[:7]
    relative_bias, output_weight = ins[-2:]
    (
        to_frame_out,
        to_token_out,
        residual_out,
        normed_out,
        query_out,
        value_out,
        weight_out,
        context_out,
        relative_out,
        attended_out,
        partial_out,
    ) = outs[:11]
    grid_in, grid_out = scratch
    rows = tokens.shape[0]
    width = output_weight.shape[0]
    member = lax.axis_index("mp")
    to_frame, to_token = crop_frames(kinds, image() * SLOTS, rows)
    to_frame_out[...] = to_frame
    to_frame_out.send()
    to_token_out[...] = to_token
    to_token_out.send()
    grid_in[...] = mm(to_frame, tokens[...]).reshape(CELLS, SLOTS, D)
    position_taps = position_kernel.ref()

    def position(lanes):
        frame_conv(grid_in, lambda a, b: position_taps[a, b : b + 1, lanes], grid_out, 3, lanes)

    over_lanes(D, position)
    residual = tokens[...].astype(F32) + split_mm(to_token, grid_out[...].reshape(ROWS, D))
    residual = residual + position_bias[...]
    residual_out[...] = residual
    if table:
        outs[13][...] = residual
        outs[13].send()
    unit, _ = norm_parts(residual)
    normed = (unit * gain[...] + shift[...]).astype(BF16)
    normed_out[...] = normed
    normed_out.send()
    pair = pair_bias[...].astype(F32)
    value = (mm(normed, qkv_weight[2]) + pair[1:2]).astype(BF16)
    value_out[...] = value
    value_out.send()
    grid_in[:, :, 0:width] = mm(to_frame, value).reshape(CELLS, SLOTS, width)
    query = mm(normed, qkv_weight[0]) + pair[0:1]
    query_out[...] = query
    query_out.send()
    keys = mm(normed, qkv_weight[1])
    weight = jnp.exp(keys - jnp.max(keys, axis=0, keepdims=True))
    weight = weight / column_sum(weight)
    weight_out[...] = weight
    weight_out.send()
    context = jnp.where(same_head(width), t_mm(weight.astype(BF16), value), 0.0).astype(BF16)
    context_out[...] = context
    context_out.send()
    if table:
        relative_kernel = outs[12]
        for one in ins[7:10]:
            one.ref()
        tap_table(member, *ins[7:10], relative_kernel.held)
        relative_kernel.send()
        relative_taps = relative_kernel.held
    else:
        relative_taps = ins[7].ref()

    def relative(lanes):
        frame_conv(
            grid_in, lambda a, b: relative_taps[a, b : b + 1, lanes], grid_out, EDGE, lanes
        )

    over_lanes(width, relative)
    if relative_bias.shape[1] == width:
        bias_row = relative_bias[...]
    else:
        bias_row = relative_bias[:, pl.ds(pl.multiple_of(member * width, 128), width)]
    framed = grid_out[:, :, 0:width].reshape(ROWS, width).astype(BF16)
    position_term = mm(to_token, framed) + bias_row
    relative_out[...] = position_term
    relative_out.send()
    attended = SCALE * mm(query.astype(BF16), context) + query * position_term
    attended = attended.astype(BF16)
    attended_out[...] = attended
    attended_out.send()
    if early:
        outs[11][:, 0:D] = normed
        outs[11][:, D:] = attended
    partial_out[...] = mm(attended, output_weight[...]).astype(BF16)


def mark(arrays, us):
    def body(scalars, ins, outs, scratch):
        outs[0][...] = jnp.zeros((8, 128), F32)

    return call(body, [((8, 128), F32)], (), us=us, after=arrays)[0]


def copy_body(scalars, ins, outs, scratch):
    outs[0][...] = ins[0][...]


def picked(source, part):
    return source[...] if part is None else source[part]


def mlp_body(parts, split, scalars, ins, outs, scratch):
    (
        residual,
        first,
        second,
        cotangent,
        output_bias,
        gain,
        shift,
        up_weight,
        up_bias,
        down_weight,
    ) = ins
    middle_out, grad_normed_out, mlp_out, grad_bias_out = outs[:4]
    hidden_out, grad_pre_out = scratch if split else outs[4:6]
    hidden_width = up_weight.shape[1]
    projected = picked(first, parts[0]).astype(F32) + picked(second, parts[1]).astype(F32)
    middle = residual[...] + projected + output_bias[...]
    middle_out[...] = middle
    middle_out.send()
    unit, _ = norm_parts(middle)
    normed = (unit * gain[...] + shift[...]).astype(BF16)
    out_grad = picked(cotangent, parts[2])
    step = min(256, hidden_width)
    for begin in range(0, hidden_width, step):
        part = slice(begin, begin + step)
        pre = mm(normed, up_weight[:, part]) + up_bias[:, part]
        below = 0.5 * (1.0 + lax.erf(pre * (2.0**-0.5)))
        hidden_out[:, part] = (pre * below).astype(BF16)
        slope = below + pre * jnp.exp(-0.5 * pre * pre) * ((2.0 * math.pi) ** -0.5)
        grad = (mm_t(out_grad, down_weight[part, :]) * slope).astype(BF16)
        grad_pre_out[:, part] = grad
        grad_bias_out[:, part] = column_sum(grad.astype(F32))
    grad_bias_out.send()
    mlp_out[...] = mm(hidden_out[...], down_weight[...]).astype(BF16)
    mlp_out.send()
    grad_normed_out[...] = mm_t(grad_pre_out[...], up_weight[...]).astype(BF16)
    if not split:
        outs[6][...] = normed
        return
    keep, send = outs[4:6]
    core = lax.axis_index("dp") & 1
    for side in range(2):

        @pl.when(core == side)
        def _():
            up, down = (keep, send) if side == 0 else (send, keep)
            up[:, 0:hidden_width] = grad_pre_out[...]
            up[:, hidden_width:] = normed
            down[:, 0:hidden_width] = hidden_out[...]
            down[:, hidden_width:] = out_grad


def back_body(parts, split, scalars, ins, outs, scratch):
    (
        mine,
        other,
        out_grad,
        middle,
        gain,
        output_weight,
        query,
        to_frame,
        value,
        relative_kernel,
        context,
        relative,
        weight,
        to_token,
        qkv_weight,
    ) = ins[:15]
    grad_middle_out, grad_normed_out, wide_sums, head_sums = outs[:4]
    grid_grad, grid_value, grid_back = scratch
    width = relative_kernel.shape[2]
    unit, inverse = norm_parts(middle[...])
    grad = picked(mine, parts[0]).astype(F32) + picked(other, parts[1]).astype(F32)
    cotangent = picked(out_grad, parts[2]).astype(F32)
    grad_middle = cotangent + norm_back(grad, unit, inverse, gain[...])
    grad_middle_out[...] = grad_middle
    grad_middle_out.send()
    projected = grad_middle.astype(BF16)
    attended = mm_t(projected, output_weight[...])
    attended_low = attended.astype(BF16)
    query_all = query[...]
    grad_relative = attended * query_all
    shape = (CELLS, SLOTS, width)
    grid_grad[...] = mm(to_frame[...], grad_relative.astype(BF16)).reshape(shape)
    grid_value[...] = mm(to_frame[...], value[...]).reshape(shape)
    taps = relative_kernel.ref()

    def convolve(lanes):
        frame_conv(
            grid_grad,
            lambda a, b: taps[EDGE - 1 - a, EDGE - 1 - b : EDGE - b, lanes],
            grid_back,
            EDGE,
            lanes,
        )
        frame_taps(grid_grad, grid_value, head_sums, EDGE, lanes)

    over_lanes(width, convolve)
    wide_sums[0:1] = column_sum(projected.astype(F32))
    wide_sums[1:2] = column_sum(grad * unit)
    wide_sums[2:3] = column_sum(grad)
    wide_sums[3:4] = column_sum(cotangent)
    wide_sums[4:8] = jnp.zeros((4, D), F32)
    wide_sums.send()
    grad_query = SCALE * mm_t(attended_low, context[...]) + attended * relative[...]
    grad_context = SCALE * t_mm(query_all.astype(BF16), attended_low)
    grad_context = jnp.where(same_head(width), grad_context, 0.0)
    context_sum = lax.dot_general(
        jnp.ones((8, width), F32),
        grad_context * context[...].astype(F32),
        (((1,), (1,)), ((), ())),
        preferred_element_type=F32,
        precision=lax.Precision.HIGHEST,
    )[0:1]
    grad_context_low = grad_context.astype(BF16)
    weight_all = weight[...]
    grad_key = weight_all * (mm_t(value[...], grad_context_low) - context_sum)
    framed = grid_back[...].reshape(ROWS, width).astype(BF16)
    grad_value = mm(to_token[...], framed) + mm(weight_all.astype(BF16), grad_context_low)
    grad_query = grad_query.astype(BF16)
    grad_value = grad_value.astype(BF16)
    head_sums[49:50] = column_sum(grad_relative)
    head_sums[50:51] = column_sum(grad_query.astype(F32))
    head_sums[51:52] = column_sum(grad_value.astype(F32))
    head_sums[52:56] = jnp.zeros((4, width), F32)
    head_sums.send()
    grad_key = grad_key.astype(BF16)
    if split:
        keep, send = outs[4:]
        core = lax.axis_index("dp") & 1
        for which in range(2):

            @pl.when(core == which)
            def _():
                first, second = (keep, send) if which == 0 else (send, keep)
                first[:, 0:width] = grad_query
                first[:, width:D] = grad_key
                first[:, D:] = jnp.zeros_like(grad_value)
                second[:, 0:D] = projected
                second[:, D:] = grad_value

    else:
        outs[4][...] = projected
    grad_normed = None
    for index, low in enumerate((grad_query, grad_key, grad_value)):
        if not split:
            outs[5][index] = low
        term = mm_t(low, qkv_weight[index])
        grad_normed = term if grad_normed is None else grad_normed + term
    if len(ins) > 15:
        grad_normed_out[0] = grad_normed.astype(BF16)
        grad_normed_out[1] = ins[15][...]
    else:
        grad_normed_out[...] = grad_normed.astype(BF16)


def last_body(scalars, ins, outs, scratch):
    (
        mine,
        other,
        residual,
        gain,
        grad_middle,
        to_frame,
        tokens,
        position_kernel,
        to_token,
        middle,
        mlp_mine,
        down_bias,
    ) = ins[:12]
    block_out, token_grad, sums_out = outs
    grid_grad, grid_in, grid_back, sums = scratch
    unit, inverse = norm_parts(residual[...])
    grad = mine[...].astype(F32) + other[0].astype(F32)
    grad_residual = grad_middle[...] + norm_back(grad, unit, inverse, gain[...])
    grid_grad[...] = mm(to_frame[...], grad_residual.astype(BF16)).reshape(CELLS, SLOTS, D)
    grid_in[...] = mm(to_frame[...], tokens[...]).reshape(CELLS, SLOTS, D)
    taps = position_kernel.ref()
    block_out[...] = (
        middle[...] + (mlp_mine[...].astype(F32) + other[1].astype(F32)) + down_bias[...]
    )
    block_out.send()

    def convolve(lanes):
        frame_conv(
            grid_grad, lambda a, b: taps[2 - a, 2 - b : 3 - b, lanes], grid_back, 3, lanes
        )
        frame_taps(grid_grad, grid_in, sums, 3, lanes)

    over_lanes(D, convolve)
    framed = grid_back[...].reshape(ROWS, D).astype(BF16)
    token_grad[...] = grad_residual + mm(to_token[...], framed)
    token_grad.send()
    sums[9:10] = column_sum(grad_residual)
    sums[10:11] = column_sum(grad * unit)
    sums[11:12] = column_sum(grad)
    sums[12:16] = jnp.zeros((4, D), F32)
    if len(ins) == 12:
        sums_out[...] = sums[0:16]
        return
    here, came = ins[12:]
    total = here[...].astype(F32) + came[...].astype(F32)
    half, width = SMALL // 2, total.shape[1]
    sums[16:, 0:width] = total[0:half]
    sums[16:, width:] = total[half:]
    sums_out[...] = sums[...].astype(BF16)


def turn(values, distance, axis="dp"):
    size = lax.axis_size(axis)
    return lax.ppermute(values, axis, [(i, i ^ distance) for i in range(size)])


def step_bits():
    bits = list(range(1, lax.axis_size("dp").bit_length() - 1))
    return bits, bits[1::-1] + bits[2:]


def step_turn(values, step):
    orders = step_bits()
    size = lax.axis_size("dp")
    return lax.ppermute(values, "dp", [(i, i ^ (1 << orders[i & 1][step])) for i in range(size)])


def step_side(step):
    first, second = step_bits()
    me = lax.axis_index("dp")
    return (me >> jnp.where(me & 1 == 0, first[step], second[step])) & 1


def rows_of(side, count):
    return pl.ds(pl.multiple_of(side * count, 16), count)


def mlp_grads_body(scalars, ins, outs, scratch):
    hidden_width = ins[0].shape[1] - D
    core, side = lax.axis_index("dp") & 1, step_side(0)
    for which in range(2):

        @pl.when(core == which)
        def _():
            for target, place in ((outs[1], 1 - side), (outs[0], side)):
                columns = pl.ds(pl.multiple_of(place * D, 128), D)
                total = None
                for one in ins:
                    wide, narrow = one[:, columns], one[:, hidden_width:]
                    term = t_mm(narrow, wide) if which == 0 else t_mm(wide, narrow)
                    total = term if total is None else total + term
                target[...] = total.astype(BF16)


def attention_grads_body(images, scalars, ins, outs, scratch):
    stay, go = outs
    normed, attended = ins[:images], ins[images : 2 * images]
    far_early = ins[2 * images : 3 * images]
    late = ins[3 * images :]
    normed = [*normed, *far_early]
    width = D // 2

    def attended_of(place):
        return attended[place][...] if place < images else far_early[place - images][:, D:]

    def total(term):
        out = None
        for place in range(2 * images):
            out = term(place) if out is None else out + term(place)
        return out.astype(BF16)

    core, side = lax.axis_index("dp") & 1, step_side(0)

    @pl.when(core == 0)
    def _():
        for target, half in ((go, 1 - side), (stay, side)):
            columns = pl.ds(pl.multiple_of(half * width, 128), width)
            target[...] = total(lambda place: t_mm(normed[place][:, columns], late[place][:, 0:D]))

    for which in range(2):

        @pl.when((core == 1) & (side == which))
        def _():
            first, second = (stay, go) if which == 0 else (go, stay)
            first[...] = total(lambda place: t_mm(attended_of(place), late[place][:, 0:D]))
            for index in range(2):
                columns = slice(index * width, (index + 1) * width)
                second[:, columns] = total(
                    lambda place: t_mm(normed[place][:, columns], late[place][:, D:])
                )


def halve_body(step, scalars, ins, outs, scratch):
    here, came = ins
    here.ref()
    came.ref()
    if len(outs) == 1:
        outs[0][...] = (here[...].astype(F32) + came[...].astype(F32)).astype(BF16)
        return
    stay, go = outs
    count = stay.shape[0]
    side = step_side(step)
    for target, place in ((go, 1 - side), (stay, side)):
        rows = rows_of(place, count)
        target[...] = (here[rows, :].astype(F32) + came[rows, :].astype(F32)).astype(BF16)
        target.send()


def join_body(step, scalars, ins, outs, scratch):
    here, came, *more = ins
    side = step_side(step)
    added = sum(one.shape[0] for one in more)
    extra = 2 * here.shape[0] + added - outs[0].shape[0]
    count = here.shape[0] - extra
    outs[0].held[rows_of(side, count), :] = here[0:count, :]
    outs[0].held[rows_of(1 - side, count), :] = came[0:count, :]
    if extra:
        total = here[count:, :].astype(F32) + came[count:, :].astype(F32)
        outs[0][2 * count : 2 * count + extra, :] = total.astype(BF16)
    place = 2 * count + extra
    for one in more:
        outs[0][place : place + one.shape[0], :] = one[...]
        place += one.shape[0]


def group_body(scalars, ins, outs, scratch):
    head_one, head_two, wide_one, wide_two, bias_one, bias_two = ins
    (rows,) = scratch
    width = rows.shape[1]
    rows[0:50] = head_one[0:50] + head_two[0:50]
    wide = wide_one[0:4] + wide_two[0:4]
    rows[50:54] = wide[:, 0:width]
    rows[54:58] = wide[:, width:]
    bias = bias_one[...] + bias_two[...]
    for piece in range(4):
        rows[58 + piece : 59 + piece] = bias[:, piece * width : (piece + 1) * width]
    rows[62:64] = head_one[50:52] + head_two[50:52]
    outs[0][...] = rows[...].astype(BF16)


def sum_body(scalars, ins, outs, scratch):
    here, came, mine, far = ins
    count = here.shape[0]
    outs[0][0:count, :] = (here[...].astype(F32) + came[...].astype(F32)).astype(BF16)
    first = mine[0:EXTRA, :].astype(F32) + far[0:EXTRA, :].astype(F32)
    outs[0][count:, :] = first.astype(BF16)
    (rows,) = scratch
    member = lax.axis_index("mp")
    half, width = SMALL // 2, D // 2

    def unfolded(one):
        return jnp.concatenate([one[EXTRA:, 0:width], one[EXTRA:, width:]], axis=0).astype(F32)

    own, others = unfolded(mine), unfolded(far)
    rows[:, 0:width] = jnp.where(member == 0, own, others)
    rows[:, width:] = jnp.where(member == 0, others, own)
    rows[50:54, 0:width] = own[50:54]
    rows[50:54, width:] = own[54:58]
    for row in range(2):
        rows[54 + row : 55 + row, 0:width] = own[58 + 2 * row : 59 + 2 * row]
        rows[54 + row : 55 + row, width:] = own[59 + 2 * row : 60 + 2 * row]
    rows[56:57, 0:width] = own[62:63]
    rows[56:57, width:] = own[63:64]
    outs[1][...] = rows[...].astype(BF16)


def mlp_half_body(own, scalars, ins, outs, scratch):
    (block,) = ins
    up, down, wide, tall, sems = scratch
    outs[0][...] = jnp.zeros((8, 128), F32)
    core = lax.axis_index("dp") & 1

    def pieces(source, target, write):
        copies, count = [], source.shape[0] // 4
        for piece in range(4):
            rows = slice(piece * count, (piece + 1) * count)
            write(rows)
            copies.append(
                pltpu.make_async_copy(source.at[rows, :], target.at[rows, :], sems.at[piece])
            )
            copies[-1].start()
        for copy in copies:
            copy.wait()

    @pl.when(core == (0 if own else 1))
    def _():
        def write(rows):
            for tile in range(block.shape[0] // D):
                begin = tile * D + rows.start
                part = block[begin : begin + rows.stop - rows.start, :]
                wide[rows, tile * D : (tile + 1) * D] = part.astype(F32)

        pieces(wide, up, write)

    @pl.when(core == (1 if own else 0))
    def _():
        def write(rows):
            tall[rows, :] = block[rows, :].astype(F32)

        pieces(tall, down, write)


def attention_final_body(scalars, ins, outs, scratch):
    mine, other = ins
    grad_out, position, up_bias, pair_bias, three, five, seven = outs[:7]
    vectors = outs[7:]
    grad_qkv, planes, sems, small, own = scratch
    width = D // 2
    core = lax.axis_index("dp") & 1
    sent = []
    for index in range(3):
        sent.append(pltpu.make_async_copy(planes.at[index], grad_qkv.at[index], sems.at[index]))
    for side in range(2):

        @pl.when(core == side)
        def _():
            first, second = (mine, other) if side == 0 else (other, mine)
            for index in range(2):
                columns = slice(index * width, (index + 1) * width)
                planes[index] = first[0:D, columns].astype(F32)
                sent[index].start()
                planes[2, columns, :] = second[width:D, columns].astype(F32)
            sent[2].start()
            grad_out[...] = second[0:width, :].astype(F32)

    grad_out.send()
    total = mine[D:, :].astype(F32) + other[D:, :].astype(F32)
    own[...] = total[0:EXTRA]
    small[...] = total[EXTRA:]
    for row in range(3):
        position[row] = own[3 * row : 3 * row + 3]
    position.send()
    for place, vector in zip((9, 10, 11), vectors[:3]):
        vector[...] = own[place : place + 1]
    for place, vector in zip((49, 50, 51, 52, 53), vectors[3:]):
        vector[...] = small[place : place + 1]
    for vector in vectors:
        vector.send()
    up_bias[:, 0:D] = small[54:55]
    up_bias[:, D:] = small[55:56]
    up_bias.send()
    pair_bias[0:1] = small[56:57, 0:width]
    pair_bias[1:2] = small[56:57, width:]
    pair_bias.send()
    for row in range(3):
        begin = EDGE * (row + 2) + 2
        three[row] = small[begin : begin + 3, 0:128]
    three.send()
    for row in range(5):
        begin = EDGE * (row + 1) + 1
        five[row] = small[begin : begin + 5, 128:320]
    five.send()
    for row in range(EDGE):
        begin = EDGE * row
        seven[row] = pltpu.roll(small[begin : begin + EDGE, 256:512], 192, 1)[:, 0:192]
    seven.send()
    for copy in sent:
        copy.wait()


def halve(keep, came, step, after=(), us=0.0):
    outs = [((keep.shape[0] // 2, D), BF16)] * 2
    body = functools.partial(halve_body, step)
    keep, send = call(body, outs, (keep, came), us=us, after=after)
    return keep, step_turn(send, step)


def join(keep, came, step, extra=0, more=(), after=(), us=0.0):
    height = (keep.shape[0] - extra) * 2 + extra + sum(one.shape[0] for one in more)
    body = functools.partial(join_body, step)
    return call(body, [((height, D), BF16)], (keep, came, *more), us=us, after=after)[0]


def half_write(own, block, after, fill):
    scratch = [pltpu.VMEM(one.shape, F32) for one in fill] + [pltpu.SemaphoreType.DMA((4,))]
    body = functools.partial(mlp_half_body, own)
    return call(body, [((8, 128), F32)], (block,), scratch, us=0.0, after=after, fill=fill)


def sum_small(values):
    size = lax.axis_size("dp")
    if size & (size - 1):
        return lax.psum(values, "dp")
    for bit in range(size.bit_length() - 1):
        values = values + turn(values, 1 << bit)
    return values


def whole_body(products, scalars, ins, outs, scratch):
    for target, pairs in zip(outs, products):
        total = None
        for left, right in pairs:
            one, two = (ins[i][...] if part is None else ins[i][part] for i, part in (left, right))
            term = t_mm(one, two)
            total = term if total is None else total + term
        target[...] = total.astype(BF16)


def per_device(
    tokens,
    out_grad,
    crop_image,
    crop_res,
    position_kernel,
    position_bias,
    gain_one,
    shift_one,
    qkv_weight,
    query_value_bias,
    relative_three,
    relative_five,
    relative_seven,
    relative_bias,
    output_weight,
    output_bias,
    gain_two,
    shift_two,
    up_weight,
    up_bias,
    down_weight,
    down_bias,
):
    group = lax.axis_size("mp")
    member = lax.axis_index("mp")
    rows = tokens.shape[0]
    width = qkv_weight.shape[2]
    hidden_width = up_weight.shape[1]
    pair = group == 2
    size = lax.axis_size("dp")
    blocks = (
        pair
        and size >= 4
        and size & (size - 1) == 0
        and 2 * width == D
        and hidden_width == 2 * D
        and D % (size * 8) == 0
    )

    def row(vector):
        return vector.reshape(1, -1)

    if not blocks:
        full_kernel = jnp.concatenate(
            [
                jnp.pad(relative_three, ((2, 2), (2, 2), (0, 0))),
                jnp.pad(relative_five, ((1, 1), (1, 1), (0, 0))),
                relative_seven,
            ],
            axis=2,
        )
        kernel_part = lax.dynamic_slice_in_dim(full_kernel, member * width, width, 2)
        bias_part = row(lax.dynamic_slice_in_dim(relative_bias, member * width, width, 0))
    else:
        kernel_part, bias_part = None, row(relative_bias)
    qkv_planes = jnp.transpose(qkv_weight, (1, 0, 2))

    if pair:
        token_list = [tokens, turn(tokens, 1, "mp")]
        images = [lambda: lax.axis_index("mp"), lambda: 1 - lax.axis_index("mp")]
    else:
        token_list = list(lax.all_gather(tokens, "mp", axis=0))
        grad_list = list(lax.all_gather(out_grad, "mp", axis=0))
        images = [functools.partial(int, j) for j in range(group)]

    def own(parts):
        if pair:
            return parts[0]
        return lax.dynamic_index_in_dim(jnp.stack(parts), member, 0, keepdims=False)

    fronts = []
    for index, (image, one) in enumerate(zip(images, token_list)):
        table = blocks and index == 0
        outs = [
            Far((ROWS, rows), BF16),
            Far((rows, ROWS), BF16),
            ((rows, D), F32),
            Far((rows, D), BF16),
            Far((rows, width), F32),
            Far((rows, width), BF16),
            Far((rows, width), F32),
            Far((width, width), BF16),
            Far((rows, width), F32),
            Far((rows, width), BF16),
            ((rows, D), BF16),
        ]
        if blocks:
            outs.append(((rows, D + width), BF16))
        args = [
            crop_res,
            Far(one) if index == 0 else one,
            Far(position_kernel),
            Far(row(position_bias)),
            Far(row(gain_one)),
            Far(row(shift_one)),
            Far(qkv_planes),
            Far(query_value_bias),
        ]
        if table:
            outs += [Far((EDGE, EDGE, width), F32), Far((rows, D), F32)]
            args += [Far(relative_three), Far(relative_five), Far(relative_seven)]
        else:
            args.append(Far(kernel_part))
        args += [Far(bias_part), Far(output_weight)]
        scratch = [pltpu.VMEM((CELLS, SLOTS, D), F32)] * 2
        body = functools.partial(front_body, image, table, blocks)
        if index:
            args = [one.what[0] if isinstance(one, Far) and one.what[0] is not kernel_part else one for one in args]
        bring = (up_weight, down_weight) if pair and index else ()
        us = 5.0 if index else 50.0
        made = call(body, outs, args, scratch, us=us, smem=1, bring=bring)
        if bring:
            up_weight, down_weight = made[-2:]
        if table:
            kernel_part, kept_residual = made[12:14]
        fronts.append(made[: 12 if blocks else 11])
    to_frame, to_token, residual, normed, query, value, weight, context = tuple(zip(*fronts))[:8]
    relative, attended, partial, *early = tuple(zip(*fronts))[8:]

    if pair:
        (ready,) = call(copy_body, [((rows, D), BF16)], partial[:1], us=0.3, after=[token_list[1]])
        first, second = turn(ready, 1, "mp"), turn(partial[1], 1, "mp")
        grad_list, grad_parts = [out_grad, turn(out_grad, 1, "mp")], [None, None]
        addends = [(partial[0], second), (partial[1], first)]
        places = [(None, None), (None, None)]
        order = (1, 0)
        arrived = mark([grad_list[1], partial[1]], ARRIVED)
    else:
        total = lax.psum(jnp.stack(partial), "mp")
        grad_parts = [None] * group
        addends = [(one, jnp.zeros_like(one)) for one in total]
        places = [(None, None)] * group
        order = range(group)
    mlps = [None] * group
    for index in order:
        outs = [Far((rows, D), F32), ((rows, D), BF16), Far((rows, D), BF16)]
        outs.append(Far((1, hidden_width), F32))
        scratch = []
        if blocks:
            outs += [((rows, hidden_width + D), BF16)] * 2
            scratch = [pltpu.VMEM((rows, hidden_width), BF16)] * 2
        else:
            outs += [((rows, hidden_width), BF16)] * 2 + [((rows, D), BF16)]
        args = (
            residual[index],
            *addends[index],
            grad_list[index],
            row(output_bias),
            row(gain_two),
            row(shift_two),
            up_weight,
            row(up_bias.astype(F32)),
            down_weight,
        )
        body = functools.partial(mlp_body, (*places[index], grad_parts[index]), blocks)
        after = []
        if pair:
            after = [mlps[1][1]] if index == 0 else [arrived]
        mlps[index] = call(body, outs, args, scratch, us=2.5, after=after)
    middle, grad_two_part, mlp_part, grad_up_bias, *mlp_rows = zip(*mlps)

    if pair:
        back_addends = [
            (grad_two_part[0], turn(grad_two_part[1], 1, "mp")),
            (grad_two_part[1], turn(grad_two_part[0], 1, "mp")),
        ]
    else:
        total = lax.psum(jnp.stack(grad_two_part), "mp")
        back_addends = [(one, jnp.zeros_like(one)) for one in total]

    steps = len(step_bits()[0])
    if blocks:
        args = (*mlp_rows[0], *(turn(one, 1) for one in mlp_rows[1]))
        after = [mark([back_addends[0][1]], 46.0)]
        mlp_keep, mlp_send = call(mlp_grads_body, [((D, D), BF16)] * 2, args, us=2.0, after=after)
        mlp_came = step_turn(mlp_send, 0)

    backs = []
    for index in range(group):
        carry = pair and index == 1
        outs = [
            Far((rows, D), F32),
            ((2, rows, D) if carry else (rows, D), BF16),
            Far((8, D), F32),
            Far((56, width), F32),
        ]
        if blocks:
            outs += [((rows, D + width), BF16)] * 2
        else:
            outs += [((rows, D), BF16), ((3, rows, width), BF16)]
        args = [
            *back_addends[index],
            grad_list[index],
            middle[index],
            row(gain_two),
            output_weight,
            query[index],
            to_frame[index],
            value[index],
            kernel_part,
            context[index],
            relative[index],
            weight[index],
            to_token[index],
            qkv_planes,
        ]
        if carry:
            args.append(mlp_part[1])
        scratch = [pltpu.VMEM((CELLS, SLOTS, width), F32)] * 3
        body = functools.partial(back_body, (None, None, grad_parts[index]), blocks)
        after = [mlp_keep] if blocks else []
        if pair and index:
            after.append(backs[0][1])
        backs.append(call(body, outs, args, scratch, us=25.0 if index else 0.0, after=after))
    grad_middle, grad_one_part, wide_sums, head_sums, *late = zip(*backs)

    if blocks:
        mlp_keep, mlp_came = halve(mlp_keep, mlp_came, 1, after=[backs[1][1]], us=WEIGHTS["h1"])
        outs = [((width, D), BF16)] * 2
        args = (*normed, *attended, *(turn(one, 1) for one in early[0]))
        args += (*late[0], *(turn(one, 1) for one in late[1]))
        body = functools.partial(attention_grads_body, group)
        keep, send = call(body, outs, args, us=2.0, after=[mlp_keep])
        came = step_turn(send, 0)
        outs = [((SMALL, width), BF16)]
        args = (*head_sums, *wide_sums, *grad_up_bias)
        scratch = [pltpu.VMEM((SMALL, width), F32)]
        (group_sums,) = call(group_body, outs, args, scratch, us=0.0, after=[keep])
        group_came = step_turn(group_sums, steps - 1)
    if not blocks:
        hidden, grad_pre, normed_two = mlp_rows
        grad_projected, grad_qkv = late
        args = (*normed_two, *grad_pre, *hidden, *grad_list)
        args += (*normed, *grad_qkv, *attended, *grad_projected)

        def spot(kind, image, part=None):
            return kind * group + image, part

        each = range(group)
        products = [
            [(spot(0, j), spot(1, j)) for j in each],
            [(spot(2, j), spot(3, j, grad_parts[j])) for j in each],
        ]
        products += [[(spot(4, j), spot(5, j, plane)) for j in each] for plane in range(3)]
        products += [[(spot(6, j), spot(7, j)) for j in each]]
        outs = [((D, hidden_width), BF16), ((hidden_width, D), BF16)]
        outs += [((D, width), BF16)] * 3 + [((width, D), BF16)]
        wholes = call(functools.partial(whole_body, products), outs, args, us=6.0, vmem=40)
        grad_up, grad_down, *planes, grad_out = (lax.psum(one, "dp").astype(F32) for one in wholes)
        grad_qkv_planes = jnp.stack(planes)

    if pair:
        mine, mlp_mine = grad_one_part[0], mlp_part[0]
        other = turn(grad_one_part[1], 1, "mp")
    else:
        sums = [jnp.stack(grad_one_part), jnp.stack(mlp_part)]
        mine, mlp_mine = (lax.psum_scatter(one, "mp", scatter_dimension=0) for one in sums)
        other = jnp.zeros((2, rows, D), BF16)
    outs = [Far((rows, D), F32), Far((rows, D), F32)]
    height = EXTRA + SMALL // 2 if blocks else EXTRA
    outs.append(((height, D), BF16 if blocks else F32))
    args = [
        mine,
        other,
        kept_residual if blocks else own(residual),
        row(gain_one),
        own(grad_middle),
        own(to_frame),
        tokens,
        position_kernel,
        own(to_token),
        own(middle),
        mlp_mine,
        row(down_bias),
    ]
    if blocks:
        args += [group_sums, group_came]
    scratch = [pltpu.VMEM((CELLS, SLOTS, D), F32)] * 3
    scratch.append(pltpu.VMEM((height, D), F32))
    after = []
    if blocks:
        for step in range(2, steps):
            us = WEIGHTS["h2"]
            mlp_keep, mlp_came = halve(mlp_keep, mlp_came, step, after=[keep], us=us)
        keep, came = halve(keep, came, 1, after=[mlp_keep], us=WEIGHTS["p1"])
        after = [keep, mark([group_came, group_sums], HELD)]
    block_out, token_grad, own_sums = call(
        last_body, outs, args, scratch, us=WEIGHTS["last"], after=after
    )

    if blocks:
        far_sums = turn(own_sums, 1, "mp")
        mark_last = own_sums
        for step in range(2, steps):
            keep, came = halve(keep, came, step, after=[mark_last], us=WEIGHTS["p2"])
            mark_last = keep
        outs = [(mlp_keep.shape, BF16)]
        body = functools.partial(halve_body, None)
        args = (mlp_keep, mlp_came)
        (mlp_keep,) = call(body, outs, args, us=WEIGHTS["total"], after=[mark_last])
        mlp_came = step_turn(mlp_keep, steps - 1)
        args = (keep, came, own_sums, far_sums)
        outs = [((keep.shape[0] + EXTRA, D), BF16), ((SMALL, D), BF16)]
        scratch = [pltpu.VMEM((SMALL, D), F32)]
        us = WEIGHTS["pack"]
        keep, small = call(sum_body, outs, args, scratch, us=us, after=[mlp_keep])
        extra, more = EXTRA, [small]
        for step in reversed(range(steps)):
            came = step_turn(keep, step)
            us = WEIGHTS.get(f"j{step}", 0.0)
            mlp_keep = join(mlp_keep, mlp_came, step, after=[keep], us=us)
            mlp_came = step_turn(mlp_keep, step - 1) if step else turn(mlp_keep, 1)
            mark_last = mlp_keep
            if not step:
                shapes = [(D, hidden_width), (hidden_width, D)]
                fill = [jax.ShapeDtypeStruct(shape, F32) for shape in shapes]
                mark_last, grad_up, grad_down = half_write(True, mlp_keep, [], fill)
            us = WEIGHTS.get(f"a{step}", 0.0)
            keep = join(keep, came, step, extra, more, after=[mark_last], us=us)
            extra, more = EXTRA + SMALL, []
        came = turn(keep, 1)
        finished, grad_up, grad_down = half_write(False, mlp_came, [keep], (grad_up, grad_down))
        shapes = [(width, D), (3, 3, D), (1, hidden_width), (2, width)]
        shapes += [relative_three.shape, relative_five.shape, relative_seven.shape]
        outs = [Far(shape, F32) for shape in shapes + [(1, D)] * 8]
        scratch = [pltpu.VMEM((3, D, width), F32), pltpu.SemaphoreType.DMA((3,))]
        scratch += [pltpu.VMEM((SMALL, D), F32), pltpu.VMEM((EXTRA, D), F32)]
        made = call(
            attention_final_body,
            outs,
            (keep, came),
            scratch,
            after=[finished],
            fill=[jax.ShapeDtypeStruct((3, D, width), F32)],
        )
        grad_out, position, up_sum, pair_sum, three, five, seven, *vectors, grad_qkv_planes = made
        vectors = [one.reshape(D) for one in vectors]
        return (
            block_out,
            token_grad,
            position,
            *vectors[0:3],
            jnp.transpose(grad_qkv_planes, (1, 0, 2)),
            pair_sum,
            three,
            five,
            seven,
            vectors[3],
            grad_out,
            *vectors[4:7],
            grad_up,
            up_sum.reshape(hidden_width),
            grad_down,
            vectors[7],
        )

    head_total = functools.reduce(jnp.add, head_sums)
    wide_total = functools.reduce(jnp.add, wide_sums)
    own_total = lax.psum(own_sums[:12], "mp")
    relative_total = lax.all_gather(head_total[:50], "mp", axis=1, tiled=True)
    bias_total = functools.reduce(jnp.add, grad_up_bias)
    pieces = [own_total, wide_total[:4], relative_total]
    private = jnp.concatenate([bias_total.reshape(-1), head_total[50:52].reshape(-1)])
    pieces.append(jnp.pad(private, (0, -private.shape[0] % D)).reshape(-1, D))
    total = sum_small(jnp.concatenate(pieces, axis=0))
    kernel_grad = total[16:65].reshape(EDGE, EDGE, D)
    tail = total[66:].reshape(-1)
    return (
        block_out,
        token_grad,
        total[:9].reshape(3, 3, D),
        total[9],
        total[10],
        total[11],
        jnp.transpose(grad_qkv_planes, (1, 0, 2)),
        tail[hidden_width : hidden_width + 2 * width].reshape(2, width),
        kernel_grad[2:5, 2:5, : 2 * HEAD],
        kernel_grad[1:6, 1:6, 2 * HEAD : 5 * HEAD],
        kernel_grad[:, :, 5 * HEAD :],
        total[65],
        grad_out,
        total[12],
        total[13],
        total[14],
        grad_up,
        tail[:hidden_width],
        grad_down,
        total[15],
    )


def solution(mesh):
    in_specs = (
        P(("dp", "mp"), None),
        P(("dp", "mp"), None),
        P("dp"),
        P("dp"),
        P(),
        P(),
        P(),
        P(),
        P(None, None, "mp"),
        P(None, "mp"),
        P(),
        P(),
        P(),
        P(),
        P("mp", None),
        P(),
        P(),
        P(),
        P(None, "mp"),
        P("mp"),
        P("mp", None),
        P(),
    )
    out_specs = (
        P(("dp", "mp"), None),
        P(("dp", "mp"), None),
        P(),
        P(),
        P(),
        P(),
        P(None, None, "mp"),
        P(None, "mp"),
        P(),
        P(),
        P(),
        P(),
        P("mp", None),
        P(),
        P(),
        P(),
        P(None, "mp"),
        P("mp"),
        P("mp", None),
        P(),
    )
    return jax.shard_map(
        per_device, mesh=mesh, in_specs=in_specs, out_specs=out_specs, check_vma=False
    )
```

```python
import functools
import math

import jax
import jax.numpy as jnp
from jax import lax
from jax.experimental import pallas as pl
from jax.experimental.pallas import tpu as pltpu
from jax.sharding import PartitionSpec as P

HEAD = 64
D = 512
EPSILON = 1e-06
SLOTS = 8
EDGE = 7
CELLS = EDGE * EDGE
ROWS = CELLS * SLOTS
SCALE = HEAD ** (-0.5)
SMALL = 64
EXTRA = 16
HELD = 60.0
ARRIVED = 46.0
WEIGHTS = dict(
    h1=0.0, h2=0.0, p1=40.0, last=0.0, p2=0.0, total=0.0, pack=40.0, j2=0.0, a2=0.0, j1=0.0, a1=40.0, j0=0.0, a0=40.0
)
BF16 = jnp.bfloat16
F32 = jnp.float32


def mm(left, right):
    return jnp.dot(left, right, preferred_element_type=F32)


def mm_t(left, right):
    return lax.dot_general(left, right, (((1,), (1,)), ((), ())), preferred_element_type=F32)


def t_mm(left, right):
    return lax.dot_general(left, right, (((0,), (0,)), ((), ())), preferred_element_type=F32)


def split_mm(onehot, values):
    high = values.astype(BF16)
    low = (values - high.astype(F32)).astype(BF16)
    return mm(onehot, high) + mm(onehot, low)


class Source:
    def __init__(self, ref, copy=None):
        self.held, self.copy, self.shape = ref, copy, ref.shape

    def ref(self):
        if self.copy is not None:
            self.copy.wait()
            self.copy = None
        return self.held

    def __getitem__(self, index):
        return self.ref()[index]


class Result:
    def __init__(self, ref, copy=None):
        self.held, self.copy, self.sent, self.shape = ref, copy, copy is None, ref.shape

    def __setitem__(self, index, value):
        self.held[index] = value

    def __getitem__(self, index):
        return self.held[index]

    def send(self):
        if not self.sent:
            self.copy.start()
            self.sent = True


class Far:
    def __init__(self, *what):
        self.what = what


def call(body, outs, args, scratch=(), us=3.0, smem=0, vmem=24, after=(), bring=(), fill=()):
    far_in = [isinstance(one, Far) for one in args[smem:]]
    far_out = [isinstance(one, Far) for one in outs]
    arrays = [one.what[0] if isinstance(one, Far) else one for one in args[smem:]]
    outs = [one.what if isinstance(one, Far) else one for one in outs]
    filled_in = [one for one in fill if not isinstance(one, jax.ShapeDtypeStruct)]

    def kernel(*refs):
        refs = list(refs)

        def take(count):
            taken = refs[:count]
            del refs[:count]
            return taken

        far_scalars, given = take(smem), take(len(arrays))
        distant, _ = take(len(bring)), take(len(after) + len(filled_in))
        places, brought, filled = take(len(outs)), take(len(bring)), take(len(fill))
        near_scalars = take(smem)
        scalar_sems = take(1)[0] if smem else None
        near_in, near_out = take(sum(far_in)), take(sum(far_out))
        scalars = []
        for index, (away, near) in enumerate(zip(far_scalars, near_scalars)):
            copy = pltpu.make_async_copy(away, near, scalar_sems.at[index])
            copy.start()
            scalars.append(Source(near, copy))
        in_sems = take(1)[0] if any(far_in) else None
        out_sems = take(1)[0] if any(far_out) else None
        bring_sems = take(1)[0] if bring else None
        ins, made, moves = [], [], []
        for ref, far in zip(given, far_in):
            if far:
                index = sum(one.copy is not None for one in ins)
                copy = pltpu.make_async_copy(ref, near_in[index], in_sems.at[index])
                copy.start()
                ins.append(Source(near_in[index], copy))
            else:
                ins.append(Source(ref))
        for index, (source, target) in enumerate(zip(distant, brought)):
            moves.append(pltpu.make_async_copy(source, target, bring_sems.at[index]))
            moves[-1].start()
        for ref, far in zip(places, far_out):
            if far:
                index = sum(one.copy is not None for one in made)
                copy = pltpu.make_async_copy(near_out[index], ref, out_sems.at[index])
                made.append(Result(near_out[index], copy))
            else:
                made.append(Result(ref))
        body(scalars, ins, made, filled + refs)
        for one in made:
            one.send()
        for one in scalars + ins:
            one.ref()
        for one in made:
            if one.copy is not None:
                one.copy.wait()
        for copy in moves:
            copy.wait()

    shapes = [pltpu.SMEM(one.shape, one.dtype) for one in args[:smem]]
    if smem:
        shapes.append(pltpu.SemaphoreType.DMA((smem,)))
    shapes += [pltpu.VMEM(one.shape, one.dtype) for one, far in zip(arrays, far_in) if far]
    shapes += [pltpu.VMEM(*one) for one, far in zip(outs, far_out) if far]
    if any(far_in):
        shapes.append(pltpu.SemaphoreType.DMA((sum(far_in),)))
    if any(far_out):
        shapes.append(pltpu.SemaphoreType.DMA((sum(far_out),)))
    if bring:
        shapes.append(pltpu.SemaphoreType.DMA((len(bring),)))
    near, far = pl.BlockSpec(memory_space=pltpu.VMEM), pl.BlockSpec(memory_space=pltpu.HBM)
    operands = [
        pltpu.with_memory_space_constraint(one, pltpu.HBM) if away else one
        for one, away in zip(arrays, far_in)
    ]
    brought_far = [pltpu.with_memory_space_constraint(one, pltpu.HBM) for one in bring]
    scalars_far = [pltpu.with_memory_space_constraint(one, pltpu.HBM) for one in args[:smem]]
    return pl.pallas_call(
        kernel,
        out_shape=[
            pltpu.HBM(*one) if away else jax.ShapeDtypeStruct(*one)
            for one, away in zip(outs, far_out)
        ]
        + [jax.ShapeDtypeStruct(one.shape, one.dtype) for one in bring]
        + [pltpu.HBM(one.shape, one.dtype) for one in fill],
        in_specs=[far] * smem
        + [far if away else near for away in far_in]
        + [far] * len(bring)
        + [pl.BlockSpec(memory_space=pl.ANY)] * len(after)
        + [far] * len(filled_in),
        out_specs=[far if away else near for away in far_out]
        + [near] * len(bring)
        + [far] * len(fill),
        input_output_aliases={
            len(args) + len(bring) + len(after) + index: len(outs) + len(bring) + index
            for index in range(len(filled_in))
        },
        scratch_shapes=shapes + list(scratch),
        compiler_params=pltpu.CompilerParams(vmem_limit_bytes=vmem << 20),
        cost_estimate=pl.CostEstimate(
            flops=int(us * 1.0e8), bytes_accessed=1 << 12, transcendentals=0
        ),
    )(*scalars_far, *operands, *brought_far, *after, *filled_in)


def over_lanes(width, body, unroll=False):
    if width % 128:
        body(slice(0, width))
    elif unroll:
        for begin in range(0, width, 128):
            body(slice(begin, begin + 128))
    else:

        @pl.loop(0, width // 128)
        def _(step):
            body(pl.ds(pl.multiple_of(step * 128, 128), 128))


def frame_conv(source, tap, target, edge, lanes):
    half = (edge - 1) // 2
    for i in range(EDGE):
        total = [None] * EDGE
        for a in range(edge):
            row = i + a - half
            if not 0 <= row < EDGE:
                continue
            cells = [source[row * EDGE + j, :, lanes] for j in range(EDGE)]
            for b in range(edge):
                weight = tap(a, b)
                for j in range(EDGE):
                    column = j + b - half
                    if 0 <= column < EDGE:
                        term = cells[column] * weight
                        total[j] = term if total[j] is None else total[j] + term
        for j in range(EDGE):
            target[i * EDGE + j, :, lanes] = total[j]


def frame_taps(grad, source, target, edge, lanes):
    half = (edge - 1) // 2
    for a in range(edge):
        total = [None] * edge
        for i in range(EDGE):
            row = i + a - half
            if not 0 <= row < EDGE:
                continue
            cells = [source[row * EDGE + j, :, lanes] for j in range(EDGE)]
            for j in range(EDGE):
                own = grad[i * EDGE + j, :, lanes]
                for b in range(edge):
                    column = j + b - half
                    if 0 <= column < EDGE:
                        term = own * cells[column]
                        total[b] = term if total[b] is None else total[b] + term
        for b in range(edge):
            row = a * edge + b
            target[row : row + 1, lanes] = jnp.sum(total[b], axis=0, keepdims=True)


def crop_frames(kinds, base, rows):
    sub = lax.broadcasted_iota(jnp.int32, (SLOTS, rows), 0)
    lane = lax.broadcasted_iota(jnp.int32, (SLOTS, rows), 1)
    place = lax.broadcasted_iota(jnp.int32, (8, ROWS), 1)
    slot = place & (SLOTS - 1)
    cell = place >> 3
    down = (cell * 37) >> 8
    across = cell - down * EDGE
    begin = jnp.zeros((SLOTS, rows), jnp.int32)
    whole = jnp.zeros((SLOTS, rows), jnp.int32)
    begin_row = jnp.zeros((8, ROWS), jnp.int32)
    whole_row = jnp.zeros((8, ROWS), jnp.int32)
    start = jnp.int32(0)
    for s in range(SLOTS):
        large = (kinds[base + s] == 0).astype(jnp.int32)
        begin = jnp.where(sub == s, start, begin)
        whole = jnp.where(sub == s, large, whole)
        begin_row = jnp.where(slot == s, start, begin_row)
        whole_row = jnp.where(slot == s, large, whole_row)
        start = start + 9 + 40 * large
    tiles = []
    for i in range(EDGE):
        for j in range(EDGE):
            small = begin + (i * 3 + j) if i < 3 and j < 3 else jnp.full_like(begin, -1)
            token = jnp.where(whole == 1, begin + (i * EDGE + j), small)
            tiles.append(jnp.where(token == lane, 1.0, 0.0))
    to_frame = jnp.concatenate(tiles, axis=0).astype(BF16)
    corner = jnp.where((down < 3) & (across < 3), begin_row + down * 3 + across, -1)
    token_row = jnp.where(whole_row == 1, begin_row + cell, corner)
    height = lax.broadcasted_iota(jnp.int32, (rows, ROWS), 0)
    to_token = jnp.where(height == token_row[0:1], 1.0, 0.0).astype(BF16)
    return to_frame, to_token


def norm_parts(values):
    average = jnp.mean(values, axis=-1, keepdims=True)
    centred = values - average
    variance = jnp.mean(centred * centred, axis=-1, keepdims=True)
    inverse = lax.rsqrt(variance + EPSILON)
    return centred * inverse, inverse


def norm_back(grad, unit, inverse, gain):
    scaled = grad * gain
    first = jnp.mean(scaled, axis=-1, keepdims=True)
    second = jnp.mean(scaled * unit, axis=-1, keepdims=True)
    return (scaled - first - unit * second) * inverse


def column_sum(values):
    return jnp.sum(values, axis=0, keepdims=True)


def same_head(width):
    rows = lax.broadcasted_iota(jnp.int32, (width, width), 0) // HEAD
    columns = lax.broadcasted_iota(jnp.int32, (width, width), 1) // HEAD
    return rows == columns


def tap_table(member, three, five, seven, table):
    table[...] = jnp.zeros(table.shape, F32)

    @pl.when(member == 0)
    def _():
        table[2:5, 2:5, 0:128] = three[...]
        for row in range(5):
            table[1 + row, 1:6, 128:256] = five[row, :, 0:128]

    @pl.when(member == 1)
    def _():
        for row in range(5):
            table[1 + row, 1:6, 0:64] = five[row, :, 128:192]
        lane = lax.broadcasted_iota(jnp.int32, (EDGE, 128), 1)
        for row in range(EDGE):
            near = pltpu.roll(seven[row, :, 0:128], 64, 1)
            wide = jnp.concatenate([seven[row, :, 128:192], jnp.zeros((EDGE, 64), F32)], axis=1)
            far = pltpu.roll(wide, 64, 1)
            table[row, :, 0:128] = jnp.where(lane < 64, table[row, :, 0:128], near)
            table[row, :, 128:256] = jnp.where(lane < 64, near, far)


def front_body(image, table, early, scalars, ins, outs, scratch):
    (kinds,) = scalars
    tokens, position_kernel, position_bias, gain, shift, qkv_weight, pair_bias = ins[:7]
    relative_bias, output_weight = ins[-2:]
    (
        to_frame_out,
        to_token_out,
        residual_out,
        normed_out,
        query_out,
        value_out,
        weight_out,
        context_out,
        relative_out,
        attended_out,
        partial_out,
    ) = outs[:11]
    grid_in, grid_out = scratch
    rows = tokens.shape[0]
    width = output_weight.shape[0]
    member = lax.axis_index("mp")
    to_frame, to_token = crop_frames(kinds, image() * SLOTS, rows)
    to_frame_out[...] = to_frame
    to_frame_out.send()
    to_token_out[...] = to_token
    to_token_out.send()
    grid_in[...] = mm(to_frame, tokens[...]).reshape(CELLS, SLOTS, D)
    position_taps = position_kernel.ref()

    def position(lanes):
        frame_conv(grid_in, lambda a, b: position_taps[a, b : b + 1, lanes], grid_out, 3, lanes)

    over_lanes(D, position)
    residual = tokens[...].astype(F32) + split_mm(to_token, grid_out[...].reshape(ROWS, D))
    residual = residual + position_bias[...]
    residual_out[...] = residual
    if table:
        outs[13][...] = residual
        outs[13].send()
    unit, _ = norm_parts(residual)
    normed = (unit * gain[...] + shift[...]).astype(BF16)
    normed_out[...] = normed
    normed_out.send()
    pair = pair_bias[...].astype(F32)
    value = (mm(normed, qkv_weight[2]) + pair[1:2]).astype(BF16)
    value_out[...] = value
    value_out.send()
    grid_in[:, :, 0:width] = mm(to_frame, value).reshape(CELLS, SLOTS, width)
    query = mm(normed, qkv_weight[0]) + pair[0:1]
    query_out[...] = query
    query_out.send()
    keys = mm(normed, qkv_weight[1])
    weight = jnp.exp(keys - jnp.max(keys, axis=0, keepdims=True))
    weight = weight / column_sum(weight)
    weight_out[...] = weight
    weight_out.send()
    context = jnp.where(same_head(width), t_mm(weight.astype(BF16), value), 0.0).astype(BF16)
    context_out[...] = context
    context_out.send()
    if table:
        relative_kernel = outs[12]
        for one in ins[7:10]:
            one.ref()
        tap_table(member, *ins[7:10], relative_kernel.held)
        relative_kernel.send()
        relative_taps = relative_kernel.held
    else:
        relative_taps = ins[7].ref()

    def relative(lanes):
        frame_conv(
            grid_in, lambda a, b: relative_taps[a, b : b + 1, lanes], grid_out, EDGE, lanes
        )

    over_lanes(width, relative)
    if relative_bias.shape[1] == width:
        bias_row = relative_bias[...]
    else:
        bias_row = relative_bias[:, pl.ds(pl.multiple_of(member * width, 128), width)]
    framed = grid_out[:, :, 0:width].reshape(ROWS, width).astype(BF16)
    position_term = mm(to_token, framed) + bias_row
    relative_out[...] = position_term
    relative_out.send()
    attended = SCALE * mm(query.astype(BF16), context) + query * position_term
    attended = attended.astype(BF16)
    attended_out[...] = attended
    attended_out.send()
    if early:
        outs[11][:, 0:D] = normed
        outs[11][:, D:] = attended
    partial_out[...] = mm(attended, output_weight[...]).astype(BF16)


def mark(arrays, us):
    def body(scalars, ins, outs, scratch):
        outs[0][...] = jnp.zeros((8, 128), F32)

    return call(body, [((8, 128), F32)], (), us=us, after=arrays)[0]


def copy_body(scalars, ins, outs, scratch):
    outs[0][...] = ins[0][...]


def picked(source, part):
    return source[...] if part is None else source[part]


def mlp_body(parts, split, scalars, ins, outs, scratch):
    (
        residual,
        first,
        second,
        cotangent,
        output_bias,
        gain,
        shift,
        up_weight,
        up_bias,
        down_weight,
    ) = ins
    middle_out, grad_normed_out, mlp_out, grad_bias_out = outs[:4]
    hidden_out, grad_pre_out = scratch if split else outs[4:6]
    hidden_width = up_weight.shape[1]
    projected = picked(first, parts[0]).astype(F32) + picked(second, parts[1]).astype(F32)
    middle = residual[...] + projected + output_bias[...]
    middle_out[...] = middle
    middle_out.send()
    unit, _ = norm_parts(middle)
    normed = (unit * gain[...] + shift[...]).astype(BF16)
    out_grad = picked(cotangent, parts[2])
    step = min(256, hidden_width)
    for begin in range(0, hidden_width, step):
        part = slice(begin, begin + step)
        pre = mm(normed, up_weight[:, part]) + up_bias[:, part]
        below = 0.5 * (1.0 + lax.erf(pre * (2.0**-0.5)))
        hidden_out[:, part] = (pre * below).astype(BF16)
        slope = below + pre * jnp.exp(-0.5 * pre * pre) * ((2.0 * math.pi) ** -0.5)
        grad = (mm_t(out_grad, down_weight[part, :]) * slope).astype(BF16)
        grad_pre_out[:, part] = grad
        grad_bias_out[:, part] = column_sum(grad.astype(F32))
    grad_bias_out.send()
    mlp_out[...] = mm(hidden_out[...], down_weight[...]).astype(BF16)
    mlp_out.send()
    grad_normed_out[...] = mm_t(grad_pre_out[...], up_weight[...]).astype(BF16)
    if not split:
        outs[6][...] = normed
        return
    keep, send = outs[4:6]
    core = lax.axis_index("dp") & 1
    for side in range(2):

        @pl.when(core == side)
        def _():
            up, down = (keep, send) if side == 0 else (send, keep)
            up[:, 0:hidden_width] = grad_pre_out[...]
            up[:, hidden_width:] = normed
            down[:, 0:hidden_width] = hidden_out[...]
            down[:, hidden_width:] = out_grad


def back_body(parts, split, scalars, ins, outs, scratch):
    (
        mine,
        other,
        out_grad,
        middle,
        gain,
        output_weight,
        query,
        to_frame,
        value,
        relative_kernel,
        context,
        relative,
        weight,
        to_token,
        qkv_weight,
    ) = ins[:15]
    grad_middle_out, grad_normed_out, wide_sums, head_sums = outs[:4]
    grid_grad, grid_value, grid_back = scratch
    width = relative_kernel.shape[2]
    unit, inverse = norm_parts(middle[...])
    grad = picked(mine, parts[0]).astype(F32) + picked(other, parts[1]).astype(F32)
    cotangent = picked(out_grad, parts[2]).astype(F32)
    grad_middle = cotangent + norm_back(grad, unit, inverse, gain[...])
    grad_middle_out[...] = grad_middle
    grad_middle_out.send()
    projected = grad_middle.astype(BF16)
    attended = mm_t(projected, output_weight[...])
    attended_low = attended.astype(BF16)
    query_all = query[...]
    grad_relative = attended * query_all
    shape = (CELLS, SLOTS, width)
    grid_grad[...] = mm(to_frame[...], grad_relative.astype(BF16)).reshape(shape)
    grid_value[...] = mm(to_frame[...], value[...]).reshape(shape)
    taps = relative_kernel.ref()

    def convolve(lanes):
        frame_conv(
            grid_grad,
            lambda a, b: taps[EDGE - 1 - a, EDGE - 1 - b : EDGE - b, lanes],
            grid_back,
            EDGE,
            lanes,
        )
        frame_taps(grid_grad, grid_value, head_sums, EDGE, lanes)

    over_lanes(width, convolve, True)
    wide_sums[0:1] = column_sum(projected.astype(F32))
    wide_sums[1:2] = column_sum(grad * unit)
    wide_sums[2:3] = column_sum(grad)
    wide_sums[3:4] = column_sum(cotangent)
    wide_sums[4:8] = jnp.zeros((4, D), F32)
    wide_sums.send()
    grad_query = SCALE * mm_t(attended_low, context[...]) + attended * relative[...]
    grad_context = SCALE * t_mm(query_all.astype(BF16), attended_low)
    grad_context = jnp.where(same_head(width), grad_context, 0.0)
    context_sum = lax.dot_general(
        jnp.ones((8, width), F32),
        grad_context * context[...].astype(F32),
        (((1,), (1,)), ((), ())),
        preferred_element_type=F32,
        precision=lax.Precision.HIGHEST,
    )[0:1]
    grad_context_low = grad_context.astype(BF16)
    weight_all = weight[...]
    grad_key = weight_all * (mm_t(value[...], grad_context_low) - context_sum)
    framed = grid_back[...].reshape(ROWS, width).astype(BF16)
    grad_value = mm(to_token[...], framed) + mm(weight_all.astype(BF16), grad_context_low)
    grad_query = grad_query.astype(BF16)
    grad_value = grad_value.astype(BF16)
    head_sums[49:50] = column_sum(grad_relative)
    head_sums[50:51] = column_sum(grad_query.astype(F32))
    head_sums[51:52] = column_sum(grad_value.astype(F32))
    head_sums[52:56] = jnp.zeros((4, width), F32)
    head_sums.send()
    grad_key = grad_key.astype(BF16)
    if split:
        keep, send = outs[4:]
        core = lax.axis_index("dp") & 1
        for which in range(2):

            @pl.when(core == which)
            def _():
                first, second = (keep, send) if which == 0 else (send, keep)
                first[:, 0:width] = grad_query
                first[:, width:D] = grad_key
                first[:, D:] = jnp.zeros_like(grad_value)
                second[:, 0:D] = projected
                second[:, D:] = grad_value

    else:
        outs[4][...] = projected
    grad_normed = None
    for index, low in enumerate((grad_query, grad_key, grad_value)):
        if not split:
            outs[5][index] = low
        term = mm_t(low, qkv_weight[index])
        grad_normed = term if grad_normed is None else grad_normed + term
    if len(ins) > 15:
        grad_normed_out[0] = grad_normed.astype(BF16)
        grad_normed_out[1] = ins[15][...]
    else:
        grad_normed_out[...] = grad_normed.astype(BF16)


def last_body(scalars, ins, outs, scratch):
    (
        mine,
        other,
        residual,
        gain,
        grad_middle,
        to_frame,
        tokens,
        position_kernel,
        to_token,
        middle,
        mlp_mine,
        down_bias,
    ) = ins[:12]
    block_out, token_grad, sums_out = outs
    grid_grad, grid_in, grid_back, sums = scratch
    unit, inverse = norm_parts(residual[...])
    grad = mine[...].astype(F32) + other[0].astype(F32)
    grad_residual = grad_middle[...] + norm_back(grad, unit, inverse, gain[...])
    grid_grad[...] = mm(to_frame[...], grad_residual.astype(BF16)).reshape(CELLS, SLOTS, D)
    grid_in[...] = mm(to_frame[...], tokens[...]).reshape(CELLS, SLOTS, D)
    taps = position_kernel.ref()
    block_out[...] = (
        middle[...] + (mlp_mine[...].astype(F32) + other[1].astype(F32)) + down_bias[...]
    )
    block_out.send()

    def convolve(lanes):
        frame_conv(
            grid_grad, lambda a, b: taps[2 - a, 2 - b : 3 - b, lanes], grid_back, 3, lanes
        )
        frame_taps(grid_grad, grid_in, sums, 3, lanes)

    over_lanes(D, convolve)
    framed = grid_back[...].reshape(ROWS, D).astype(BF16)
    token_grad[...] = grad_residual + mm(to_token[...], framed)
    token_grad.send()
    sums[9:10] = column_sum(grad_residual)
    sums[10:11] = column_sum(grad * unit)
    sums[11:12] = column_sum(grad)
    sums[12:16] = jnp.zeros((4, D), F32)
    if len(ins) == 12:
        sums_out[...] = sums[0:16]
        return
    here, came = ins[12:]
    total = here[...].astype(F32) + came[...].astype(F32)
    half, width = SMALL // 2, total.shape[1]
    sums[16:, 0:width] = total[0:half]
    sums[16:, width:] = total[half:]
    sums_out[...] = sums[...].astype(BF16)


def turn(values, distance, axis="dp"):
    size = lax.axis_size(axis)
    return lax.ppermute(values, axis, [(i, i ^ distance) for i in range(size)])


def step_bits():
    bits = list(range(1, lax.axis_size("dp").bit_length() - 1))
    return bits, bits[1::-1] + bits[2:]


def step_turn(values, step):
    orders = step_bits()
    size = lax.axis_size("dp")
    return lax.ppermute(values, "dp", [(i, i ^ (1 << orders[i & 1][step])) for i in range(size)])


def step_side(step):
    first, second = step_bits()
    me = lax.axis_index("dp")
    return (me >> jnp.where(me & 1 == 0, first[step], second[step])) & 1


def rows_of(side, count):
    return pl.ds(pl.multiple_of(side * count, 16), count)


def mlp_grads_body(scalars, ins, outs, scratch):
    hidden_width = ins[0].shape[1] - D
    core, side = lax.axis_index("dp") & 1, step_side(0)
    for which in range(2):

        @pl.when(core == which)
        def _():
            for target, place in ((outs[1], 1 - side), (outs[0], side)):
                columns = pl.ds(pl.multiple_of(place * D, 128), D)
                total = None
                for one in ins:
                    wide, narrow = one[:, columns], one[:, hidden_width:]
                    term = t_mm(narrow, wide) if which == 0 else t_mm(wide, narrow)
                    total = term if total is None else total + term
                target[...] = total.astype(BF16)


def attention_grads_body(images, scalars, ins, outs, scratch):
    stay, go = outs
    normed, attended = ins[:images], ins[images : 2 * images]
    far_early = ins[2 * images : 3 * images]
    late = ins[3 * images :]
    normed = [*normed, *far_early]
    width = D // 2

    def attended_of(place):
        return attended[place][...] if place < images else far_early[place - images][:, D:]

    def total(term):
        out = None
        for place in range(2 * images):
            out = term(place) if out is None else out + term(place)
        return out.astype(BF16)

    core, side = lax.axis_index("dp") & 1, step_side(0)

    @pl.when(core == 0)
    def _():
        for target, half in ((go, 1 - side), (stay, side)):
            columns = pl.ds(pl.multiple_of(half * width, 128), width)
            target[...] = total(lambda place: t_mm(normed[place][:, columns], late[place][:, 0:D]))

    for which in range(2):

        @pl.when((core == 1) & (side == which))
        def _():
            first, second = (stay, go) if which == 0 else (go, stay)
            first[...] = total(lambda place: t_mm(attended_of(place), late[place][:, 0:D]))
            for index in range(2):
                columns = slice(index * width, (index + 1) * width)
                second[:, columns] = total(
                    lambda place: t_mm(normed[place][:, columns], late[place][:, D:])
                )


def halve_body(step, scalars, ins, outs, scratch):
    here, came = ins
    here.ref()
    came.ref()
    if len(outs) == 1:
        outs[0][...] = (here[...].astype(F32) + came[...].astype(F32)).astype(BF16)
        return
    stay, go = outs
    count = stay.shape[0]
    side = step_side(step)
    for target, place in ((go, 1 - side), (stay, side)):
        rows = rows_of(place, count)
        target[...] = (here[rows, :].astype(F32) + came[rows, :].astype(F32)).astype(BF16)
        target.send()


def join_body(step, scalars, ins, outs, scratch):
    here, came, *more = ins
    side = step_side(step)
    added = sum(one.shape[0] for one in more)
    extra = 2 * here.shape[0] + added - outs[0].shape[0]
    count = here.shape[0] - extra
    outs[0].held[rows_of(side, count), :] = here[0:count, :]
    outs[0].held[rows_of(1 - side, count), :] = came[0:count, :]
    if extra:
        total = here[count:, :].astype(F32) + came[count:, :].astype(F32)
        outs[0][2 * count : 2 * count + extra, :] = total.astype(BF16)
    place = 2 * count + extra
    for one in more:
        outs[0][place : place + one.shape[0], :] = one[...]
        place += one.shape[0]


def group_body(scalars, ins, outs, scratch):
    head_one, head_two, wide_one, wide_two, bias_one, bias_two = ins
    (rows,) = scratch
    width = rows.shape[1]
    rows[0:50] = head_one[0:50] + head_two[0:50]
    wide = wide_one[0:4] + wide_two[0:4]
    rows[50:54] = wide[:, 0:width]
    rows[54:58] = wide[:, width:]
    bias = bias_one[...] + bias_two[...]
    for piece in range(4):
        rows[58 + piece : 59 + piece] = bias[:, piece * width : (piece + 1) * width]
    rows[62:64] = head_one[50:52] + head_two[50:52]
    outs[0][...] = rows[...].astype(BF16)


def sum_body(scalars, ins, outs, scratch):
    here, came, mine, far = ins
    count = here.shape[0]
    outs[0][0:count, :] = (here[...].astype(F32) + came[...].astype(F32)).astype(BF16)
    first = mine[0:EXTRA, :].astype(F32) + far[0:EXTRA, :].astype(F32)
    outs[0][count:, :] = first.astype(BF16)
    (rows,) = scratch
    member = lax.axis_index("mp")
    half, width = SMALL // 2, D // 2

    def unfolded(one):
        return jnp.concatenate([one[EXTRA:, 0:width], one[EXTRA:, width:]], axis=0).astype(F32)

    own, others = unfolded(mine), unfolded(far)
    rows[:, 0:width] = jnp.where(member == 0, own, others)
    rows[:, width:] = jnp.where(member == 0, others, own)
    rows[50:54, 0:width] = own[50:54]
    rows[50:54, width:] = own[54:58]
    for row in range(2):
        rows[54 + row : 55 + row, 0:width] = own[58 + 2 * row : 59 + 2 * row]
        rows[54 + row : 55 + row, width:] = own[59 + 2 * row : 60 + 2 * row]
    rows[56:57, 0:width] = own[62:63]
    rows[56:57, width:] = own[63:64]
    outs[1][...] = rows[...].astype(BF16)


def mlp_half_body(own, scalars, ins, outs, scratch):
    (block,) = ins
    up, down, wide, tall, sems = scratch
    outs[0][...] = jnp.zeros((8, 128), F32)
    core = lax.axis_index("dp") & 1

    def pieces(source, target, write):
        copies, count = [], source.shape[0] // 4
        for piece in range(4):
            rows = slice(piece * count, (piece + 1) * count)
            write(rows)
            copies.append(
                pltpu.make_async_copy(source.at[rows, :], target.at[rows, :], sems.at[piece])
            )
            copies[-1].start()
        for copy in copies:
            copy.wait()

    @pl.when(core == (0 if own else 1))
    def _():
        def write(rows):
            for tile in range(block.shape[0] // D):
                begin = tile * D + rows.start
                part = block[begin : begin + rows.stop - rows.start, :]
                wide[rows, tile * D : (tile + 1) * D] = part.astype(F32)

        pieces(wide, up, write)

    @pl.when(core == (1 if own else 0))
    def _():
        def write(rows):
            tall[rows, :] = block[rows, :].astype(F32)

        pieces(tall, down, write)


def attention_final_body(scalars, ins, outs, scratch):
    mine, other = ins
    grad_out, position, up_bias, pair_bias, three, five, seven = outs[:7]
    vectors = outs[7:]
    grad_qkv, planes, sems, small, own = scratch
    width = D // 2
    core = lax.axis_index("dp") & 1
    sent = []
    for index in range(3):
        sent.append(pltpu.make_async_copy(planes.at[index], grad_qkv.at[index], sems.at[index]))
    for side in range(2):

        @pl.when(core == side)
        def _():
            first, second = (mine, other) if side == 0 else (other, mine)
            for index in range(2):
                columns = slice(index * width, (index + 1) * width)
                planes[index] = first[0:D, columns].astype(F32)
                sent[index].start()
                planes[2, columns, :] = second[width:D, columns].astype(F32)
            sent[2].start()
            grad_out[...] = second[0:width, :].astype(F32)

    grad_out.send()
    total = mine[D:, :].astype(F32) + other[D:, :].astype(F32)
    own[...] = total[0:EXTRA]
    small[...] = total[EXTRA:]
    for row in range(3):
        position[row] = own[3 * row : 3 * row + 3]
    position.send()
    for place, vector in zip((9, 10, 11), vectors[:3]):
        vector[...] = own[place : place + 1]
    for place, vector in zip((49, 50, 51, 52, 53), vectors[3:]):
        vector[...] = small[place : place + 1]
    for vector in vectors:
        vector.send()
    up_bias[:, 0:D] = small[54:55]
    up_bias[:, D:] = small[55:56]
    up_bias.send()
    pair_bias[0:1] = small[56:57, 0:width]
    pair_bias[1:2] = small[56:57, width:]
    pair_bias.send()
    for row in range(3):
        begin = EDGE * (row + 2) + 2
        three[row] = small[begin : begin + 3, 0:128]
    three.send()
    for row in range(5):
        begin = EDGE * (row + 1) + 1
        five[row] = small[begin : begin + 5, 128:320]
    five.send()
    for row in range(EDGE):
        begin = EDGE * row
        seven[row] = pltpu.roll(small[begin : begin + EDGE, 256:512], 192, 1)[:, 0:192]
    seven.send()
    for copy in sent:
        copy.wait()


def halve(keep, came, step, after=(), us=0.0):
    outs = [((keep.shape[0] // 2, D), BF16)] * 2
    body = functools.partial(halve_body, step)
    keep, send = call(body, outs, (keep, came), us=us, after=after)
    return keep, step_turn(send, step)


def join(keep, came, step, extra=0, more=(), after=(), us=0.0):
    height = (keep.shape[0] - extra) * 2 + extra + sum(one.shape[0] for one in more)
    body = functools.partial(join_body, step)
    return call(body, [((height, D), BF16)], (keep, came, *more), us=us, after=after)[0]


def half_write(own, block, after, fill):
    scratch = [pltpu.VMEM(one.shape, F32) for one in fill] + [pltpu.SemaphoreType.DMA((4,))]
    body = functools.partial(mlp_half_body, own)
    return call(body, [((8, 128), F32)], (block,), scratch, us=0.0, after=after, fill=fill)


def sum_small(values):
    size = lax.axis_size("dp")
    if size & (size - 1):
        return lax.psum(values, "dp")
    for bit in range(size.bit_length() - 1):
        values = values + turn(values, 1 << bit)
    return values


def whole_body(products, scalars, ins, outs, scratch):
    for target, pairs in zip(outs, products):
        total = None
        for left, right in pairs:
            one, two = (ins[i][...] if part is None else ins[i][part] for i, part in (left, right))
            term = t_mm(one, two)
            total = term if total is None else total + term
        target[...] = total.astype(BF16)


def per_device(
    tokens,
    out_grad,
    crop_image,
    crop_res,
    position_kernel,
    position_bias,
    gain_one,
    shift_one,
    qkv_weight,
    query_value_bias,
    relative_three,
    relative_five,
    relative_seven,
    relative_bias,
    output_weight,
    output_bias,
    gain_two,
    shift_two,
    up_weight,
    up_bias,
    down_weight,
    down_bias,
):
    group = lax.axis_size("mp")
    member = lax.axis_index("mp")
    rows = tokens.shape[0]
    width = qkv_weight.shape[2]
    hidden_width = up_weight.shape[1]
    pair = group == 2
    size = lax.axis_size("dp")
    blocks = (
        pair
        and size >= 4
        and size & (size - 1) == 0
        and 2 * width == D
        and hidden_width == 2 * D
        and D % (size * 8) == 0
    )

    def row(vector):
        return vector.reshape(1, -1)

    if not blocks:
        full_kernel = jnp.concatenate(
            [
                jnp.pad(relative_three, ((2, 2), (2, 2), (0, 0))),
                jnp.pad(relative_five, ((1, 1), (1, 1), (0, 0))),
                relative_seven,
            ],
            axis=2,
        )
        kernel_part = lax.dynamic_slice_in_dim(full_kernel, member * width, width, 2)
        bias_part = row(lax.dynamic_slice_in_dim(relative_bias, member * width, width, 0))
    else:
        kernel_part, bias_part = None, row(relative_bias)
    qkv_planes = jnp.transpose(qkv_weight, (1, 0, 2))

    if pair:
        token_list = [tokens, turn(tokens, 1, "mp")]
        images = [lambda: lax.axis_index("mp"), lambda: 1 - lax.axis_index("mp")]
    else:
        token_list = list(lax.all_gather(tokens, "mp", axis=0))
        grad_list = list(lax.all_gather(out_grad, "mp", axis=0))
        images = [functools.partial(int, j) for j in range(group)]

    def own(parts):
        if pair:
            return parts[0]
        return lax.dynamic_index_in_dim(jnp.stack(parts), member, 0, keepdims=False)

    fronts = []
    for index, (image, one) in enumerate(zip(images, token_list)):
        table = blocks and index == 0
        outs = [
            Far((ROWS, rows), BF16),
            Far((rows, ROWS), BF16),
            ((rows, D), F32),
            Far((rows, D), BF16),
            Far((rows, width), F32),
            Far((rows, width), BF16),
            Far((rows, width), F32),
            Far((width, width), BF16),
            Far((rows, width), F32),
            Far((rows, width), BF16),
            ((rows, D), BF16),
        ]
        if blocks:
            outs.append(((rows, D + width), BF16))
        args = [
            crop_res,
            Far(one) if index == 0 else one,
            Far(position_kernel),
            Far(row(position_bias)),
            Far(row(gain_one)),
            Far(row(shift_one)),
            Far(qkv_planes),
            Far(query_value_bias),
        ]
        if table:
            outs += [Far((EDGE, EDGE, width), F32), Far((rows, D), F32)]
            args += [Far(relative_three), Far(relative_five), Far(relative_seven)]
        else:
            args.append(Far(kernel_part))
        args += [Far(bias_part), Far(output_weight)]
        scratch = [pltpu.VMEM((CELLS, SLOTS, D), F32)] * 2
        body = functools.partial(front_body, image, table, blocks)
        if index:
            args = [one.what[0] if isinstance(one, Far) and one.what[0] is not kernel_part else one for one in args]
        bring = (up_weight, down_weight) if pair and index else ()
        us = 5.0 if index else 50.0
        made = call(body, outs, args, scratch, us=us, smem=1, bring=bring)
        if bring:
            up_weight, down_weight = made[-2:]
        if table:
            kernel_part, kept_residual = made[12:14]
        fronts.append(made[: 12 if blocks else 11])
    to_frame, to_token, residual, normed, query, value, weight, context = tuple(zip(*fronts))[:8]
    relative, attended, partial, *early = tuple(zip(*fronts))[8:]

    if pair:
        (ready,) = call(copy_body, [((rows, D), BF16)], partial[:1], us=0.3, after=[token_list[1]])
        first, second = turn(ready, 1, "mp"), turn(partial[1], 1, "mp")
        grad_list, grad_parts = [out_grad, turn(out_grad, 1, "mp")], [None, None]
        addends = [(partial[0], second), (partial[1], first)]
        places = [(None, None), (None, None)]
        order = (1, 0)
        arrived = mark([grad_list[1], partial[1]], ARRIVED)
    else:
        total = lax.psum(jnp.stack(partial), "mp")
        grad_parts = [None] * group
        addends = [(one, jnp.zeros_like(one)) for one in total]
        places = [(None, None)] * group
        order = range(group)
    mlps = [None] * group
    for index in order:
        outs = [Far((rows, D), F32), ((rows, D), BF16), Far((rows, D), BF16)]
        outs.append(Far((1, hidden_width), F32))
        scratch = []
        if blocks:
            outs += [((rows, hidden_width + D), BF16)] * 2
            scratch = [pltpu.VMEM((rows, hidden_width), BF16)] * 2
        else:
            outs += [((rows, hidden_width), BF16)] * 2 + [((rows, D), BF16)]
        args = (
            residual[index],
            *addends[index],
            grad_list[index],
            row(output_bias),
            row(gain_two),
            row(shift_two),
            up_weight,
            row(up_bias.astype(F32)),
            down_weight,
        )
        body = functools.partial(mlp_body, (*places[index], grad_parts[index]), blocks)
        after = []
        if pair:
            after = [mlps[1][1]] if index == 0 else [arrived]
        mlps[index] = call(body, outs, args, scratch, us=2.5, after=after)
    middle, grad_two_part, mlp_part, grad_up_bias, *mlp_rows = zip(*mlps)

    if pair:
        back_addends = [
            (grad_two_part[0], turn(grad_two_part[1], 1, "mp")),
            (grad_two_part[1], turn(grad_two_part[0], 1, "mp")),
        ]
    else:
        total = lax.psum(jnp.stack(grad_two_part), "mp")
        back_addends = [(one, jnp.zeros_like(one)) for one in total]

    steps = len(step_bits()[0])
    if blocks:
        args = (*mlp_rows[0], *(turn(one, 1) for one in mlp_rows[1]))
        after = [mark([back_addends[0][1]], 46.0)]
        mlp_keep, mlp_send = call(mlp_grads_body, [((D, D), BF16)] * 2, args, us=2.0, after=after)
        mlp_came = step_turn(mlp_send, 0)

    backs = []
    for index in range(group):
        carry = pair and index == 1
        outs = [
            Far((rows, D), F32),
            ((2, rows, D) if carry else (rows, D), BF16),
            Far((8, D), F32),
            Far((56, width), F32),
        ]
        if blocks:
            outs += [((rows, D + width), BF16)] * 2
        else:
            outs += [((rows, D), BF16), ((3, rows, width), BF16)]
        args = [
            *back_addends[index],
            grad_list[index],
            middle[index],
            row(gain_two),
            output_weight,
            query[index],
            to_frame[index],
            value[index],
            kernel_part,
            context[index],
            relative[index],
            weight[index],
            to_token[index],
            qkv_planes,
        ]
        if carry:
            args.append(mlp_part[1])
        scratch = [pltpu.VMEM((CELLS, SLOTS, width), F32)] * 3
        body = functools.partial(back_body, (None, None, grad_parts[index]), blocks)
        after = [mlp_keep] if blocks else []
        if pair and index:
            after.append(backs[0][1])
        backs.append(call(body, outs, args, scratch, us=25.0 if index else 0.0, after=after))
    grad_middle, grad_one_part, wide_sums, head_sums, *late = zip(*backs)

    if blocks:
        mlp_keep, mlp_came = halve(mlp_keep, mlp_came, 1, after=[backs[1][1]], us=WEIGHTS["h1"])
        outs = [((width, D), BF16)] * 2
        args = (*normed, *attended, *(turn(one, 1) for one in early[0]))
        args += (*late[0], *(turn(one, 1) for one in late[1]))
        body = functools.partial(attention_grads_body, group)
        keep, send = call(body, outs, args, us=2.0, after=[mlp_keep])
        came = step_turn(send, 0)
        outs = [((SMALL, width), BF16)]
        args = (*head_sums, *wide_sums, *grad_up_bias)
        scratch = [pltpu.VMEM((SMALL, width), F32)]
        (group_sums,) = call(group_body, outs, args, scratch, us=0.0, after=[keep])
        group_came = step_turn(group_sums, steps - 1)
    if not blocks:
        hidden, grad_pre, normed_two = mlp_rows
        grad_projected, grad_qkv = late
        args = (*normed_two, *grad_pre, *hidden, *grad_list)
        args += (*normed, *grad_qkv, *attended, *grad_projected)

        def spot(kind, image, part=None):
            return kind * group + image, part

        each = range(group)
        products = [
            [(spot(0, j), spot(1, j)) for j in each],
            [(spot(2, j), spot(3, j, grad_parts[j])) for j in each],
        ]
        products += [[(spot(4, j), spot(5, j, plane)) for j in each] for plane in range(3)]
        products += [[(spot(6, j), spot(7, j)) for j in each]]
        outs = [((D, hidden_width), BF16), ((hidden_width, D), BF16)]
        outs += [((D, width), BF16)] * 3 + [((width, D), BF16)]
        wholes = call(functools.partial(whole_body, products), outs, args, us=6.0, vmem=40)
        grad_up, grad_down, *planes, grad_out = (lax.psum(one, "dp").astype(F32) for one in wholes)
        grad_qkv_planes = jnp.stack(planes)

    if pair:
        mine, mlp_mine = grad_one_part[0], mlp_part[0]
        other = turn(grad_one_part[1], 1, "mp")
    else:
        sums = [jnp.stack(grad_one_part), jnp.stack(mlp_part)]
        mine, mlp_mine = (lax.psum_scatter(one, "mp", scatter_dimension=0) for one in sums)
        other = jnp.zeros((2, rows, D), BF16)
    outs = [Far((rows, D), F32), Far((rows, D), F32)]
    height = EXTRA + SMALL // 2 if blocks else EXTRA
    outs.append(((height, D), BF16 if blocks else F32))
    args = [
        mine,
        other,
        kept_residual if blocks else own(residual),
        row(gain_one),
        own(grad_middle),
        own(to_frame),
        tokens,
        position_kernel,
        own(to_token),
        own(middle),
        mlp_mine,
        row(down_bias),
    ]
    if blocks:
        args += [group_sums, group_came]
    scratch = [pltpu.VMEM((CELLS, SLOTS, D), F32)] * 3
    scratch.append(pltpu.VMEM((height, D), F32))
    after = []
    if blocks:
        for step in range(2, steps):
            us = WEIGHTS["h2"]
            mlp_keep, mlp_came = halve(mlp_keep, mlp_came, step, after=[keep], us=us)
        keep, came = halve(keep, came, 1, after=[mlp_keep], us=WEIGHTS["p1"])
        after = [keep, mark([group_came, group_sums], HELD)]
    block_out, token_grad, own_sums = call(
        last_body, outs, args, scratch, us=WEIGHTS["last"], after=after
    )

    if blocks:
        far_sums = turn(own_sums, 1, "mp")
        mark_last = own_sums
        for step in range(2, steps):
            keep, came = halve(keep, came, step, after=[mark_last], us=WEIGHTS["p2"])
            mark_last = keep
        outs = [(mlp_keep.shape, BF16)]
        body = functools.partial(halve_body, None)
        args = (mlp_keep, mlp_came)
        (mlp_keep,) = call(body, outs, args, us=WEIGHTS["total"], after=[mark_last])
        mlp_came = step_turn(mlp_keep, steps - 1)
        args = (keep, came, own_sums, far_sums)
        outs = [((keep.shape[0] + EXTRA, D), BF16), ((SMALL, D), BF16)]
        scratch = [pltpu.VMEM((SMALL, D), F32)]
        us = WEIGHTS["pack"]
        keep, small = call(sum_body, outs, args, scratch, us=us, after=[mlp_keep])
        extra, more = EXTRA, [small]
        for step in reversed(range(steps)):
            came = step_turn(keep, step)
            us = WEIGHTS.get(f"j{step}", 0.0)
            mlp_keep = join(mlp_keep, mlp_came, step, after=[keep], us=us)
            mlp_came = step_turn(mlp_keep, step - 1) if step else turn(mlp_keep, 1)
            mark_last = mlp_keep
            if not step:
                shapes = [(D, hidden_width), (hidden_width, D)]
                fill = [jax.ShapeDtypeStruct(shape, F32) for shape in shapes]
                mark_last, grad_up, grad_down = half_write(True, mlp_keep, [], fill)
            us = WEIGHTS.get(f"a{step}", 0.0)
            keep = join(keep, came, step, extra, more, after=[mark_last], us=us)
            extra, more = EXTRA + SMALL, []
        came = turn(keep, 1)
        finished, grad_up, grad_down = half_write(False, mlp_came, [keep], (grad_up, grad_down))
        shapes = [(width, D), (3, 3, D), (1, hidden_width), (2, width)]
        shapes += [relative_three.shape, relative_five.shape, relative_seven.shape]
        outs = [Far(shape, F32) for shape in shapes + [(1, D)] * 8]
        scratch = [pltpu.VMEM((3, D, width), F32), pltpu.SemaphoreType.DMA((3,))]
        scratch += [pltpu.VMEM((SMALL, D), F32), pltpu.VMEM((EXTRA, D), F32)]
        made = call(
            attention_final_body,
            outs,
            (keep, came),
            scratch,
            after=[finished],
            fill=[jax.ShapeDtypeStruct((3, D, width), F32)],
        )
        grad_out, position, up_sum, pair_sum, three, five, seven, *vectors, grad_qkv_planes = made
        vectors = [one.reshape(D) for one in vectors]
        return (
            block_out,
            token_grad,
            position,
            *vectors[0:3],
            jnp.transpose(grad_qkv_planes, (1, 0, 2)),
            pair_sum,
            three,
            five,
            seven,
            vectors[3],
            grad_out,
            *vectors[4:7],
            grad_up,
            up_sum.reshape(hidden_width),
            grad_down,
            vectors[7],
        )

    head_total = functools.reduce(jnp.add, head_sums)
    wide_total = functools.reduce(jnp.add, wide_sums)
    own_total = lax.psum(own_sums[:12], "mp")
    relative_total = lax.all_gather(head_total[:50], "mp", axis=1, tiled=True)
    bias_total = functools.reduce(jnp.add, grad_up_bias)
    pieces = [own_total, wide_total[:4], relative_total]
    private = jnp.concatenate([bias_total.reshape(-1), head_total[50:52].reshape(-1)])
    pieces.append(jnp.pad(private, (0, -private.shape[0] % D)).reshape(-1, D))
    total = sum_small(jnp.concatenate(pieces, axis=0))
    kernel_grad = total[16:65].reshape(EDGE, EDGE, D)
    tail = total[66:].reshape(-1)
    return (
        block_out,
        token_grad,
        total[:9].reshape(3, 3, D),
        total[9],
        total[10],
        total[11],
        jnp.transpose(grad_qkv_planes, (1, 0, 2)),
        tail[hidden_width : hidden_width + 2 * width].reshape(2, width),
        kernel_grad[2:5, 2:5, : 2 * HEAD],
        kernel_grad[1:6, 1:6, 2 * HEAD : 5 * HEAD],
        kernel_grad[:, :, 5 * HEAD :],
        total[65],
        grad_out,
        total[12],
        total[13],
        total[14],
        grad_up,
        tail[:hidden_width],
        grad_down,
        total[15],
    )


def solution(mesh):
    in_specs = (
        P(("dp", "mp"), None),
        P(("dp", "mp"), None),
        P("dp"),
        P("dp"),
        P(),
        P(),
        P(),
        P(),
        P(None, None, "mp"),
        P(None, "mp"),
        P(),
        P(),
        P(),
        P(),
        P("mp", None),
        P(),
        P(),
        P(),
        P(None, "mp"),
        P("mp"),
        P("mp", None),
        P(),
    )
    out_specs = (
        P(("dp", "mp"), None),
        P(("dp", "mp"), None),
        P(),
        P(),
        P(),
        P(),
        P(None, None, "mp"),
        P(None, "mp"),
        P(),
        P(),
        P(),
        P(),
        P("mp", None),
        P(),
        P(),
        P(),
        P(None, "mp"),
        P("mp"),
        P("mp", None),
        P(),
    )
    return jax.shard_map(
        per_device, mesh=mesh, in_specs=in_specs, out_specs=out_specs, check_vma=False
    )
```

```python
import functools
import math

import jax
import jax.numpy as jnp
from jax import lax
from jax.experimental import pallas as pl
from jax.experimental.pallas import tpu as pltpu
from jax.sharding import PartitionSpec as P

HEAD = 64
D = 512
EPSILON = 1e-06
SLOTS = 8
EDGE = 7
CELLS = EDGE * EDGE
ROWS = CELLS * SLOTS
SCALE = HEAD ** (-0.5)
SMALL = 64
EXTRA = 16
HELD = 60.0
ARRIVED = 46.0
WEIGHTS = dict(
    h1=0.0, h2=0.0, p1=40.0, last=0.0, p2=0.0, total=0.0, pack=40.0, j2=0.0, a2=0.0, j1=0.0, a1=40.0, j0=0.0, a0=40.0
)
BF16 = jnp.bfloat16
F32 = jnp.float32


def mm(left, right):
    return jnp.dot(left, right, preferred_element_type=F32)


def mm_t(left, right):
    return lax.dot_general(left, right, (((1,), (1,)), ((), ())), preferred_element_type=F32)


def t_mm(left, right):
    return lax.dot_general(left, right, (((0,), (0,)), ((), ())), preferred_element_type=F32)


def split_mm(onehot, values):
    high = values.astype(BF16)
    low = (values - high.astype(F32)).astype(BF16)
    return mm(onehot, high) + mm(onehot, low)


class Source:
    def __init__(self, ref, copy=None):
        self.held, self.copy, self.shape = ref, copy, ref.shape

    def ref(self):
        if self.copy is not None:
            self.copy.wait()
            self.copy = None
        return self.held

    def __getitem__(self, index):
        return self.ref()[index]


class Result:
    def __init__(self, ref, copy=None):
        self.held, self.copy, self.sent, self.shape = ref, copy, copy is None, ref.shape

    def __setitem__(self, index, value):
        self.held[index] = value

    def __getitem__(self, index):
        return self.held[index]

    def send(self):
        if not self.sent:
            self.copy.start()
            self.sent = True


class Far:
    def __init__(self, *what):
        self.what = what


def call(body, outs, args, scratch=(), us=3.0, smem=0, vmem=24, after=(), bring=(), fill=()):
    far_in = [isinstance(one, Far) for one in args[smem:]]
    far_out = [isinstance(one, Far) for one in outs]
    arrays = [one.what[0] if isinstance(one, Far) else one for one in args[smem:]]
    outs = [one.what if isinstance(one, Far) else one for one in outs]
    filled_in = [one for one in fill if not isinstance(one, jax.ShapeDtypeStruct)]

    def kernel(*refs):
        refs = list(refs)

        def take(count):
            taken = refs[:count]
            del refs[:count]
            return taken

        far_scalars, given = take(smem), take(len(arrays))
        distant, _ = take(len(bring)), take(len(after) + len(filled_in))
        places, brought, filled = take(len(outs)), take(len(bring)), take(len(fill))
        near_scalars = take(smem)
        scalar_sems = take(1)[0] if smem else None
        near_in, near_out = take(sum(far_in)), take(sum(far_out))
        scalars = []
        for index, (away, near) in enumerate(zip(far_scalars, near_scalars)):
            copy = pltpu.make_async_copy(away, near, scalar_sems.at[index])
            copy.start()
            scalars.append(Source(near, copy))
        in_sems = take(1)[0] if any(far_in) else None
        out_sems = take(1)[0] if any(far_out) else None
        bring_sems = take(1)[0] if bring else None
        ins, made, moves = [], [], []
        for ref, far in zip(given, far_in):
            if far:
                index = sum(one.copy is not None for one in ins)
                copy = pltpu.make_async_copy(ref, near_in[index], in_sems.at[index])
                copy.start()
                ins.append(Source(near_in[index], copy))
            else:
                ins.append(Source(ref))
        for index, (source, target) in enumerate(zip(distant, brought)):
            moves.append(pltpu.make_async_copy(source, target, bring_sems.at[index]))
            moves[-1].start()
        for ref, far in zip(places, far_out):
            if far:
                index = sum(one.copy is not None for one in made)
                copy = pltpu.make_async_copy(near_out[index], ref, out_sems.at[index])
                made.append(Result(near_out[index], copy))
            else:
                made.append(Result(ref))
        body(scalars, ins, made, filled + refs)
        for one in made:
            one.send()
        for one in scalars + ins:
            one.ref()
        for one in made:
            if one.copy is not None:
                one.copy.wait()
        for copy in moves:
            copy.wait()

    shapes = [pltpu.SMEM(one.shape, one.dtype) for one in args[:smem]]
    if smem:
        shapes.append(pltpu.SemaphoreType.DMA((smem,)))
    shapes += [pltpu.VMEM(one.shape, one.dtype) for one, far in zip(arrays, far_in) if far]
    shapes += [pltpu.VMEM(*one) for one, far in zip(outs, far_out) if far]
    if any(far_in):
        shapes.append(pltpu.SemaphoreType.DMA((sum(far_in),)))
    if any(far_out):
        shapes.append(pltpu.SemaphoreType.DMA((sum(far_out),)))
    if bring:
        shapes.append(pltpu.SemaphoreType.DMA((len(bring),)))
    near, far = pl.BlockSpec(memory_space=pltpu.VMEM), pl.BlockSpec(memory_space=pltpu.HBM)
    operands = [
        pltpu.with_memory_space_constraint(one, pltpu.HBM) if away else one
        for one, away in zip(arrays, far_in)
    ]
    brought_far = [pltpu.with_memory_space_constraint(one, pltpu.HBM) for one in bring]
    scalars_far = [pltpu.with_memory_space_constraint(one, pltpu.HBM) for one in args[:smem]]
    return pl.pallas_call(
        kernel,
        out_shape=[
            pltpu.HBM(*one) if away else jax.ShapeDtypeStruct(*one)
            for one, away in zip(outs, far_out)
        ]
        + [jax.ShapeDtypeStruct(one.shape, one.dtype) for one in bring]
        + [pltpu.HBM(one.shape, one.dtype) for one in fill],
        in_specs=[far] * smem
        + [far if away else near for away in far_in]
        + [far] * len(bring)
        + [pl.BlockSpec(memory_space=pl.ANY)] * len(after)
        + [far] * len(filled_in),
        out_specs=[far if away else near for away in far_out]
        + [near] * len(bring)
        + [far] * len(fill),
        input_output_aliases={
            len(args) + len(bring) + len(after) + index: len(outs) + len(bring) + index
            for index in range(len(filled_in))
        },
        scratch_shapes=shapes + list(scratch),
        compiler_params=pltpu.CompilerParams(vmem_limit_bytes=vmem << 20),
        cost_estimate=pl.CostEstimate(
            flops=int(us * 1.0e8), bytes_accessed=1 << 12, transcendentals=0
        ),
    )(*scalars_far, *operands, *brought_far, *after, *filled_in)


def over_lanes(width, body, unroll=False):
    if width % 128:
        body(slice(0, width))
    elif unroll:
        for begin in range(0, width, 128):
            body(slice(begin, begin + 128))
    else:

        @pl.loop(0, width // 128)
        def _(step):
            body(pl.ds(pl.multiple_of(step * 128, 128), 128))


def frame_conv(source, tap, target, edge, lanes):
    half = (edge - 1) // 2
    for i in range(EDGE):
        total = [None] * EDGE
        for a in range(edge):
            row = i + a - half
            if not 0 <= row < EDGE:
                continue
            cells = [source[row * EDGE + j, :, lanes] for j in range(EDGE)]
            for b in range(edge):
                weight = tap(a, b)
                for j in range(EDGE):
                    column = j + b - half
                    if 0 <= column < EDGE:
                        term = cells[column] * weight
                        total[j] = term if total[j] is None else total[j] + term
        for j in range(EDGE):
            target[i * EDGE + j, :, lanes] = total[j]


def frame_taps(grad, source, target, edge, lanes):
    half = (edge - 1) // 2
    for a in range(edge):
        total = [None] * edge
        for i in range(EDGE):
            row = i + a - half
            if not 0 <= row < EDGE:
                continue
            cells = [source[row * EDGE + j, :, lanes] for j in range(EDGE)]
            for j in range(EDGE):
                own = grad[i * EDGE + j, :, lanes]
                for b in range(edge):
                    column = j + b - half
                    if 0 <= column < EDGE:
                        term = own * cells[column]
                        total[b] = term if total[b] is None else total[b] + term
        for b in range(edge):
            row = a * edge + b
            target[row : row + 1, lanes] = jnp.sum(total[b], axis=0, keepdims=True)


def crop_frames(kinds, base, rows):
    sub = lax.broadcasted_iota(jnp.int32, (SLOTS, rows), 0)
    lane = lax.broadcasted_iota(jnp.int32, (SLOTS, rows), 1)
    place = lax.broadcasted_iota(jnp.int32, (8, ROWS), 1)
    slot = place & (SLOTS - 1)
    cell = place >> 3
    down = (cell * 37) >> 8
    across = cell - down * EDGE
    begin = jnp.zeros((SLOTS, rows), jnp.int32)
    whole = jnp.zeros((SLOTS, rows), jnp.int32)
    begin_row = jnp.zeros((8, ROWS), jnp.int32)
    whole_row = jnp.zeros((8, ROWS), jnp.int32)
    start = jnp.int32(0)
    for s in range(SLOTS):
        large = (kinds[base + s] == 0).astype(jnp.int32)
        begin = jnp.where(sub == s, start, begin)
        whole = jnp.where(sub == s, large, whole)
        begin_row = jnp.where(slot == s, start, begin_row)
        whole_row = jnp.where(slot == s, large, whole_row)
        start = start + 9 + 40 * large
    tiles = []
    for i in range(EDGE):
        for j in range(EDGE):
            small = begin + (i * 3 + j) if i < 3 and j < 3 else jnp.full_like(begin, -1)
            token = jnp.where(whole == 1, begin + (i * EDGE + j), small)
            tiles.append(jnp.where(token == lane, 1.0, 0.0))
    to_frame = jnp.concatenate(tiles, axis=0).astype(BF16)
    corner = jnp.where((down < 3) & (across < 3), begin_row + down * 3 + across, -1)
    token_row = jnp.where(whole_row == 1, begin_row + cell, corner)
    height = lax.broadcasted_iota(jnp.int32, (rows, ROWS), 0)
    to_token = jnp.where(height == token_row[0:1], 1.0, 0.0).astype(BF16)
    return to_frame, to_token


def norm_parts(values):
    average = jnp.mean(values, axis=-1, keepdims=True)
    centred = values - average
    variance = jnp.mean(centred * centred, axis=-1, keepdims=True)
    inverse = lax.rsqrt(variance + EPSILON)
    return centred * inverse, inverse


def norm_back(grad, unit, inverse, gain):
    scaled = grad * gain
    first = jnp.mean(scaled, axis=-1, keepdims=True)
    second = jnp.mean(scaled * unit, axis=-1, keepdims=True)
    return (scaled - first - unit * second) * inverse


def column_sum(values):
    return jnp.sum(values, axis=0, keepdims=True)


def same_head(width):
    rows = lax.broadcasted_iota(jnp.int32, (width, width), 0) // HEAD
    columns = lax.broadcasted_iota(jnp.int32, (width, width), 1) // HEAD
    return rows == columns


def tap_table(member, three, five, seven, table):
    table[...] = jnp.zeros(table.shape, F32)

    @pl.when(member == 0)
    def _():
        table[2:5, 2:5, 0:128] = three[...]
        for row in range(5):
            table[1 + row, 1:6, 128:256] = five[row, :, 0:128]

    @pl.when(member == 1)
    def _():
        for row in range(5):
            table[1 + row, 1:6, 0:64] = five[row, :, 128:192]
        lane = lax.broadcasted_iota(jnp.int32, (EDGE, 128), 1)
        for row in range(EDGE):
            near = pltpu.roll(seven[row, :, 0:128], 64, 1)
            wide = jnp.concatenate([seven[row, :, 128:192], jnp.zeros((EDGE, 64), F32)], axis=1)
            far = pltpu.roll(wide, 64, 1)
            table[row, :, 0:128] = jnp.where(lane < 64, table[row, :, 0:128], near)
            table[row, :, 128:256] = jnp.where(lane < 64, near, far)


def front_body(image, table, early, scalars, ins, outs, scratch):
    (kinds,) = scalars
    tokens, position_kernel, position_bias, gain, shift, qkv_weight, pair_bias = ins[:7]
    relative_bias, output_weight = ins[-2:]
    (
        to_frame_out,
        to_token_out,
        residual_out,
        normed_out,
        query_out,
        value_out,
        weight_out,
        context_out,
        relative_out,
        attended_out,
        partial_out,
    ) = outs[:11]
    grid_in, grid_out = scratch
    rows = tokens.shape[0]
    width = output_weight.shape[0]
    member = lax.axis_index("mp")
    to_frame, to_token = crop_frames(kinds, image() * SLOTS, rows)
    to_frame_out[...] = to_frame
    to_frame_out.send()
    to_token_out[...] = to_token
    to_token_out.send()
    grid_in[...] = mm(to_frame, tokens[...]).reshape(CELLS, SLOTS, D)
    position_taps = position_kernel.ref()

    def position(lanes):
        frame_conv(grid_in, lambda a, b: position_taps[a, b : b + 1, lanes], grid_out, 3, lanes)

    over_lanes(D, position)
    residual = tokens[...].astype(F32) + split_mm(to_token, grid_out[...].reshape(ROWS, D))
    residual = residual + position_bias[...]
    residual_out[...] = residual
    if table:
        outs[13][...] = residual
        outs[13].send()
    unit, _ = norm_parts(residual)
    normed = (unit * gain[...] + shift[...]).astype(BF16)
    normed_out[...] = normed
    normed_out.send()
    pair = pair_bias[...].astype(F32)
    value = (mm(normed, qkv_weight[2]) + pair[1:2]).astype(BF16)
    value_out[...] = value
    value_out.send()
    grid_in[:, :, 0:width] = mm(to_frame, value).reshape(CELLS, SLOTS, width)
    query = mm(normed, qkv_weight[0]) + pair[0:1]
    query_out[...] = query
    query_out.send()
    keys = mm(normed, qkv_weight[1])
    weight = jnp.exp(keys - jnp.max(keys, axis=0, keepdims=True))
    weight = weight / column_sum(weight)
    weight_out[...] = weight
    weight_out.send()
    context = jnp.where(same_head(width), t_mm(weight.astype(BF16), value), 0.0).astype(BF16)
    context_out[...] = context
    context_out.send()
    if table:
        relative_kernel = outs[12]
        for one in ins[7:10]:
            one.ref()
        tap_table(member, *ins[7:10], relative_kernel.held)
        relative_kernel.send()
        relative_taps = relative_kernel.held
    else:
        relative_taps = ins[7].ref()

    def relative(lanes):
        frame_conv(
            grid_in, lambda a, b: relative_taps[a, b : b + 1, lanes], grid_out, EDGE, lanes
        )

    over_lanes(width, relative)
    if relative_bias.shape[1] == width:
        bias_row = relative_bias[...]
    else:
        bias_row = relative_bias[:, pl.ds(pl.multiple_of(member * width, 128), width)]
    framed = grid_out[:, :, 0:width].reshape(ROWS, width).astype(BF16)
    position_term = mm(to_token, framed) + bias_row
    relative_out[...] = position_term
    relative_out.send()
    attended = SCALE * mm(query.astype(BF16), context) + query * position_term
    attended = attended.astype(BF16)
    attended_out[...] = attended
    attended_out.send()
    if early:
        outs[11][:, 0:D] = normed
        outs[11][:, D:] = attended
    partial_out[...] = mm(attended, output_weight[...]).astype(BF16)


def mark(arrays, us):
    def body(scalars, ins, outs, scratch):
        outs[0][...] = jnp.zeros((8, 128), F32)

    return call(body, [((8, 128), F32)], (), us=us, after=arrays)[0]


def copy_body(scalars, ins, outs, scratch):
    outs[0][...] = ins[0][...]


def picked(source, part):
    return source[...] if part is None else source[part]


def mlp_body(parts, split, scalars, ins, outs, scratch):
    (
        residual,
        first,
        second,
        cotangent,
        output_bias,
        gain,
        shift,
        up_weight,
        up_bias,
        down_weight,
    ) = ins
    middle_out, grad_normed_out, mlp_out, grad_bias_out = outs[:4]
    hidden_out, grad_pre_out = scratch if split else outs[4:6]
    hidden_width = up_weight.shape[1]
    projected = picked(first, parts[0]).astype(F32) + picked(second, parts[1]).astype(F32)
    middle = residual[...] + projected + output_bias[...]
    middle_out[...] = middle
    middle_out.send()
    unit, _ = norm_parts(middle)
    normed = (unit * gain[...] + shift[...]).astype(BF16)
    out_grad = picked(cotangent, parts[2])
    step = min(256, hidden_width)
    for begin in range(0, hidden_width, step):
        part = slice(begin, begin + step)
        pre = mm(normed, up_weight[:, part]) + up_bias[:, part]
        below = 0.5 * (1.0 + lax.erf(pre * (2.0**-0.5)))
        hidden_out[:, part] = (pre * below).astype(BF16)
        slope = below + pre * jnp.exp(-0.5 * pre * pre) * ((2.0 * math.pi) ** -0.5)
        grad = (mm_t(out_grad, down_weight[part, :]) * slope).astype(BF16)
        grad_pre_out[:, part] = grad
        grad_bias_out[:, part] = column_sum(grad.astype(F32))
    grad_bias_out.send()
    mlp_out[...] = mm(hidden_out[...], down_weight[...]).astype(BF16)
    mlp_out.send()
    grad_normed_out[...] = mm_t(grad_pre_out[...], up_weight[...]).astype(BF16)
    if not split:
        outs[6][...] = normed
        return
    keep, send = outs[4:6]
    core = lax.axis_index("dp") & 1
    for side in range(2):

        @pl.when(core == side)
        def _():
            up, down = (keep, send) if side == 0 else (send, keep)
            up[:, 0:hidden_width] = grad_pre_out[...]
            up[:, hidden_width:] = normed
            down[:, 0:hidden_width] = hidden_out[...]
            down[:, hidden_width:] = out_grad


def back_body(parts, split, scalars, ins, outs, scratch):
    (
        mine,
        other,
        out_grad,
        middle,
        gain,
        output_weight,
        query,
        to_frame,
        value,
        relative_kernel,
        context,
        relative,
        weight,
        to_token,
        qkv_weight,
    ) = ins[:15]
    grad_middle_out, grad_normed_out, wide_sums, head_sums = outs[:4]
    grid_grad, grid_value, grid_back = scratch
    width = relative_kernel.shape[2]
    unit, inverse = norm_parts(middle[...])
    grad = picked(mine, parts[0]).astype(F32) + picked(other, parts[1]).astype(F32)
    cotangent = picked(out_grad, parts[2]).astype(F32)
    grad_middle = cotangent + norm_back(grad, unit, inverse, gain[...])
    grad_middle_out[...] = grad_middle
    grad_middle_out.send()
    projected = grad_middle.astype(BF16)
    attended = mm_t(projected, output_weight[...])
    attended_low = attended.astype(BF16)
    query_all = query[...]
    grad_relative = attended * query_all
    shape = (CELLS, SLOTS, width)
    grid_grad[...] = mm(to_frame[...], grad_relative.astype(BF16)).reshape(shape)
    grid_value[...] = mm(to_frame[...], value[...]).reshape(shape)
    taps = relative_kernel.ref()

    def convolve(lanes):
        frame_conv(
            grid_grad,
            lambda a, b: taps[EDGE - 1 - a, EDGE - 1 - b : EDGE - b, lanes],
            grid_back,
            EDGE,
            lanes,
        )
        frame_taps(grid_grad, grid_value, head_sums, EDGE, lanes)

    over_lanes(width, convolve, True)
    wide_sums[0:1] = column_sum(projected.astype(F32))
    wide_sums[1:2] = column_sum(grad * unit)
    wide_sums[2:3] = column_sum(grad)
    wide_sums[3:4] = column_sum(cotangent)
    wide_sums[4:8] = jnp.zeros((4, D), F32)
    wide_sums.send()
    grad_query = SCALE * mm_t(attended_low, context[...]) + attended * relative[...]
    grad_context = SCALE * t_mm(query_all.astype(BF16), attended_low)
    grad_context = jnp.where(same_head(width), grad_context, 0.0)
    context_sum = lax.dot_general(
        jnp.ones((8, width), F32),
        grad_context * context[...].astype(F32),
        (((1,), (1,)), ((), ())),
        preferred_element_type=F32,
        precision=lax.Precision.HIGHEST,
    )[0:1]
    grad_context_low = grad_context.astype(BF16)
    weight_all = weight[...]
    grad_key = weight_all * (mm_t(value[...], grad_context_low) - context_sum)
    framed = grid_back[...].reshape(ROWS, width).astype(BF16)
    grad_value = mm(to_token[...], framed) + mm(weight_all.astype(BF16), grad_context_low)
    grad_query = grad_query.astype(BF16)
    grad_value = grad_value.astype(BF16)
    head_sums[49:50] = column_sum(grad_relative)
    head_sums[50:51] = column_sum(grad_query.astype(F32))
    head_sums[51:52] = column_sum(grad_value.astype(F32))
    head_sums[52:56] = jnp.zeros((4, width), F32)
    head_sums.send()
    grad_key = grad_key.astype(BF16)
    if split:
        keep, send = outs[4:]
        core = lax.axis_index("dp") & 1
        for which in range(2):

            @pl.when(core == which)
            def _():
                first, second = (keep, send) if which == 0 else (send, keep)
                first[:, 0:width] = grad_query
                first[:, width:D] = grad_key
                first[:, D:] = jnp.zeros_like(grad_value)
                second[:, 0:D] = projected
                second[:, D:] = grad_value

    else:
        outs[4][...] = projected
    grad_normed = None
    for index, low in enumerate((grad_query, grad_key, grad_value)):
        if not split:
            outs[5][index] = low
        term = mm_t(low, qkv_weight[index])
        grad_normed = term if grad_normed is None else grad_normed + term
    if len(ins) > 15:
        grad_normed_out[0] = grad_normed.astype(BF16)
        grad_normed_out[1] = ins[15][...]
    else:
        grad_normed_out[...] = grad_normed.astype(BF16)


def last_body(scalars, ins, outs, scratch):
    (
        mine,
        other,
        residual,
        gain,
        grad_middle,
        to_frame,
        tokens,
        position_kernel,
        to_token,
        middle,
        mlp_mine,
        down_bias,
    ) = ins[:12]
    block_out, token_grad, sums_out = outs
    grid_grad, grid_in, grid_back, sums = scratch
    unit, inverse = norm_parts(residual[...])
    grad = mine[...].astype(F32) + other[0].astype(F32)
    grad_residual = grad_middle[...] + norm_back(grad, unit, inverse, gain[...])
    grid_grad[...] = mm(to_frame[...], grad_residual.astype(BF16)).reshape(CELLS, SLOTS, D)
    grid_in[...] = mm(to_frame[...], tokens[...]).reshape(CELLS, SLOTS, D)
    taps = position_kernel.ref()
    block_out[...] = (
        middle[...] + (mlp_mine[...].astype(F32) + other[1].astype(F32)) + down_bias[...]
    )
    block_out.send()

    def convolve(lanes):
        frame_conv(
            grid_grad, lambda a, b: taps[2 - a, 2 - b : 3 - b, lanes], grid_back, 3, lanes
        )
        frame_taps(grid_grad, grid_in, sums, 3, lanes)

    over_lanes(D, convolve)
    framed = grid_back[...].reshape(ROWS, D).astype(BF16)
    token_grad[...] = grad_residual + mm(to_token[...], framed)
    token_grad.send()
    sums[9:10] = column_sum(grad_residual)
    sums[10:11] = column_sum(grad * unit)
    sums[11:12] = column_sum(grad)
    sums[12:16] = jnp.zeros((4, D), F32)
    if len(ins) == 12:
        sums_out[...] = sums[0:16]
        return
    here, came = ins[12:]
    total = here[...].astype(F32) + came[...].astype(F32)
    half, width = SMALL // 2, total.shape[1]
    sums[16:, 0:width] = total[0:half]
    sums[16:, width:] = total[half:]
    sums_out[...] = sums[...].astype(BF16)


def turn(values, distance, axis="dp"):
    size = lax.axis_size(axis)
    return lax.ppermute(values, axis, [(i, i ^ distance) for i in range(size)])


def step_bits():
    bits = list(range(1, lax.axis_size("dp").bit_length() - 1))
    return bits, bits[1::-1] + bits[2:]


def step_turn(values, step):
    orders = step_bits()
    size = lax.axis_size("dp")
    return lax.ppermute(values, "dp", [(i, i ^ (1 << orders[i & 1][step])) for i in range(size)])


def step_side(step):
    first, second = step_bits()
    me = lax.axis_index("dp")
    return (me >> jnp.where(me & 1 == 0, first[step], second[step])) & 1


def rows_of(side, count):
    return pl.ds(pl.multiple_of(side * count, 16), count)


def mlp_grads_body(scalars, ins, outs, scratch):
    hidden_width = ins[0].shape[1] - D
    core, side = lax.axis_index("dp") & 1, step_side(0)
    for which in range(2):

        @pl.when(core == which)
        def _():
            for target, place in ((outs[1], 1 - side), (outs[0], side)):
                columns = pl.ds(pl.multiple_of(place * D, 128), D)
                total = None
                for one in ins:
                    wide, narrow = one[:, columns], one[:, hidden_width:]
                    term = t_mm(narrow, wide) if which == 0 else t_mm(wide, narrow)
                    total = term if total is None else total + term
                target[...] = total.astype(BF16)


def attention_grads_body(images, scalars, ins, outs, scratch):
    stay, go = outs
    normed, attended = ins[:images], ins[images : 2 * images]
    far_early = ins[2 * images : 3 * images]
    late = ins[3 * images :]
    normed = [*normed, *far_early]
    width = D // 2

    def attended_of(place):
        return attended[place][...] if place < images else far_early[place - images][:, D:]

    def total(term):
        out = None
        for place in range(2 * images):
            out = term(place) if out is None else out + term(place)
        return out.astype(BF16)

    core, side = lax.axis_index("dp") & 1, step_side(0)

    @pl.when(core == 0)
    def _():
        for target, half in ((go, 1 - side), (stay, side)):
            columns = pl.ds(pl.multiple_of(half * width, 128), width)
            target[...] = total(lambda place: t_mm(normed[place][:, columns], late[place][:, 0:D]))

    for which in range(2):

        @pl.when((core == 1) & (side == which))
        def _():
            first, second = (stay, go) if which == 0 else (go, stay)
            first[...] = total(lambda place: t_mm(attended_of(place), late[place][:, 0:D]))
            for index in range(2):
                columns = slice(index * width, (index + 1) * width)
                second[:, columns] = total(
                    lambda place: t_mm(normed[place][:, columns], late[place][:, D:])
                )


def halve_body(step, scalars, ins, outs, scratch):
    here, came = ins
    here.ref()
    came.ref()
    if len(outs) == 1:
        outs[0][...] = (here[...].astype(F32) + came[...].astype(F32)).astype(BF16)
        return
    stay, go = outs
    count = stay.shape[0]
    side = step_side(step)
    for target, place in ((go, 1 - side), (stay, side)):
        rows = rows_of(place, count)
        target[...] = (here[rows, :].astype(F32) + came[rows, :].astype(F32)).astype(BF16)
        target.send()


def join_body(step, scalars, ins, outs, scratch):
    here, came, *more = ins
    side = step_side(step)
    added = sum(one.shape[0] for one in more)
    extra = 2 * here.shape[0] + added - outs[0].shape[0]
    count = here.shape[0] - extra
    outs[0].held[rows_of(side, count), :] = here[0:count, :]
    outs[0].held[rows_of(1 - side, count), :] = came[0:count, :]
    if extra:
        total = here[count:, :].astype(F32) + came[count:, :].astype(F32)
        outs[0][2 * count : 2 * count + extra, :] = total.astype(BF16)
    place = 2 * count + extra
    for one in more:
        outs[0][place : place + one.shape[0], :] = one[...]
        place += one.shape[0]


def group_body(scalars, ins, outs, scratch):
    head_one, head_two, wide_one, wide_two, bias_one, bias_two = ins
    (rows,) = scratch
    width = rows.shape[1]
    rows[0:50] = head_one[0:50] + head_two[0:50]
    wide = wide_one[0:4] + wide_two[0:4]
    rows[50:54] = wide[:, 0:width]
    rows[54:58] = wide[:, width:]
    bias = bias_one[...] + bias_two[...]
    for piece in range(4):
        rows[58 + piece : 59 + piece] = bias[:, piece * width : (piece + 1) * width]
    rows[62:64] = head_one[50:52] + head_two[50:52]
    outs[0][...] = rows[...].astype(BF16)


def sum_body(scalars, ins, outs, scratch):
    here, came, mine, far = ins
    count = here.shape[0]
    outs[0][0:count, :] = (here[...].astype(F32) + came[...].astype(F32)).astype(BF16)
    first = mine[0:EXTRA, :].astype(F32) + far[0:EXTRA, :].astype(F32)
    outs[0][count:, :] = first.astype(BF16)
    (rows,) = scratch
    member = lax.axis_index("mp")
    half, width = SMALL // 2, D // 2

    def unfolded(one):
        return jnp.concatenate([one[EXTRA:, 0:width], one[EXTRA:, width:]], axis=0).astype(F32)

    own, others = unfolded(mine), unfolded(far)
    rows[:, 0:width] = jnp.where(member == 0, own, others)
    rows[:, width:] = jnp.where(member == 0, others, own)
    rows[50:54, 0:width] = own[50:54]
    rows[50:54, width:] = own[54:58]
    for row in range(2):
        rows[54 + row : 55 + row, 0:width] = own[58 + 2 * row : 59 + 2 * row]
        rows[54 + row : 55 + row, width:] = own[59 + 2 * row : 60 + 2 * row]
    rows[56:57, 0:width] = own[62:63]
    rows[56:57, width:] = own[63:64]
    outs[1][...] = rows[...].astype(BF16)


def mlp_half_body(own, scalars, ins, outs, scratch):
    (block,) = ins
    up, down, wide, tall, sems = scratch
    outs[0][...] = jnp.zeros((8, 128), F32)
    core = lax.axis_index("dp") & 1

    def pieces(source, target, write):
        copies, count = [], source.shape[0] // 4
        for piece in range(4):
            rows = slice(piece * count, (piece + 1) * count)
            write(rows)
            copies.append(
                pltpu.make_async_copy(source.at[rows, :], target.at[rows, :], sems.at[piece])
            )
            copies[-1].start()
        for copy in copies:
            copy.wait()

    @pl.when(core == (0 if own else 1))
    def _():
        def write(rows):
            for tile in range(block.shape[0] // D):
                begin = tile * D + rows.start
                part = block[begin : begin + rows.stop - rows.start, :]
                wide[rows, tile * D : (tile + 1) * D] = part.astype(F32)

        pieces(wide, up, write)

    @pl.when(core == (1 if own else 0))
    def _():
        def write(rows):
            tall[rows, :] = block[rows, :].astype(F32)

        pieces(tall, down, write)


def attention_final_body(scalars, ins, outs, scratch):
    mine, other = ins
    grad_out, position, up_bias, pair_bias, three, five, seven = outs[:7]
    vectors = outs[7:]
    grad_qkv, planes, sems, small, own = scratch
    width = D // 2
    core = lax.axis_index("dp") & 1
    sent = []
    for index in range(3):
        sent.append(pltpu.make_async_copy(planes.at[index], grad_qkv.at[index], sems.at[index]))
    for side in range(2):

        @pl.when(core == side)
        def _():
            first, second = (mine, other) if side == 0 else (other, mine)
            for index in range(2):
                columns = slice(index * width, (index + 1) * width)
                planes[index] = first[0:D, columns].astype(F32)
                sent[index].start()
                planes[2, columns, :] = second[width:D, columns].astype(F32)
            sent[2].start()
            grad_out[...] = second[0:width, :].astype(F32)

    grad_out.send()
    total = mine[D:, :].astype(F32) + other[D:, :].astype(F32)
    own[...] = total[0:EXTRA]
    small[...] = total[EXTRA:]
    for row in range(3):
        position[row] = own[3 * row : 3 * row + 3]
    position.send()
    for place, vector in zip((9, 10, 11), vectors[:3]):
        vector[...] = own[place : place + 1]
    for place, vector in zip((49, 50, 51, 52, 53), vectors[3:]):
        vector[...] = small[place : place + 1]
    for vector in vectors:
        vector.send()
    up_bias[:, 0:D] = small[54:55]
    up_bias[:, D:] = small[55:56]
    up_bias.send()
    pair_bias[0:1] = small[56:57, 0:width]
    pair_bias[1:2] = small[56:57, width:]
    pair_bias.send()
    for row in range(3):
        begin = EDGE * (row + 2) + 2
        three[row] = small[begin : begin + 3, 0:128]
    three.send()
    for row in range(5):
        begin = EDGE * (row + 1) + 1
        five[row] = small[begin : begin + 5, 128:320]
    five.send()
    for row in range(EDGE):
        begin = EDGE * row
        seven[row] = pltpu.roll(small[begin : begin + EDGE, 256:512], 192, 1)[:, 0:192]
    seven.send()
    for copy in sent:
        copy.wait()


def halve(keep, came, step, after=(), us=0.0):
    outs = [((keep.shape[0] // 2, D), BF16)] * 2
    body = functools.partial(halve_body, step)
    keep, send = call(body, outs, (keep, came), us=us, after=after)
    return keep, step_turn(send, step)


def join(keep, came, step, extra=0, more=(), after=(), us=0.0):
    height = (keep.shape[0] - extra) * 2 + extra + sum(one.shape[0] for one in more)
    body = functools.partial(join_body, step)
    return call(body, [((height, D), BF16)], (keep, came, *more), us=us, after=after)[0]


def half_write(own, block, after, fill):
    scratch = [pltpu.VMEM(one.shape, F32) for one in fill] + [pltpu.SemaphoreType.DMA((4,))]
    body = functools.partial(mlp_half_body, own)
    return call(body, [((8, 128), F32)], (block,), scratch, us=0.0, after=after, fill=fill)


def sum_small(values):
    size = lax.axis_size("dp")
    if size & (size - 1):
        return lax.psum(values, "dp")
    for bit in range(size.bit_length() - 1):
        values = values + turn(values, 1 << bit)
    return values


def whole_body(products, scalars, ins, outs, scratch):
    for target, pairs in zip(outs, products):
        total = None
        for left, right in pairs:
            one, two = (ins[i][...] if part is None else ins[i][part] for i, part in (left, right))
            term = t_mm(one, two)
            total = term if total is None else total + term
        target[...] = total.astype(BF16)


def per_device(
    tokens,
    out_grad,
    crop_image,
    crop_res,
    position_kernel,
    position_bias,
    gain_one,
    shift_one,
    qkv_weight,
    query_value_bias,
    relative_three,
    relative_five,
    relative_seven,
    relative_bias,
    output_weight,
    output_bias,
    gain_two,
    shift_two,
    up_weight,
    up_bias,
    down_weight,
    down_bias,
):
    group = lax.axis_size("mp")
    member = lax.axis_index("mp")
    rows = tokens.shape[0]
    width = qkv_weight.shape[2]
    hidden_width = up_weight.shape[1]
    pair = group == 2
    size = lax.axis_size("dp")
    blocks = (
        pair
        and size >= 4
        and size & (size - 1) == 0
        and 2 * width == D
        and hidden_width == 2 * D
        and D % (size * 8) == 0
    )

    def row(vector):
        return vector.reshape(1, -1)

    if not blocks:
        full_kernel = jnp.concatenate(
            [
                jnp.pad(relative_three, ((2, 2), (2, 2), (0, 0))),
                jnp.pad(relative_five, ((1, 1), (1, 1), (0, 0))),
                relative_seven,
            ],
            axis=2,
        )
        kernel_part = lax.dynamic_slice_in_dim(full_kernel, member * width, width, 2)
        bias_part = row(lax.dynamic_slice_in_dim(relative_bias, member * width, width, 0))
    else:
        kernel_part, bias_part = None, row(relative_bias)
    qkv_planes = jnp.transpose(qkv_weight, (1, 0, 2))

    if pair:
        token_list = [tokens, turn(tokens, 1, "mp")]
        images = [lambda: lax.axis_index("mp"), lambda: 1 - lax.axis_index("mp")]
    else:
        token_list = list(lax.all_gather(tokens, "mp", axis=0))
        grad_list = list(lax.all_gather(out_grad, "mp", axis=0))
        images = [functools.partial(int, j) for j in range(group)]

    def own(parts):
        if pair:
            return parts[0]
        return lax.dynamic_index_in_dim(jnp.stack(parts), member, 0, keepdims=False)

    mlp_vectors = [row(output_bias), row(gain_two), row(shift_two)]
    fronts = []
    for index, (image, one) in enumerate(zip(images, token_list)):
        table = blocks and index == 0
        outs = [
            Far((ROWS, rows), BF16),
            Far((rows, ROWS), BF16),
            ((rows, D), F32),
            Far((rows, D), BF16),
            Far((rows, width), F32),
            Far((rows, width), BF16),
            Far((rows, width), F32),
            Far((width, width), BF16),
            Far((rows, width), F32),
            Far((rows, width), BF16),
            ((rows, D), BF16),
        ]
        if blocks:
            outs.append(((rows, D + width), BF16))
        args = [
            crop_res,
            Far(one) if index == 0 else one,
            Far(position_kernel),
            Far(row(position_bias)),
            Far(row(gain_one)),
            Far(row(shift_one)),
            Far(qkv_planes),
            Far(query_value_bias),
        ]
        if table:
            outs += [Far((EDGE, EDGE, width), F32), Far((rows, D), F32)]
            args += [Far(relative_three), Far(relative_five), Far(relative_seven)]
        else:
            args.append(Far(kernel_part))
        args += [Far(bias_part), Far(output_weight)]
        scratch = [pltpu.VMEM((CELLS, SLOTS, D), F32)] * 2
        body = functools.partial(front_body, image, table, blocks)
        if index:
            args = [one.what[0] if isinstance(one, Far) and one.what[0] is not kernel_part else one for one in args]
        bring = (up_weight, down_weight, *mlp_vectors) if pair and index else ()
        us = 5.0 if index else 50.0
        made = call(body, outs, args, scratch, us=us, smem=1, bring=bring)
        if bring:
            up_weight, down_weight, *mlp_vectors = made[-5:]
        if table:
            kernel_part, kept_residual = made[12:14]
        fronts.append(made[: 12 if blocks else 11])
    to_frame, to_token, residual, normed, query, value, weight, context = tuple(zip(*fronts))[:8]
    relative, attended, partial, *early = tuple(zip(*fronts))[8:]

    if pair:
        (ready,) = call(copy_body, [((rows, D), BF16)], partial[:1], us=0.3, after=[token_list[1]])
        first, second = turn(ready, 1, "mp"), turn(partial[1], 1, "mp")
        grad_list, grad_parts = [out_grad, turn(out_grad, 1, "mp")], [None, None]
        addends = [(partial[0], second), (partial[1], first)]
        places = [(None, None), (None, None)]
        order = (1, 0)
        arrived = mark([grad_list[1], partial[1]], ARRIVED)
    else:
        total = lax.psum(jnp.stack(partial), "mp")
        grad_parts = [None] * group
        addends = [(one, jnp.zeros_like(one)) for one in total]
        places = [(None, None)] * group
        order = range(group)
    mlps = [None] * group
    for index in order:
        outs = [Far((rows, D), F32), ((rows, D), BF16), Far((rows, D), BF16)]
        outs.append(Far((1, hidden_width), F32))
        scratch = []
        if blocks:
            outs += [((rows, hidden_width + D), BF16)] * 2
            scratch = [pltpu.VMEM((rows, hidden_width), BF16)] * 2
        else:
            outs += [((rows, hidden_width), BF16)] * 2 + [((rows, D), BF16)]
        args = (
            residual[index],
            *addends[index],
            grad_list[index],
            *mlp_vectors,
            up_weight,
            row(up_bias.astype(F32)),
            down_weight,
        )
        body = functools.partial(mlp_body, (*places[index], grad_parts[index]), blocks)
        after = []
        if pair:
            after = [mlps[1][1]] if index == 0 else [arrived]
        mlps[index] = call(body, outs, args, scratch, us=2.5, after=after)
    middle, grad_two_part, mlp_part, grad_up_bias, *mlp_rows = zip(*mlps)

    if pair:
        back_addends = [
            (grad_two_part[0], turn(grad_two_part[1], 1, "mp")),
            (grad_two_part[1], turn(grad_two_part[0], 1, "mp")),
        ]
    else:
        total = lax.psum(jnp.stack(grad_two_part), "mp")
        back_addends = [(one, jnp.zeros_like(one)) for one in total]

    steps = len(step_bits()[0])
    if blocks:
        args = (*mlp_rows[0], *(turn(one, 1) for one in mlp_rows[1]))
        after = [mark([back_addends[0][1]], 46.0)]
        mlp_keep, mlp_send = call(mlp_grads_body, [((D, D), BF16)] * 2, args, us=2.0, after=after)
        mlp_came = step_turn(mlp_send, 0)

    backs = []
    for index in range(group):
        carry = pair and index == 1
        outs = [
            Far((rows, D), F32),
            ((2, rows, D) if carry else (rows, D), BF16),
            Far((8, D), F32),
            Far((56, width), F32),
        ]
        if blocks:
            outs += [((rows, D + width), BF16)] * 2
        else:
            outs += [((rows, D), BF16), ((3, rows, width), BF16)]
        args = [
            *back_addends[index],
            grad_list[index],
            middle[index],
            row(gain_two),
            output_weight,
            query[index],
            to_frame[index],
            value[index],
            kernel_part,
            context[index],
            relative[index],
            weight[index],
            to_token[index],
            qkv_planes,
        ]
        if carry:
            args.append(mlp_part[1])
        scratch = [pltpu.VMEM((CELLS, SLOTS, width), F32)] * 3
        body = functools.partial(back_body, (None, None, grad_parts[index]), blocks)
        after = [mlp_keep] if blocks else []
        if pair and index:
            after.append(backs[0][1])
        backs.append(call(body, outs, args, scratch, us=25.0 if index else 0.0, after=after))
    grad_middle, grad_one_part, wide_sums, head_sums, *late = zip(*backs)

    if blocks:
        mlp_keep, mlp_came = halve(mlp_keep, mlp_came, 1, after=[backs[1][1]], us=WEIGHTS["h1"])
        outs = [((width, D), BF16)] * 2
        args = (*normed, *attended, *(turn(one, 1) for one in early[0]))
        args += (*late[0], *(turn(one, 1) for one in late[1]))
        body = functools.partial(attention_grads_body, group)
        keep, send = call(body, outs, args, us=2.0, after=[mlp_keep])
        came = step_turn(send, 0)
        outs = [((SMALL, width), BF16)]
        args = (*head_sums, *wide_sums, *grad_up_bias)
        scratch = [pltpu.VMEM((SMALL, width), F32)]
        (group_sums,) = call(group_body, outs, args, scratch, us=0.0, after=[keep])
        group_came = step_turn(group_sums, steps - 1)
    if not blocks:
        hidden, grad_pre, normed_two = mlp_rows
        grad_projected, grad_qkv = late
        args = (*normed_two, *grad_pre, *hidden, *grad_list)
        args += (*normed, *grad_qkv, *attended, *grad_projected)

        def spot(kind, image, part=None):
            return kind * group + image, part

        each = range(group)
        products = [
            [(spot(0, j), spot(1, j)) for j in each],
            [(spot(2, j), spot(3, j, grad_parts[j])) for j in each],
        ]
        products += [[(spot(4, j), spot(5, j, plane)) for j in each] for plane in range(3)]
        products += [[(spot(6, j), spot(7, j)) for j in each]]
        outs = [((D, hidden_width), BF16), ((hidden_width, D), BF16)]
        outs += [((D, width), BF16)] * 3 + [((width, D), BF16)]
        wholes = call(functools.partial(whole_body, products), outs, args, us=6.0, vmem=40)
        grad_up, grad_down, *planes, grad_out = (lax.psum(one, "dp").astype(F32) for one in wholes)
        grad_qkv_planes = jnp.stack(planes)

    if pair:
        mine, mlp_mine = grad_one_part[0], mlp_part[0]
        other = turn(grad_one_part[1], 1, "mp")
    else:
        sums = [jnp.stack(grad_one_part), jnp.stack(mlp_part)]
        mine, mlp_mine = (lax.psum_scatter(one, "mp", scatter_dimension=0) for one in sums)
        other = jnp.zeros((2, rows, D), BF16)
    outs = [Far((rows, D), F32), Far((rows, D), F32)]
    height = EXTRA + SMALL // 2 if blocks else EXTRA
    outs.append(((height, D), BF16 if blocks else F32))
    args = [
        mine,
        other,
        kept_residual if blocks else own(residual),
        row(gain_one),
        own(grad_middle),
        own(to_frame),
        tokens,
        position_kernel,
        own(to_token),
        own(middle),
        mlp_mine,
        row(down_bias),
    ]
    if blocks:
        args += [group_sums, group_came]
    scratch = [pltpu.VMEM((CELLS, SLOTS, D), F32)] * 3
    scratch.append(pltpu.VMEM((height, D), F32))
    after = []
    if blocks:
        for step in range(2, steps):
            us = WEIGHTS["h2"]
            mlp_keep, mlp_came = halve(mlp_keep, mlp_came, step, after=[keep], us=us)
        keep, came = halve(keep, came, 1, after=[mlp_keep], us=WEIGHTS["p1"])
        after = [keep, mark([group_came, group_sums], HELD)]
    block_out, token_grad, own_sums = call(
        last_body, outs, args, scratch, us=WEIGHTS["last"], after=after
    )

    if blocks:
        far_sums = turn(own_sums, 1, "mp")
        mark_last = own_sums
        for step in range(2, steps):
            keep, came = halve(keep, came, step, after=[mark_last], us=WEIGHTS["p2"])
            mark_last = keep
        outs = [(mlp_keep.shape, BF16)]
        body = functools.partial(halve_body, None)
        args = (mlp_keep, mlp_came)
        (mlp_keep,) = call(body, outs, args, us=WEIGHTS["total"], after=[mark_last])
        mlp_came = step_turn(mlp_keep, steps - 1)
        args = (keep, came, own_sums, far_sums)
        outs = [((keep.shape[0] + EXTRA, D), BF16), ((SMALL, D), BF16)]
        scratch = [pltpu.VMEM((SMALL, D), F32)]
        us = WEIGHTS["pack"]
        keep, small = call(sum_body, outs, args, scratch, us=us, after=[mlp_keep])
        extra, more = EXTRA, [small]
        for step in reversed(range(steps)):
            came = step_turn(keep, step)
            us = WEIGHTS.get(f"j{step}", 0.0)
            mlp_keep = join(mlp_keep, mlp_came, step, after=[keep], us=us)
            mlp_came = step_turn(mlp_keep, step - 1) if step else turn(mlp_keep, 1)
            mark_last = mlp_keep
            if not step:
                shapes = [(D, hidden_width), (hidden_width, D)]
                fill = [jax.ShapeDtypeStruct(shape, F32) for shape in shapes]
                mark_last, grad_up, grad_down = half_write(True, mlp_keep, [], fill)
            us = WEIGHTS.get(f"a{step}", 0.0)
            keep = join(keep, came, step, extra, more, after=[mark_last], us=us)
            extra, more = EXTRA + SMALL, []
        came = turn(keep, 1)
        finished, grad_up, grad_down = half_write(False, mlp_came, [keep], (grad_up, grad_down))
        shapes = [(width, D), (3, 3, D), (1, hidden_width), (2, width)]
        shapes += [relative_three.shape, relative_five.shape, relative_seven.shape]
        outs = [Far(shape, F32) for shape in shapes + [(1, D)] * 8]
        scratch = [pltpu.VMEM((3, D, width), F32), pltpu.SemaphoreType.DMA((3,))]
        scratch += [pltpu.VMEM((SMALL, D), F32), pltpu.VMEM((EXTRA, D), F32)]
        made = call(
            attention_final_body,
            outs,
            (keep, came),
            scratch,
            after=[finished],
            fill=[jax.ShapeDtypeStruct((3, D, width), F32)],
        )
        grad_out, position, up_sum, pair_sum, three, five, seven, *vectors, grad_qkv_planes = made
        vectors = [one.reshape(D) for one in vectors]
        return (
            block_out,
            token_grad,
            position,
            *vectors[0:3],
            jnp.transpose(grad_qkv_planes, (1, 0, 2)),
            pair_sum,
            three,
            five,
            seven,
            vectors[3],
            grad_out,
            *vectors[4:7],
            grad_up,
            up_sum.reshape(hidden_width),
            grad_down,
            vectors[7],
        )

    head_total = functools.reduce(jnp.add, head_sums)
    wide_total = functools.reduce(jnp.add, wide_sums)
    own_total = lax.psum(own_sums[:12], "mp")
    relative_total = lax.all_gather(head_total[:50], "mp", axis=1, tiled=True)
    bias_total = functools.reduce(jnp.add, grad_up_bias)
    pieces = [own_total, wide_total[:4], relative_total]
    private = jnp.concatenate([bias_total.reshape(-1), head_total[50:52].reshape(-1)])
    pieces.append(jnp.pad(private, (0, -private.shape[0] % D)).reshape(-1, D))
    total = sum_small(jnp.concatenate(pieces, axis=0))
    kernel_grad = total[16:65].reshape(EDGE, EDGE, D)
    tail = total[66:].reshape(-1)
    return (
        block_out,
        token_grad,
        total[:9].reshape(3, 3, D),
        total[9],
        total[10],
        total[11],
        jnp.transpose(grad_qkv_planes, (1, 0, 2)),
        tail[hidden_width : hidden_width + 2 * width].reshape(2, width),
        kernel_grad[2:5, 2:5, : 2 * HEAD],
        kernel_grad[1:6, 1:6, 2 * HEAD : 5 * HEAD],
        kernel_grad[:, :, 5 * HEAD :],
        total[65],
        grad_out,
        total[12],
        total[13],
        total[14],
        grad_up,
        tail[:hidden_width],
        grad_down,
        total[15],
    )


def solution(mesh):
    in_specs = (
        P(("dp", "mp"), None),
        P(("dp", "mp"), None),
        P("dp"),
        P("dp"),
        P(),
        P(),
        P(),
        P(),
        P(None, None, "mp"),
        P(None, "mp"),
        P(),
        P(),
        P(),
        P(),
        P("mp", None),
        P(),
        P(),
        P(),
        P(None, "mp"),
        P("mp"),
        P("mp", None),
        P(),
    )
    out_specs = (
        P(("dp", "mp"), None),
        P(("dp", "mp"), None),
        P(),
        P(),
        P(),
        P(),
        P(None, None, "mp"),
        P(None, "mp"),
        P(),
        P(),
        P(),
        P(),
        P("mp", None),
        P(),
        P(),
        P(),
        P(None, "mp"),
        P("mp"),
        P("mp", None),
        P(),
    )
    return jax.shard_map(
        per_device, mesh=mesh, in_specs=in_specs, out_specs=out_specs, check_vma=False
    )
```
